32 devices in a mesh: group: 2 (over y), skill: 4 (over z), tensor: 2 (over core), dp: 2 (over x).
Axes of the slice: x: 2, y: 2, z: 4, core: 2. Of those that a mesh axis runs over, the one named last changes fastest.
Arguments:
- tokens: bfloat16 [12288, 8192], P(('group', 'skill'), ('tensor', 'dp')), parts along dimension 0, may hold values from -6 to 6
- base_weight: bfloat16 [8192, 1024], P(('tensor', 'dp')), may hold values from -0.0625 to 0.0625
- skill_down: bfloat16 [512, 8192, 16], P('skill', ('tensor', 'dp')), may hold values from -0.0625 to 0.0625
- skill_up: bfloat16 [512, 16, 1024], P('skill', None, ('tensor', 'dp')), may hold values from -1.5 to 1.5
- alloc: float32 [64, 512], P('group', 'skill'), parts along dimension 0, may hold values from -0.25 to 0.25
- block_tenant: int32 [96], P(('group', 'skill')), parts along dimension 0, may hold values from 0 to 31
- block_len: int32 [96], P(('group', 'skill')), parts along dimension 0, may hold values from 1 to 128, as said below
Outputs:
- values_out: bfloat16 [12288, 1024], P(('group', 'skill'), ('tensor', 'dp')), parts along dimension 0
The draws below stay inside these ranges and needn't reach their ends.
There are 2 independent parts, one for each index of `group`. The reference program is written for one: setup_inputs(seed, part) draws one part's arguments, and reference() takes and returns one part's arrays. A program takes and returns all parts, laid end to end along the dimension named above; an argument that names none is the same for every part. Nothing has to cross between parts.
Inputs may be any that keep to these rules, and one draw needn't show every extreme that they name: `block_len`: each block holds between 1 and 128 live rows; some block is full in every draw.
All inputs are finite; a program needn't handle non-finite values.
Results may differ from the reference program's by a relative error of at most 0.015.
Values may be sent and summed in bfloat16 or wider, within the bound.
No kernel may reach another device: no remote copies, remote signals or barrier semaphores. Data moves between devices by JAX's collectives and lax.ppermute only.
A program may use at most 128 MiB of HBM per device.

```python
import math
import jax
import jax.numpy as jnp
import numpy as np
from jax import lax

D = 8192
DOUT = 1024
R = 16
S = 512
BLOCK = 128
TEN = 32
NF = 4
BLOCKS = 48
TOKENS = 6144


def draw_block_len(key, part):
    key = jax.random.fold_in(key, 7)
    first, second = jax.random.split(key)
    counts = jax.random.randint(first, (BLOCKS,), 1, BLOCK + 1)
    full_at = jax.random.randint(second, (), 0, BLOCKS)
    places = jnp.arange(BLOCKS, dtype=jnp.int32)
    return jnp.where(places == full_at, BLOCK, counts).astype(jnp.int32)


def set_ends(array, rng, least, high):
    longest = array.shape.index(max(array.shape))
    spots = []
    for shift in (0, 1):
        where = [jax.random.randint(jax.random.fold_in(rng, axis), (), 0, length) for axis, length in enumerate(array.shape)]
        where[longest] = (where[longest] + shift) % array.shape[longest]
        spots.append(tuple(where))
    return array.at[spots[0]].set(least).at[spots[1]].set(high)


def level_of(key, dims, shards, smallest, top_value):
    def one(axis_at, shards_of):
        heights = jax.random.uniform(jax.random.fold_in(jax.random.fold_in(key, 6), axis_at), (shards_of,), jnp.float32, smallest / len(shards), top_value / len(shards))
        return jnp.repeat(jnp.exp(heights), dims[axis_at] // shards_of).reshape((-1,) + (1,) * (len(dims) - axis_at - 1))

    factor_of = one(*shards[0])
    for cut in shards[1:]:
        factor_of = factor_of * one(*cut)
    return factor_of


def rank_table(number_of, lean):
    loads = [(1 << 20) // math.isqrt(grade ** lean) + 1 for grade in range(1, number_of + 1)]
    spread = 1 + sum(loads) // (1 << 30)
    return np.cumsum(np.array([max(1, weight // spread) for weight in loads]))


def skewed_ids(rng, extent, count, slope):
    listing = rank_table(count, slope)
    lot = jax.random.randint(jax.random.fold_in(rng, 1), extent, 0, int(listing[count - 1]))
    standing = jnp.searchsorted(jnp.asarray(listing, jnp.int32), lot, side="right")
    return jax.random.permutation(jax.random.fold_in(rng, 2), count)[standing].astype(jnp.int32)


def gaussian(stream_key, extent, scale, most, cuts=(), kind=jnp.bfloat16):
    entries = scale * jax.random.normal(stream_key, extent, jnp.float32)
    if cuts:
        entries = entries * level_of(stream_key, extent, cuts, -0.22, 0.18)
    return jnp.clip(entries, -most, most).astype(kind)


def setup_inputs(seed: int = 0, part: int = 0) -> dict:
    key_of = jax.random.split(jax.random.key(seed), 8)
    part_keys = jax.random.split(jax.random.fold_in(key_of[7], part), 8)
    tokens = gaussian(part_keys[0], (TOKENS, D), 1.0, 6.0, ((0, 4), (1, 4)))
    base_weight = gaussian(key_of[1], (D, DOUT), D ** -0.5, 0.0625, ((0, 4),))
    skill_down = gaussian(key_of[2], (S, D, R), D ** -0.5, 0.0625, ((0, 4), (1, 4)))
    skill_up = gaussian(key_of[3], (S, R, DOUT), R ** -0.5, 1.5, ((0, 4), (2, 4)))
    alloc = gaussian(part_keys[4], (TEN, S), S ** -0.5, 0.25, ((1, 4),), jnp.float32)
    block_tenant = set_ends(skewed_ids(part_keys[5], (BLOCKS,), TEN, 2), jax.random.fold_in(part_keys[5], 3), 0, TEN - 1).astype(jnp.int32)
    block_len = draw_block_len(jax.random.fold_in(jax.random.fold_in(key_of[7], part), 71), part)
    return dict(tokens=tokens, base_weight=base_weight, skill_down=skill_down, skill_up=skill_up, alloc=alloc, block_tenant=block_tenant, block_len=block_len)


def reference(tokens, base_weight, skill_down, skill_up, alloc, block_tenant, block_len):
    high = lax.Precision.HIGHEST
    weights = alloc.astype(jnp.float32)
    composed_down = jnp.einsum("ts,sdr->tdr", weights, skill_down.astype(jnp.float32), precision=high).astype(jnp.bfloat16)
    composed_up = jnp.einsum("ts,sro->tro", weights, skill_up.astype(jnp.float32), precision=high).astype(jnp.bfloat16)
    width = D // NF
    base = jnp.zeros((TOKENS, DOUT), jnp.float32)
    for slice_index in range(NF):
        rounded = jnp.dot(tokens[:, slice_index * width:(slice_index + 1) * width], base_weight[slice_index * width:(slice_index + 1) * width], preferred_element_type=jnp.float32).astype(jnp.bfloat16)
        rounded = lax.optimization_barrier(rounded)
        base = base + rounded.astype(jnp.float32)
    grouped = tokens.reshape(BLOCKS, BLOCK, D)

    def one_block(items):
        rows, tenant = items
        lowrank = jnp.dot(rows, composed_down[tenant], preferred_element_type=jnp.float32)
        return jnp.dot(lowrank, composed_up[tenant].astype(jnp.float32), precision=high)

    adapter = lax.map(one_block, (grouped, block_tenant.astype(jnp.int32)))
    total = base.reshape(BLOCKS, BLOCK, DOUT) + adapter
    live = (jnp.arange(BLOCK, dtype=jnp.int32)[None, :] < block_len[:, None])[:, :, None]
    return jnp.where(live, total, jnp.float32(0.0)).astype(jnp.bfloat16).reshape(TOKENS, DOUT)
```

```python
import functools

import jax
import jax.numpy as jnp
from jax import lax
from jax.experimental import pallas as pl
from jax.experimental.pallas import tpu as pltpu
from jax.sharding import PartitionSpec as P

F32, BF16, I32 = jnp.float32, jnp.bfloat16, jnp.int32
MIB = 1 << 20
VMEM = pl.BlockSpec(memory_space=pltpu.VMEM)
SMEM = pl.BlockSpec(memory_space=pltpu.SMEM)
LANES = 128
NT = (((1,), (1,)), ((), ()))
TN = (((0,), (0,)), ((), ()))


def call(kernel, *, vmem=32, flops=0, nbytes=0, **kwargs):
    return pl.pallas_call(
        kernel,
        compiler_params=pltpu.CompilerParams(vmem_limit_bytes=vmem * MIB),
        cost_estimate=pl.CostEstimate(flops=flops, bytes_accessed=nbytes, transcendentals=0),
        **kwargs,
    )


def tables_kernel(n, tenants, place_ref, *refs):
    arrays, tab_ref = refs[:n], refs[n]
    me = place_ref[0]
    blocks = arrays[0].shape[1]
    sub = lax.broadcasted_iota(I32, (tenants, tenants), 0)
    lane = lax.broadcasted_iota(I32, (tenants, tenants), 1)
    wide = lax.broadcasted_iota(I32, (tenants, LANES), 1)
    tenant = lax.broadcasted_iota(I32, (tenants, LANES), 0)
    one = lax.broadcasted_iota(I32, (tenants, blocks), 0)
    zs = [lax.rem(me - k + n, n) for k in range(n)]
    present = [
        jnp.max(jnp.where(one == arrays[k][0:1, :], 1.0, 0.0), axis=1, keepdims=True)
        for k in range(n)
    ]

    def union(keep):
        total = jnp.zeros((tenants, 1), F32)
        for z, here in zip(zs, present):
            total = jnp.maximum(total, here * jnp.where(keep(z), 1.0, 0.0))
        return total

    def positions(held):
        across = jnp.sum(jnp.where(sub == lane, held, 0.0), axis=0, keepdims=True)
        return jnp.sum(jnp.where(lane < sub, across, 0.0), axis=1, keepdims=True)

    def pack(held, value):
        slot = positions(held).astype(I32)
        chosen = jnp.logical_and(slot == wide, held > 0.5)
        return jnp.sum(jnp.where(chosen, value, 0.0), axis=0, keepdims=True)

    send_right, send_left = union(lambda z: z > me), union(lambda z: z < me)
    from_left, from_right = positions(union(lambda z: z >= me)), positions(union(lambda z: z <= me))
    number = tenant.astype(F32)
    right = pack(send_right, number), pack(send_right, from_left)
    left = pack(send_left, number), pack(send_left, from_right)
    own = jnp.concatenate([arrays[0][0:1, :], jnp.zeros((1, LANES - blocks), I32)], axis=1)
    mine = own == tenant

    def at(place, rows, otherwise):
        return jnp.where(me == place, rows, otherwise)

    none = jnp.zeros((1, LANES), F32)
    final_right = jnp.sum(jnp.where(mine, from_left, 0.0), axis=0, keepdims=True)
    final_left = jnp.sum(jnp.where(mine, from_right, 0.0), axis=0, keepdims=True)
    rows = []
    for part in (0, 1):
        for hop in range(n - 1):
            rows.append(at(hop, right[part], at(n - 1 - hop, left[part], none)))
    for hop in range(n - 1):
        rows.append(at(hop + 1, final_right, at(n - 2 - hop, final_left, none)))
    for row, value in enumerate(rows):
        tab_ref[row : row + 1, :] = value.astype(I32)
    tab_ref[len(rows) : len(rows) + 1, :] = own


def make_tables(n, tenants, place, arrays):
    rows = -(-(3 * (n - 1) + 1) // 8) * 8
    return call(
        functools.partial(tables_kernel, n, tenants),
        out_shape=jax.ShapeDtypeStruct((rows, LANES), I32),
        in_specs=[SMEM] + [VMEM] * n,
        out_specs=VMEM,
    )(place, *arrays)


def compose_kernel(rank, alloc_ref, skills_ref, own_ref, kron):
    tenants, skills = alloc_ref.shape
    depth = skills * rank

    @pl.when(pl.program_id(0) == 0)
    def _():
        at = lax.broadcasted_iota(I32, (skills, depth), 1)
        row = lax.broadcasted_iota(I32, (skills, depth), 0)
        inside = jnp.logical_and(at >= row * rank, at < (row + 1) * rank)
        repeat = jnp.where(inside, 1.0, 0.0).astype(BF16)
        spread = jnp.dot(alloc_ref[...].astype(BF16), repeat, preferred_element_type=F32)
        lane = lax.rem(lax.broadcasted_iota(I32, (rank, depth), 1), rank)
        diagonal = lane == lax.broadcasted_iota(I32, (rank, depth), 0)
        for t in range(tenants):
            kron[t * rank : (t + 1) * rank, :] = jnp.where(diagonal, spread[t : t + 1, :], 0.0).astype(BF16)

    own_ref[...] = jnp.dot(kron[...], skills_ref[...], preferred_element_type=F32).astype(BF16)


def compose(alloc, library, rank, tile):
    tenants, skills = alloc.shape
    depth, width = library.shape
    return call(
        functools.partial(compose_kernel, rank),
        vmem=24,
        flops=2 * tenants * rank * depth * width,
        nbytes=2 * (depth + tenants * rank) * width,
        grid=(width // tile,),
        in_specs=[
            pl.BlockSpec((tenants, skills), lambda j: (0, 0)),
            pl.BlockSpec((depth, tile), lambda j: (0, j)),
        ],
        out_specs=pl.BlockSpec((tenants * rank, tile), lambda j: (0, j)),
        out_shape=jax.ShapeDtypeStruct((tenants * rank, width), BF16),
        scratch_shapes=[pltpu.VMEM((tenants * rank, depth), BF16)],
    )(alloc, library)


def relay_kernel(hop, n, slots, tab_ref, own_ref, *refs):
    out_ref = refs[-1]

    def one(slot, carry):
        block = own_ref[tab_ref[hop, slot]]
        if hop:
            passed = refs[0][tab_ref[n - 1 + hop, slot]]
            block = (block.astype(F32) + passed.astype(F32)).astype(BF16)
        out_ref[slot] = block
        return carry

    lax.fori_loop(0, slots, one, 0, unroll=4)


def relay(hop, n, slots, tab, own, part, arrived):
    tenants, rank, _ = own.shape
    start, size = part
    at = start // size
    ins = [tab, own] + ([arrived] if hop else [])
    return call(
        functools.partial(relay_kernel, hop, n, slots),
        vmem=16,
        nbytes=2 * rank * size * (tenants + 2 * slots),
        grid=(1,),
        in_specs=[SMEM, pl.BlockSpec((tenants, rank, size), lambda j: (0, 0, at))] + [VMEM] * (1 if hop else 0),
        out_specs=VMEM,
        out_shape=jax.ShapeDtypeStruct((slots, rank, size), BF16),
    )(*ins)


def project_kernel(n, last, tab_ref, tokens_ref, own_ref, *refs):
    arrived, total_ref, out_ref = refs[: n - 1], refs[n - 1], refs[n]
    rank = own_ref.shape[1]
    blocks = tokens_ref.shape[0] // LANES

    for b in range(blocks):
        factor = own_ref[tab_ref[3 * (n - 1), b]].astype(F32)
        for hop in range(n - 1):
            factor = factor + arrived[hop][tab_ref[2 * (n - 1) + hop, b]].astype(F32)
        rows = tokens_ref[b * LANES : (b + 1) * LANES, :]
        part = lax.dot_general(factor.astype(BF16), rows, NT, preferred_element_type=F32)
        at = slice(b * LANES, (b + 1) * LANES)
        out_ref[:, at] = (total_ref[:, at] + part).astype(out_ref.dtype)


def project(n, tab, tokens, own, part, arrived, total, last):
    tenants, rank, _ = own.shape
    rows = tokens.shape[0]
    start, size = part
    at = start // size
    return call(
        functools.partial(project_kernel, n, last),
        vmem=24,
        flops=2 * rows * size * rank,
        nbytes=2 * size * (rows + 2 * tenants * rank),
        grid=(1,),
        in_specs=[
            SMEM,
            pl.BlockSpec((rows, size), lambda j: (0, at)),
            pl.BlockSpec((tenants, rank, size), lambda j: (0, 0, at)),
        ]
        + [VMEM] * n,
        out_specs=VMEM,
        out_shape=jax.ShapeDtypeStruct((rank, rows), BF16 if last else F32),
    )(tab, tokens, own, *arrived, total)


def base_kernel(order_ref, tokens_ref, weight_ref, away_ref, keep_ref):
    q = pl.program_id(0)
    product = jnp.dot(tokens_ref[...], weight_ref[...], preferred_element_type=F32).astype(BF16)

    @pl.when(q < 2)
    def _():
        away_ref[0] = product

    @pl.when(q >= 2)
    def _():
        keep_ref[0] = product


def base_product(order, tokens, weight):
    rows, width = tokens.shape
    out = weight.shape[1] // 4
    return pl.pallas_call(
        base_kernel,
        grid_spec=pltpu.PrefetchScalarGridSpec(
            num_scalar_prefetch=1,
            grid=(4,),
            in_specs=[
                pl.BlockSpec((rows, width), lambda q, order: (0, 0), pipeline_mode=pl.Buffered(1)),
                pl.BlockSpec((width, out), lambda q, order: (0, order[q])),
            ],
            out_specs=[
                pl.BlockSpec((1, rows, out), lambda q, order: (jnp.minimum(q, 1), 0, 0)),
                pl.BlockSpec((1, rows, out), lambda q, order: (jnp.maximum(q - 2, 0), 0, 0)),
            ],
        ),
        out_shape=[jax.ShapeDtypeStruct((2, rows, out), BF16)] * 2,
        compiler_params=pltpu.CompilerParams(vmem_limit_bytes=32 * MIB),
        cost_estimate=pl.CostEstimate(
            flops=8 * rows * width * out, bytes_accessed=2 * rows * (width + 4 * out) + 8 * width * out, transcendentals=0
        ),
    )(order, tokens, weight)


def finish_kernel(n, per, tab_ref, len_ref, own_ref, *refs):
    arrived, lows, bases, out_ref = refs[: n - 1], refs[n - 1 : n + 3], refs[n + 3 : n + 6], refs[n + 6]
    step = pl.program_id(0)
    width = out_ref.shape[1]
    for j in range(per):
        b = step * per + j
        up = own_ref[tab_ref[3 * (n - 1), b]].astype(F32)
        for hop in range(n - 1):
            up = up + arrived[hop][tab_ref[2 * (n - 1) + hop, b]].astype(F32)
        up = up.astype(BF16)
        at = slice(j * LANES, (j + 1) * LANES)
        low = lows[0][:, at].astype(F32)
        for other in lows[1:]:
            low = low + other[:, at].astype(F32)
        high = low.astype(BF16)
        rest = (low - high.astype(F32)).astype(BF16)
        adapter = lax.dot_general(high, up, TN, preferred_element_type=F32)
        adapter = adapter + lax.dot_general(rest, up, TN, preferred_element_type=F32)
        total = adapter
        for base in bases:
            total = total + base[at, :].astype(F32)
        live = lax.broadcasted_iota(I32, (LANES, width), 0) < len_ref[b]
        out_ref[at, :] = jnp.where(live, total, 0.0).astype(out_ref.dtype)


def finish(n, tab, lens, own, arrived, lows, bases, per):
    rank, rows = lows[0].shape
    width = bases[0].shape[1]
    blocks = rows // LANES
    return call(
        functools.partial(finish_kernel, n, per),
        vmem=24,
        flops=4 * rows * rank * width,
        nbytes=8 * rows * width,
        grid=(blocks // per,),
        in_specs=[SMEM, SMEM, VMEM]
        + [VMEM] * (n - 1)
        + [pl.BlockSpec((rank, per * LANES), lambda j: (0, j))] * 4
        + [pl.BlockSpec((per * LANES, width), lambda j: (j, 0))] * 3,
        out_specs=pl.BlockSpec((per * LANES, width), lambda j: (j, 0)),
        out_shape=jax.ShapeDtypeStruct((rows, width), BF16),
    )(tab, lens, own, *arrived, *lows, *bases)


def swap(x, axis):
    return lax.ppermute(x, axis, [(0, 1), (1, 0)])


def line_body(n, tokens, base_weight, skill_down, skill_up, alloc, block_tenant, block_len):
    rows, width = tokens.shape
    tenants, local_skills = alloc.shape
    rank = skill_down.shape[2]
    slice_out = skill_up.shape[2]
    blocks = block_len.shape[0]
    me = lax.axis_index("skill")
    tensor, dp = lax.axis_index("tensor"), lax.axis_index("dp")
    hops = [[(h, h + 1), (n - 1 - h, n - 2 - h)] for h in range(n - 1)]
    sizes = [min(tenants, blocks * (n - 1 - h)) for h in range(n - 1)]

    own_t = block_tenant.reshape(1, blocks)
    seen = [own_t] + [
        lax.ppermute(own_t, "skill", [(j, (j + k) % n) for j in range(n)]) for k in range(1, n)
    ]
    up = compose(alloc, skill_up.reshape(local_skills * rank, slice_out), rank, slice_out)
    up = up.reshape(tenants, rank, slice_out)
    library = jnp.transpose(skill_down, (0, 2, 1)).reshape(local_skills * rank, width)
    down = compose(alloc, library, rank, 256).reshape(tenants, rank, width)
    tab = make_tables(n, tenants, me.reshape(1).astype(I32), seen)

    def chain(own, part):
        arrived = []
        for h in range(n - 1):
            message = relay(h, n, sizes[h], tab, own, part, arrived[-1] if h else None)
            arrived.append(lax.ppermute(message, "skill", hops[h]))
        return arrived

    other, mine = (1 - tensor) * 2, tensor * 2
    order = jnp.stack([other + 1 - dp, other + dp, mine + 1 - dp, mine + dp]).astype(I32)
    away, keep = base_product(order, tokens, base_weight)
    from_core = swap(away, "tensor")
    across = swap((keep[0].astype(F32) + from_core[0].astype(F32)).astype(BF16), "dp")

    up_arrived = chain(up, (0, slice_out))
    size = 512
    parts = [(s, size) for s in range(0, width, size)]
    down_arrived = [chain(down, part) for part in parts]
    low = jnp.zeros((rank, rows), F32)
    for part, arrived in zip(parts, down_arrived):
        low = project(n, tab, tokens, down, part, arrived, low, part is parts[-1])
    lows = [low, swap(low, "tensor"), swap(low, "dp")]
    lows.append(lax.ppermute(low, ("tensor", "dp"), [(0, 3), (1, 2), (2, 1), (3, 0)]))
    return finish(n, tab, block_len, up, up_arrived, lows, [keep[1], from_core[1], across], 3)


def plain_body(tokens, base_weight, skill_down, skill_up, alloc, block_tenant, block_len):
    rows, width = tokens.shape
    blocks = block_len.shape[0]
    block_rows = rows // blocks
    local_skills, slice_width, rank = skill_down.shape
    slice_out = skill_up.shape[2]
    down_size = slice_width * rank
    stacked = jnp.concatenate(
        [
            skill_down.reshape(local_skills, down_size),
            skill_up.reshape(local_skills, rank * slice_out),
        ],
        1,
    ).astype(F32)
    partial_sum = jnp.dot(alloc, stacked, precision=lax.Precision.HIGHEST)
    composed = lax.psum(partial_sum.astype(BF16), "skill")
    factors = jnp.take(composed, block_tenant, axis=0)
    down_part = factors[:, :down_size].reshape(blocks, slice_width, rank)
    up_part = factors[:, down_size:].reshape(blocks, rank, slice_out).astype(F32)
    grouped = tokens.reshape(blocks, block_rows, width)
    projected = jnp.einsum("bnd,bdr->bnr", grouped, down_part, preferred_element_type=F32)
    base_term = jnp.dot(tokens, base_weight, preferred_element_type=F32)
    lowrank = lax.psum(projected.astype(BF16), ("tensor", "dp")).astype(F32)
    base = lax.psum_scatter(
        base_term.astype(BF16), ("tensor", "dp"), scatter_dimension=1, tiled=True
    ).astype(F32)
    adapter = jnp.einsum("bnr,bro->bno", lowrank, up_part, precision=lax.Precision.HIGHEST)
    total = base.reshape(blocks, block_rows, slice_out) + adapter
    live = (jnp.arange(block_rows, dtype=I32)[None, :] < block_len[:, None])[:, :, None]
    return jnp.where(live, total, 0.0).astype(BF16).reshape(rows, slice_out)


def solution(mesh):
    placed = (
        P(("group", "skill"), ("tensor", "dp")),
        P(("tensor", "dp"), None),
        P("skill", ("tensor", "dp"), None),
        P("skill", None, ("tensor", "dp")),
        P("group", "skill"),
        P(("group", "skill")),
        P(("group", "skill")),
    )
    n = mesh.shape["skill"]
    if n == 4 and mesh.shape["tensor"] == 2 and mesh.shape["dp"] == 2:
        body = functools.partial(line_body, n)
    else:
        body = plain_body
    return jax.shard_map(
        body,
        mesh=mesh,
        in_specs=placed,
        out_specs=P(("group", "skill"), ("tensor", "dp")),
        check_vma=False,
    )
```

```python
import functools

import jax
import jax.numpy as jnp
from jax import lax
from jax.experimental import pallas as pl
from jax.experimental.pallas import tpu as pltpu
from jax.sharding import PartitionSpec as P

F32, BF16, I32 = jnp.float32, jnp.bfloat16, jnp.int32
MIB = 1 << 20
LANES = 128
LARGE = 1 << 21
SHARE = 1.0
VMEM = pl.BlockSpec(memory_space=pltpu.VMEM)
SMEM = pl.BlockSpec(memory_space=pltpu.SMEM)
ANY = pl.BlockSpec(memory_space=pl.ANY)
NT = (((1,), (1,)), ((), ()))
TN = (((0,), (0,)), ((), ()))
PLANS = ((18, 16, 12), (20, 18, 12), (23, 21, 12))


def call(kernel, ins, specs, outs, out_specs, *, after=(), vmem=24, flops=0, nbytes=0, **kwargs):
    return pl.pallas_call(
        functools.partial(kernel, len(ins)),
        in_specs=specs + [ANY] * len(after),
        out_specs=out_specs,
        out_shape=outs,
        compiler_params=pltpu.CompilerParams(vmem_limit_bytes=vmem * MIB),
        cost_estimate=pl.CostEstimate(flops=int(SHARE * flops), bytes_accessed=int(SHARE * nbytes), transcendentals=0),
        **kwargs,
    )(*[placed(x) for x in ins], *after)


def placed(x):
    if x.dtype != BF16:
        return x
    return pltpu.with_memory_space_constraint(x, pltpu.HBM if x.size >= LARGE else pltpu.VMEM)


def shape(*dims, dtype=BF16):
    return jax.ShapeDtypeStruct(dims, dtype)


def kron_kernel(rank, ins, alloc_ref, kron_ref):
    tenants, skills = alloc_ref.shape
    depth = skills * rank
    at = lax.broadcasted_iota(I32, (skills, depth), 1)
    row = lax.broadcasted_iota(I32, (skills, depth), 0)
    inside = jnp.logical_and(at >= row * rank, at < (row + 1) * rank)
    repeat = jnp.where(inside, 1.0, 0.0).astype(BF16)
    spread = jnp.dot(alloc_ref[...].astype(BF16), repeat, preferred_element_type=F32)
    lane = lax.rem(lax.broadcasted_iota(I32, (rank, depth), 1), rank)
    diagonal = lane == lax.broadcasted_iota(I32, (rank, depth), 0)
    for t in range(tenants):
        kron_ref[t * rank : (t + 1) * rank, :] = jnp.where(diagonal, spread[t : t + 1, :], 0.0).astype(BF16)


def make_kron(alloc, rank):
    tenants, skills = alloc.shape
    return call(
        functools.partial(kron_kernel, rank), [alloc], [VMEM], shape(tenants * rank, skills * rank), VMEM, vmem=16
    )


def compose_kernel(slots, ins, *refs):
    kron_ref, library_ref = refs[:2] if not slots else refs[1:3]
    own_ref = refs[-2] if slots else refs[-1]
    tenants, rank, size = own_ref.shape
    made = jnp.dot(kron_ref[...], library_ref[...], preferred_element_type=F32).astype(BF16)
    own_ref[...] = made.reshape(tenants, rank, size)
    if slots:
        copy_slots(refs[0], own_ref, refs[-1], slots)


def copy_slots(tab_ref, own_ref, out_ref, slots):
    def one(slot, carry):
        out_ref[slot] = own_ref[tab_ref[0, slot]]
        return carry

    lax.fori_loop(0, slots, one, 0, unroll=2)


def compose(kron, library, rank, part, tile, slots=0, tab=None, after=()):
    rows, depth = kron.shape
    tenants = rows // rank
    start, size = part
    at = start // tile
    outs, out_specs = [shape(tenants, rank, size)], [pl.BlockSpec((tenants, rank, tile), lambda j: (0, 0, j))]
    if slots:
        outs.append(shape(slots, rank, size))
        out_specs.append(pl.BlockSpec((slots, rank, tile), lambda j: (0, 0, j)))
    made = call(
        functools.partial(compose_kernel, slots),
        ([tab] if slots else []) + [kron, library],
        ([SMEM] if slots else []) + [VMEM, pl.BlockSpec((depth, tile), lambda j: (0, at + j))],
        outs,
        out_specs,
        after=after,
        grid=(size // tile,),
        flops=2 * rows * depth * size,
        nbytes=2 * (depth + rows) * size,
    )
    return made if slots else made[0]


def tables_kernel(n, tenants, plans, ins, place_ref, *refs):
    arrays, tab_ref, plan_ref = refs[:-2], refs[-2], refs[-1]
    me = place_ref[0]
    blocks = arrays[0].shape[1]
    sub = lax.broadcasted_iota(I32, (tenants, tenants), 0)
    lane = lax.broadcasted_iota(I32, (tenants, tenants), 1)
    wide = lax.broadcasted_iota(I32, (tenants, LANES), 1)
    tenant = lax.broadcasted_iota(I32, (tenants, LANES), 0)
    one = lax.broadcasted_iota(I32, (tenants, blocks), 0)
    zs = [lax.rem(me - k + n, n) for k in range(n)]
    groups = len(arrays)
    present = [
        [
            jnp.max(jnp.where(one == arrays[g][k : k + 1, :], 1.0, 0.0), axis=1, keepdims=True)
            for k in range(n)
        ]
        for g in range(groups)
    ]

    def union(keep, group=0):
        total = jnp.zeros((tenants, 1), F32)
        for z, here in zip(zs, present[group]):
            total = jnp.maximum(total, here * jnp.where(keep(z), 1.0, 0.0))
        return total

    def positions(held):
        across = jnp.sum(jnp.where(sub == lane, held, 0.0), axis=0, keepdims=True)
        return jnp.sum(jnp.where(lane < sub, across, 0.0), axis=1, keepdims=True)

    def pack(held, value):
        slot = positions(held).astype(I32)
        chosen = jnp.logical_and(slot == wide, held > 0.5)
        return jnp.sum(jnp.where(chosen, value, 0.0), axis=0, keepdims=True)

    send_right, send_left = union(lambda z: z > me), union(lambda z: z < me)
    from_left, from_right = positions(union(lambda z: z >= me)), positions(union(lambda z: z <= me))
    number = tenant.astype(F32)
    right = pack(send_right, number), pack(send_right, from_left)
    left = pack(send_left, number), pack(send_left, from_right)
    own = jnp.concatenate([arrays[0][0:1, :], jnp.zeros((1, LANES - blocks), I32)], axis=1)
    mine = own == tenant

    def at(place, rows, otherwise):
        return jnp.where(me == place, rows, otherwise)

    none = jnp.zeros((1, LANES), F32)
    final_right = jnp.sum(jnp.where(mine, from_left, 0.0), axis=0, keepdims=True)
    final_left = jnp.sum(jnp.where(mine, from_right, 0.0), axis=0, keepdims=True)
    rows = []
    for part in (0, 1):
        for hop in range(n - 1):
            rows.append(at(hop, right[part], at(n - 1 - hop, left[part], none)))
    for hop in range(n - 1):
        rows.append(at(hop + 1, final_right, at(n - 2 - hop, final_left, none)))
    for row, value in enumerate(rows):
        tab_ref[row : row + 1, :] = value.astype(I32)
    tab_ref[len(rows) : len(rows) + 1, :] = own
    ends_here = jnp.logical_or(me == 0, me == n - 1)
    tab_ref[len(rows) + 1 : len(rows) + 2, :] = jnp.where(ends_here, jnp.ones_like(own), jnp.zeros_like(own))

    held = jnp.zeros((tenants, LANES), F32)
    hop_of = lax.broadcasted_iota(I32, (1, LANES), 1)
    limits = [jnp.full((1, LANES), float(tenants), F32) for _ in plans]
    column = 0
    for group in range(groups):
        for hop in range(n - 1):
            for keep in (lambda z: z > hop, lambda z: z < n - 1 - hop):
                held = jnp.where(wide == column, union(keep, group), held)
                limits = [jnp.where(hop_of == column, float(p[hop]), l) for p, l in zip(plans, limits)]
                column += 1
    counts = jnp.sum(held, axis=0, keepdims=True)
    plan = jnp.int32(0)
    for limit in limits[:-1]:
        plan = plan + jnp.where(jnp.max(counts - limit) > 0.5, 1, 0)
    plan_ref[0] = plan


def make_tables(n, tenants, plans, place, arrays):
    rows = -(-(3 * (n - 1) + 2) // 8) * 8
    return call(
        functools.partial(tables_kernel, n, tenants, plans),
        [place, *arrays],
        [SMEM] + [VMEM] * len(arrays),
        [shape(rows, LANES, dtype=I32), shape(1, dtype=I32)],
        [VMEM, SMEM],
    )


def step_kernel(n, jobs, passed, ins, *refs):
    tab_ref = refs[0]
    ins -= 1
    given, outs = list(refs[1 : 1 + ins]), refs[1 + ins + passed : 1 + ins + passed + len(jobs)]
    for (hop, slots, by_tenant), out_ref in zip(jobs, outs):
        own_ref = given.pop(0)
        in_ref = given.pop(0) if hop else None

        def one(slot, carry, hop=hop, by_tenant=by_tenant, own_ref=own_ref, in_ref=in_ref, out_ref=out_ref):
            tenant = tab_ref[hop, slot]
            block = own_ref[tenant]
            if hop:
                index = tenant if by_tenant else tab_ref[n - 1 + hop, slot]
                block = (block.astype(F32) + in_ref[index].astype(F32)).astype(BF16)
            out_ref[slot] = block
            return carry

        lax.fori_loop(0, slots, one, 0, unroll=4)


def step(n, tab, jobs, after=(), through=()):
    ins, shapes, plan = [], [], []
    for hop, slots, own, arrived, by_tenant in jobs:
        plan.append((hop, slots, by_tenant))
        ins += [own, arrived] if hop else [own]
        shapes.append(jax.ShapeDtypeStruct((slots,) + own.shape[1:], BF16))
    return call(
        functools.partial(step_kernel, n, plan, len(after) + len(through)),
        [tab, *ins],
        [SMEM] + [VMEM] * len(ins),
        shapes + [shape(*x.shape) for x in through],
        [VMEM] * len(shapes) + [ANY] * len(through),
        after=list(after) + list(through),
        input_output_aliases={1 + len(ins) + len(after) + i: len(shapes) + i for i in range(len(through))},
        nbytes=sum(2 * 3 * x.size for x in shapes),
    )


def factor_of(n, b, by_tenant, tab_ref, own_ref, arrived):
    tenant = tab_ref[3 * (n - 1), b]
    factor = own_ref[tenant].astype(F32)
    outer = tab_ref[3 * (n - 1) + 1, 0] > 0
    for hop in range(n - 1):
        index = tenant if by_tenant and hop == 0 else tab_ref[2 * (n - 1) + hop, b]
        came = arrived[hop][index].astype(F32)
        used = jnp.where(outer, 1, 0) if hop == n - 2 else jnp.where(outer, 0, 1)
        factor = jnp.where(used > 0, factor + came, factor)
    return factor.astype(BF16)


def project_kernel(n, first, out, ins, tab_ref, tokens_ref, own_ref, *refs):
    arrived = refs[: n - 1]
    total_ref = None if first else refs[ins - 4]
    outs = refs[-2:] if out else refs[-1:]
    size = tokens_ref.shape[1]

    def one(b, carry):
        factor = factor_of(n, b, False, tab_ref, own_ref, arrived)
        at = pl.ds(pl.multiple_of(b * LANES, LANES), LANES)
        part = lax.dot_general(factor, tokens_ref[at, :], NT, preferred_element_type=F32)
        if not first:
            part = total_ref[:, at] + part
        outs[0][:, at] = part.astype(outs[0].dtype)
        if out:
            outs[1][b] = factor_of(n, b, True, tab_ref, refs[n - 1], refs[n : 2 * n - 1])
        return carry

    lax.fori_loop(0, tokens_ref.shape[0] // LANES, one, 0, unroll=4)


def project(n, tab, tokens, own, part, arrived, total, last, up=None, after=()):
    tenants, rank, size = own.shape
    rows = tokens.shape[0]
    at = part[0] // size
    outs = [shape(rank, rows, dtype=BF16 if last else F32)]
    ins = [tab, tokens, own, *arrived]
    if up:
        outs.append(shape(rows // LANES, rank, up[0].shape[2]))
        ins += [up[0], *up[1]]
    if total is not None:
        ins.append(total)
    return call(
        functools.partial(project_kernel, n, total is None, up is not None),
        ins,
        [SMEM, pl.BlockSpec((rows, size), lambda j: (0, at))] + [VMEM] * (len(ins) - 2),
        outs,
        [VMEM] * len(outs),
        after=after,
        grid=(1,),
        flops=2 * rows * size * rank,
        nbytes=2 * size * (rows + 2 * tenants * rank),
    )


def base_kernel(order_ref, tokens_ref, weight_ref, *refs):
    refs[-1][0] = jnp.dot(tokens_ref[...], weight_ref[...], preferred_element_type=F32).astype(BF16)


def base_product(order, tokens, weight, out, after):
    rows, width = tokens.shape
    flops, nbytes = 4 * rows * width * out, 2 * (rows * (width + 2 * out) + 2 * width * out)
    return pl.pallas_call(
        base_kernel,
        grid_spec=pltpu.PrefetchScalarGridSpec(
            num_scalar_prefetch=1,
            grid=(2, 2),
            in_specs=[
                pl.BlockSpec((rows // 2, width), lambda q, m, order: ((q + m) % 2, 0)),
                pl.BlockSpec((width, out), lambda q, m, order: (0, order[q])),
            ]
            + [ANY] * len(after),
            out_specs=pl.BlockSpec((1, rows // 2, out), lambda q, m, order: (q, (q + m) % 2, 0)),
        ),
        out_shape=shape(2, rows, out),
        compiler_params=pltpu.CompilerParams(vmem_limit_bytes=24 * MIB),
        cost_estimate=pl.CostEstimate(flops=int(SHARE * flops), bytes_accessed=int(SHARE * nbytes), transcendentals=0),
    )(order, placed(tokens), placed(weight), *after)


def gather_kernel(ins, a_ref, b_ref, c_ref, out_ref):
    out_ref[...] = (a_ref[0].astype(F32) + b_ref[0].astype(F32) + c_ref[...].astype(F32)).astype(out_ref.dtype)


def gather_base(keep, from_core, across):
    rows, width = across.shape
    half = pl.BlockSpec((1, rows, width), lambda j: (1, 0, 0))
    whole = pl.BlockSpec((rows, width), lambda j: (0, 0))
    return call(
        gather_kernel,
        [keep, from_core, across],
        [half, half, whole],
        shape(rows, width),
        whole,
        nbytes=8 * rows * width,
        grid=(1,),
    )


def finish_kernel(per, ins, len_ref, up_ref, *refs):
    lows, base_ref, out_ref = refs[:4], refs[4], refs[5]
    width = out_ref.shape[1]
    for j in range(per):
        b = pl.program_id(0) * per + j
        at = slice(j * LANES, (j + 1) * LANES)
        low = lows[0][:, at].astype(F32)
        for other in lows[1:]:
            low = low + other[:, at].astype(F32)
        high = low.astype(BF16)
        rest = (low - high.astype(F32)).astype(BF16)
        total = lax.dot_general(high, up_ref[b], TN, preferred_element_type=F32)
        total = total + lax.dot_general(rest, up_ref[b], TN, preferred_element_type=F32)
        total = total + base_ref[at, :].astype(F32)
        live = lax.broadcasted_iota(I32, (LANES, width), 0) < len_ref[b]
        out_ref[at, :] = jnp.where(live, total, 0.0).astype(out_ref.dtype)


def finish(lens, up, lows, base, per):
    rank, rows = lows[0].shape
    width = base.shape[1]
    blocks = rows // LANES
    whole = pl.BlockSpec((per * LANES, width), lambda j: (j, 0))
    return call(
        functools.partial(finish_kernel, per),
        [lens, up, *lows, base],
        [SMEM, VMEM] + [pl.BlockSpec((rank, per * LANES), lambda j: (0, j))] * 4 + [whole],
        shape(rows, width),
        whole,
        grid=(blocks // per,),
        flops=4 * rows * rank * width,
        nbytes=8 * rows * width,
    )


def swap(x, axis):
    return lax.ppermute(x, axis, [(0, 1), (1, 0)])


def ends(x):
    return lax.ppermute(x, "skill", [(0, 1), (1, 0), (2, 3), (3, 2)])


def middle(x):
    pairs = [(2 + c, 4 + c) for c in (0, 1)] + [(0, 1), (6, 7)]
    return lax.ppermute(x, ("skill", "tensor"), pairs + [(b, a) for a, b in pairs])


def line_body(tokens, base_weight, skill_down, skill_up, alloc, block_tenant, block_len):
    n = 4
    rows, width = tokens.shape
    tenants, local_skills = alloc.shape
    rank = skill_down.shape[2]
    out = skill_up.shape[2]
    blocks = block_len.shape[0]
    me = lax.axis_index("skill")
    tensor, dp = lax.axis_index("tensor"), lax.axis_index("dp")
    hops = [ends, middle, ends]
    full = [min(tenants, blocks * (n - 1 - h)) for h in range(n - 1)]
    plans = [[min(f, p) for f, p in zip(full, plan)] for plan in PLANS] + [full]
    tile = width // 8
    parts = [(0, 3 * tile), (3 * tile, 3 * tile), (6 * tile, 2 * tile)]

    own_t = block_tenant.reshape(1, blocks)
    seen = jnp.concatenate(
        [own_t]
        + [lax.ppermute(own_t, "skill", [(j, (j + k) % n) for j in range(n)]) for k in range(1, n)],
        axis=0,
    )
    seen = [seen, swap(seen, "group")]
    kron = make_kron(alloc, rank)
    library = jnp.transpose(skill_down, (0, 2, 1)).reshape(local_skills * rank, width)
    own_up = compose(kron, skill_up.reshape(local_skills * rank, out), rank, (0, out), out, after=[seen[0]])
    up_0 = ends(own_up)
    own_0 = compose(kron, library, rank, parts[0], tile, after=[own_up])
    tab, plan = make_tables(n, tenants, plans, me.reshape(1).astype(I32), seen)
    other, mine = (1 - tensor) * 2, tensor * 2
    order_away = jnp.stack([other + 1 - dp, other + dp]).astype(I32)
    order_keep = jnp.stack([mine + 1 - dp, mine + dp]).astype(I32)

    def planned(sizes):
        owns, arrived, up_came = [own_0], [[], [], []], [up_0]

        def job(h, k):
            return h, sizes[h], owns[k], arrived[k][h - 1] if h else None, False

        def up_job(h):
            return h, sizes[h], own_up, up_came[h - 1], h == 1

        first, up_1 = step(n, tab, [job(0, 0), up_job(1)])
        arrived[0].append(ends(first))
        up_came.append(middle(up_1))
        sent = []
        for k in (1, 2):
            own, message = compose(kron, library, rank, parts[k], tile, sizes[0], tab)
            owns.append(own)
            sent.append(message)
            arrived[k].append(ends(message))

        to_1, up_2 = step(n, tab, [job(1, 0), up_job(2)], sent)
        arrived[0].append(middle(to_1))
        up_came.append(ends(up_2))
        away = base_product(order_away, tokens, base_weight, out, [to_1])

        to_1, to_2, away = step(n, tab, [job(1, 1), job(2, 0)], [], [away])
        arrived[1].append(middle(to_1))
        arrived[0].append(ends(to_2))
        from_core = swap(away, "tensor")
        keep = base_product(order_keep, tokens, base_weight, out, [to_1])

        to_1, to_2, keep = step(n, tab, [job(1, 2), job(2, 1)], [from_core, up_came[2]], [keep])
        arrived[2].append(middle(to_1))
        arrived[1].append(ends(to_2))
        near = (keep[0].astype(F32) + from_core[0].astype(F32)).astype(BF16)
        across = swap(near, "dp")
        low, up = project(n, tab, tokens, owns[0], parts[0], arrived[0], None, False, (own_up, up_came), [to_1])

        (to_2,) = step(n, tab, [job(2, 2)], [low])
        arrived[2].append(ends(to_2))
        (low,) = project(n, tab, tokens, owns[1], parts[1], arrived[1], low, False)
        base = gather_base(keep, from_core, across)
        (low,) = project(n, tab, tokens, owns[2], parts[2], arrived[2], low, True, None, [base])
        return low, up, base

    low, up, base = lax.switch(plan[0], [functools.partial(planned, sizes) for sizes in plans])
    lows = [low, swap(low, "tensor"), swap(low, "dp")]
    lows.append(lax.ppermute(low, ("tensor", "dp"), [(0, 3), (1, 2), (2, 1), (3, 0)]))
    return finish(block_len, up, lows, base, 6)


def plain_body(tokens, base_weight, skill_down, skill_up, alloc, block_tenant, block_len):
    rows, width = tokens.shape
    blocks = block_len.shape[0]
    block_rows = rows // blocks
    local_skills, slice_width, rank = skill_down.shape
    slice_out = skill_up.shape[2]
    down_size = slice_width * rank
    stacked = jnp.concatenate(
        [
            skill_down.reshape(local_skills, down_size),
            skill_up.reshape(local_skills, rank * slice_out),
        ],
        1,
    ).astype(F32)
    partial_sum = jnp.dot(alloc, stacked, precision=lax.Precision.HIGHEST)
    composed = lax.psum(partial_sum.astype(BF16), "skill")
    factors = jnp.take(composed, block_tenant, axis=0)
    down_part = factors[:, :down_size].reshape(blocks, slice_width, rank)
    up_part = factors[:, down_size:].reshape(blocks, rank, slice_out).astype(F32)
    grouped = tokens.reshape(blocks, block_rows, width)
    projected = jnp.einsum("bnd,bdr->bnr", grouped, down_part, preferred_element_type=F32)
    base_term = jnp.dot(tokens, base_weight, preferred_element_type=F32)
    lowrank = lax.psum(projected.astype(BF16), ("tensor", "dp")).astype(F32)
    base = lax.psum_scatter(
        base_term.astype(BF16), ("tensor", "dp"), scatter_dimension=1, tiled=True
    ).astype(F32)
    adapter = jnp.einsum("bnr,bro->bno", lowrank, up_part, precision=lax.Precision.HIGHEST)
    total = base.reshape(blocks, block_rows, slice_out) + adapter
    live = (jnp.arange(block_rows, dtype=I32)[None, :] < block_len[:, None])[:, :, None]
    return jnp.where(live, total, 0.0).astype(BF16).reshape(rows, slice_out)


def solution(mesh):
    placed = (
        P(("group", "skill"), ("tensor", "dp")),
        P(("tensor", "dp"), None),
        P("skill", ("tensor", "dp"), None),
        P("skill", None, ("tensor", "dp")),
        P("group", "skill"),
        P(("group", "skill")),
        P(("group", "skill")),
    )
    fits = (mesh.shape["skill"], mesh.shape["tensor"], mesh.shape["dp"]) == (4, 2, 2)
    body = line_body if fits else plain_body
    return jax.shard_map(
        body,
        mesh=mesh,
        in_specs=placed,
        out_specs=P(("group", "skill"), ("tensor", "dp")),
        check_vma=False,
    )
```

```python
import functools

import jax
import jax.numpy as jnp
from jax import lax
from jax.experimental import pallas as pl
from jax.experimental.pallas import tpu as pltpu
from jax.sharding import PartitionSpec as P

F32, BF16, I32 = jnp.float32, jnp.bfloat16, jnp.int32
MIB = 1 << 20
LANES = 128
LARGE = 1 << 21
PER = 6
SHARE = 1.0
VMEM = pl.BlockSpec(memory_space=pltpu.VMEM)
SMEM = pl.BlockSpec(memory_space=pltpu.SMEM)
ANY = pl.BlockSpec(memory_space=pl.ANY)
NT = (((1,), (1,)), ((), ()))
TN = (((0,), (0,)), ((), ()))
PLANS = ((17, 15, 10), (18, 16, 11), (20, 17, 12), (23, 20, 12))


def call(kernel, ins, specs, outs, out_specs, *, after=(), free=None, vmem=24, flops=0, nbytes=0, **kwargs):
    return pl.pallas_call(
        functools.partial(kernel, len(ins)),
        in_specs=specs + [ANY] * len(after),
        out_specs=out_specs,
        out_shape=outs,
        compiler_params=pltpu.CompilerParams(vmem_limit_bytes=vmem * MIB),
        cost_estimate=pl.CostEstimate(flops=int(SHARE * flops), bytes_accessed=int(SHARE * nbytes), transcendentals=0),
        **kwargs,
    )(*[x if free is True or x is free else placed(x) for x in ins], *after)


def placed(x):
    if x.dtype != BF16:
        return x
    return pltpu.with_memory_space_constraint(x, pltpu.HBM if x.size >= LARGE else pltpu.VMEM)


def shape(*dims, dtype=BF16):
    return jax.ShapeDtypeStruct(dims, dtype)


def kron_kernel(rank, ins, alloc_ref, kron_ref):
    tenants, skills = alloc_ref.shape
    depth = skills * rank
    at = lax.broadcasted_iota(I32, (skills, depth), 1)
    row = lax.broadcasted_iota(I32, (skills, depth), 0)
    inside = jnp.logical_and(at >= row * rank, at < (row + 1) * rank)
    repeat = jnp.where(inside, 1.0, 0.0).astype(BF16)
    spread = jnp.dot(alloc_ref[...].astype(BF16), repeat, preferred_element_type=F32)
    lane = lax.rem(lax.broadcasted_iota(I32, (rank, depth), 1), rank)
    diagonal = lane == lax.broadcasted_iota(I32, (rank, depth), 0)
    for t in range(tenants):
        kron_ref[t * rank : (t + 1) * rank, :] = jnp.where(diagonal, spread[t : t + 1, :], 0.0).astype(BF16)


def first_kernel(rank, ins, alloc_ref, library_ref, own_ref, kron_ref):
    kron_kernel(rank, 1, alloc_ref, kron_ref)
    made = jnp.dot(kron_ref[...], library_ref[...], preferred_element_type=F32).astype(BF16)
    own_ref[...] = made.reshape(own_ref.shape)


def compose_first(alloc, library, rank):
    tenants, skills = alloc.shape
    depth, out = library.shape
    return call(
        functools.partial(first_kernel, rank),
        [pltpu.with_memory_space_constraint(x, pltpu.HBM) for x in (alloc, library)],
        [pl.BlockSpec(x.shape, lambda j: (0, 0)) for x in (alloc, library)],
        [shape(tenants, rank, out), shape(tenants * rank, depth)],
        [VMEM] * 2,
        free=True,
        grid=(1,),
        flops=2 * tenants * rank * depth * out,
        nbytes=2 * depth * out,
    )


def compose_kernel(slots, ins, *refs):
    kron_ref, library_ref = refs[:2] if not slots else refs[1:3]
    own_ref = refs[-2] if slots else refs[-1]
    tenants, rank, size = own_ref.shape
    made = jnp.dot(kron_ref[...], library_ref[...], preferred_element_type=F32).astype(BF16)
    own_ref[...] = made.reshape(tenants, rank, size)
    if slots:
        copy_slots(refs[0], own_ref, refs[-1], slots)


def copy_slots(tab_ref, own_ref, out_ref, slots):
    def one(slot, carry):
        out_ref[slot] = own_ref[tab_ref[0, slot]]
        return carry

    lax.fori_loop(0, slots, one, 0, unroll=2)


def compose(kron, library, rank, part, tile, slots=0, tab=None, after=()):
    rows, depth = kron.shape
    tenants = rows // rank
    start, size = part
    at = start // tile
    outs, out_specs = [shape(tenants, rank, size)], [pl.BlockSpec((tenants, rank, tile), lambda j: (0, 0, j))]
    if slots:
        outs.append(shape(slots, rank, size))
        out_specs.append(pl.BlockSpec((slots, rank, tile), lambda j: (0, 0, j)))
    made = call(
        functools.partial(compose_kernel, slots),
        ([tab] if slots else []) + [kron, library],
        ([SMEM] if slots else []) + [VMEM, pl.BlockSpec((depth, tile), lambda j: (0, at + j))],
        outs,
        out_specs,
        after=after,
        grid=(size // tile,),
        flops=2 * rows * depth * size,
        nbytes=2 * (depth + rows) * size,
    )
    return made if slots else made[0]


def tables_kernel(n, tenants, plans, ins, place_ref, len_ref, *refs):
    arrays, tab_ref, plan_ref = refs[:-2], refs[-2], refs[-1]
    me = place_ref[0]
    blocks = arrays[0].shape[1]
    sub = lax.broadcasted_iota(I32, (tenants, tenants), 0)
    lane = lax.broadcasted_iota(I32, (tenants, tenants), 1)
    wide = lax.broadcasted_iota(I32, (tenants, LANES), 1)
    tenant = lax.broadcasted_iota(I32, (tenants, LANES), 0)
    one = lax.broadcasted_iota(I32, (tenants, blocks), 0)
    zs = [lax.rem(me - k + n, n) for k in range(n)]
    groups = len(arrays)
    present = [
        [
            jnp.max(jnp.where(one == arrays[g][k : k + 1, :], 1.0, 0.0), axis=1, keepdims=True)
            for k in range(n)
        ]
        for g in range(groups)
    ]

    def union(keep, group=0):
        total = jnp.zeros((tenants, 1), F32)
        for z, here in zip(zs, present[group]):
            total = jnp.maximum(total, here * jnp.where(keep(z), 1.0, 0.0))
        return total

    def positions(held):
        across = jnp.sum(jnp.where(sub == lane, held, 0.0), axis=0, keepdims=True)
        return jnp.sum(jnp.where(lane < sub, across, 0.0), axis=1, keepdims=True)

    def pack(held, value):
        slot = positions(held).astype(I32)
        chosen = jnp.logical_and(slot == wide, held > 0.5)
        return jnp.sum(jnp.where(chosen, value, 0.0), axis=0, keepdims=True)

    send_right, send_left = union(lambda z: z > me), union(lambda z: z < me)
    from_left, from_right = positions(union(lambda z: z >= me)), positions(union(lambda z: z <= me))
    number = tenant.astype(F32)
    right = pack(send_right, number), pack(send_right, from_left)
    left = pack(send_left, number), pack(send_left, from_right)
    own = jnp.concatenate([arrays[0][0:1, :], jnp.zeros((1, LANES - blocks), I32)], axis=1)
    mine = own == tenant

    def at(place, rows, otherwise):
        return jnp.where(me == place, rows, otherwise)

    none = jnp.zeros((1, LANES), F32)
    final_right = jnp.sum(jnp.where(mine, from_left, 0.0), axis=0, keepdims=True)
    final_left = jnp.sum(jnp.where(mine, from_right, 0.0), axis=0, keepdims=True)
    rows = []
    for part in (0, 1):
        for hop in range(n - 1):
            rows.append(at(hop, right[part], at(n - 1 - hop, left[part], none)))
    for hop in range(n - 1):
        rows.append(at(hop + 1, final_right, at(n - 2 - hop, final_left, none)))
    for row, value in enumerate(rows):
        tab_ref[row : row + 1, :] = value.astype(I32)
    tab_ref[len(rows) : len(rows) + 1, :] = own
    tab_ref[len(rows) + 2 : len(rows) + 3, :] = jnp.concatenate([len_ref[...], jnp.zeros((1, LANES - blocks), I32)], axis=1)
    ends_here = jnp.logical_or(me == 0, me == n - 1)
    tab_ref[len(rows) + 1 : len(rows) + 2, :] = jnp.where(ends_here, jnp.ones_like(own), jnp.zeros_like(own))

    held = jnp.zeros((tenants, LANES), F32)
    hop_of = lax.broadcasted_iota(I32, (1, LANES), 1)
    limits = [jnp.full((1, LANES), float(tenants), F32) for _ in plans]
    column = 0
    for group in range(groups):
        for hop in range(n - 1):
            for keep in (lambda z: z > hop, lambda z: z < n - 1 - hop):
                held = jnp.where(wide == column, union(keep, group), held)
                limits = [jnp.where(hop_of == column, float(p[hop]), l) for p, l in zip(plans, limits)]
                column += 1
    counts = jnp.sum(held, axis=0, keepdims=True)
    plan = jnp.int32(0)
    for limit in limits[:-1]:
        plan = plan + jnp.where(jnp.max(counts - limit) > 0.5, 1, 0)
    plan_ref[0] = plan


def make_tables(n, tenants, plans, place, lens, arrays):
    rows = -(-(3 * (n - 1) + 3) // 8) * 8
    return call(
        functools.partial(tables_kernel, n, tenants, plans),
        [place, lens, *arrays],
        [SMEM] + [VMEM] * (1 + len(arrays)),
        [shape(rows, LANES, dtype=I32), shape(1, dtype=I32)],
        [VMEM, SMEM],
    )


def step_kernel(n, jobs, passed, ins, tab_ref, *refs):
    given, outs = list(refs[: ins - 1]), refs[ins - 1 + passed :]
    for (hop, slots, pieces), out_ref in zip(jobs, outs):
        both = slots is None
        if both:
            slots = out_ref.shape[0] // 2
            fresh_ref = given.pop(0)

            @pl.when(tab_ref[3 * (n - 1) + 1, 0] > 0)
            def _(fresh_ref=fresh_ref, out_ref=out_ref):
                out_ref[: fresh_ref.shape[0]] = fresh_ref[...]

        held = [(given.pop(0), given.pop(0) if hop else None) for _ in pieces]

        def one(slot, carry, hop=hop, pieces=pieces, held=held, out_ref=out_ref, both=both, slots=slots):
            tenant = tab_ref[hop, slot]
            at = 0
            made = []
            for by_tenant, (own_ref, in_ref) in zip(pieces, held):
                block = own_ref[tenant]
                if hop:
                    index = tenant if by_tenant else tab_ref[n - 1 + hop, slot]
                    block = (block.astype(F32) + in_ref[index].astype(F32)).astype(BF16)
                made.append(block)
            block = jnp.concatenate(made, axis=1) if len(made) > 1 else made[0]
            if both:
                half = out_ref.shape[2]
                out_ref[slot] = block[:, :half]
                out_ref[slots + slot] = block[:, half:]
            else:
                out_ref[slot] = block
            return carry

        def all_slots(one=one, slots=slots):
            lax.fori_loop(0, slots, one, 0, unroll=4)

        if both:
            pl.when(tab_ref[3 * (n - 1) + 1, 0] == 0)(all_slots)
        else:
            all_slots()


def step(n, tab, jobs, after=(), through=()):
    ins, shapes, plan = [], [], []
    for hop, slots, pieces in jobs:
        columns = sum(own.shape[2] for own, _, _ in pieces)
        if isinstance(slots, tuple):
            plan.append((hop, None, [by_tenant for _, _, by_tenant in pieces]))
            ins.append(slots[1])
            slots, columns = 2 * slots[0], columns // 2
            assert slots >= ins[-1].shape[0] and columns == ins[-1].shape[2]
        else:
            plan.append((hop, slots, [by_tenant for _, _, by_tenant in pieces]))
        for own, arrived, _ in pieces:
            ins += [own, arrived] if hop else [own]
        shapes.append(shape(slots, pieces[0][0].shape[1], columns))
    return call(
        functools.partial(step_kernel, n, plan, len(after) + len(through)),
        [tab, *ins],
        [SMEM] + [VMEM] * len(ins),
        shapes + [shape(*x.shape) for x in through],
        [VMEM] * len(shapes) + [ANY] * len(through),
        after=list(after) + list(through),
        input_output_aliases={1 + len(ins) + len(after) + i: len(shapes) + i for i in range(len(through))},
        nbytes=sum(2 * 3 * x.size for x in shapes),
    )


def read(ref, slot, start, size):
    half = ref.shape[2]
    if start + size <= half and start == 0 and size == half:
        return ref[slot]
    slots = ref.shape[0] // 2
    pieces = []
    while size:
        part, at = divmod(start, half)
        count = min(size, half - at)
        pieces.append(ref[part * slots + slot, :, at : at + count])
        start, size = start + count, size - count
    return jnp.concatenate(pieces, axis=1) if len(pieces) > 1 else pieces[0]


def factor_of(n, b, by_tenant, tab_ref, own_ref, arrived, lead=0):
    tenant = tab_ref[3 * (n - 1), b]
    factor = own_ref[tenant].astype(F32)
    outer = tab_ref[3 * (n - 1) + 1, 0] > 0
    for hop in range(n - 1):
        index = tenant if by_tenant and hop == 0 else tab_ref[2 * (n - 1) + hop, b]
        came = read(arrived[hop], index, lead, own_ref.shape[2]) if hop == n - 2 else arrived[hop][index]
        came = came.astype(F32)
        used = jnp.where(outer, 1, 0) if hop == n - 2 else jnp.where(outer, 0, 1)
        factor = jnp.where(used > 0, factor + came, factor)
    return factor.astype(BF16)


def project_kernel(n, first, out, ins, tab_ref, tokens_ref, own_ref, *refs):
    arrived = refs[: n - 1]
    total_ref = None if first else refs[ins - 4]
    outs = refs[-2:] if out else refs[-1:]
    size = tokens_ref.shape[1]

    def one(b, carry):
        factor = factor_of(n, b, False, tab_ref, own_ref, arrived)
        at = pl.ds(pl.multiple_of(b * LANES, LANES), LANES)
        part = lax.dot_general(factor, tokens_ref[at, :], NT, preferred_element_type=F32)
        if not first:
            part = total_ref[:, at] + part
        outs[0][:, at] = part.astype(outs[0].dtype)
        if out:
            outs[1][b] = factor_of(n, b, True, tab_ref, refs[n - 1], refs[n : 2 * n - 1], own_ref.shape[2])
        return carry

    lax.fori_loop(0, tokens_ref.shape[0] // LANES, one, 0, unroll=4)


def project(n, tab, tokens, own, part, arrived, total, last, up=None, after=()):
    tenants, rank, size = own.shape
    rows = tokens.shape[0]
    at = part[0] // size
    outs = [shape(rank, rows, dtype=BF16 if last else F32)]
    ins = [tab, tokens, own, *arrived]
    if up:
        outs.append(shape(rows // LANES, rank, up[0].shape[2]))
        ins += [up[0], *up[1]]
    if total is not None:
        ins.append(total)
    return call(
        functools.partial(project_kernel, n, total is None, up is not None),
        ins,
        [SMEM, pl.BlockSpec((rows, size), lambda j: (0, at))] + [VMEM] * (len(ins) - 2),
        outs,
        [VMEM] * len(outs),
        after=after,
        free=tokens,
        grid=(1,),
        flops=2 * rows * size * rank,
        nbytes=2 * size * (rows + 2 * tenants * rank),
    )


def base_kernel(order_ref, tokens_ref, first_ref, second_ref, *refs):
    for weight_ref, out_ref in ((first_ref, refs[-2]), (second_ref, refs[-1])):
        out_ref[...] = jnp.dot(tokens_ref[...], weight_ref[...], preferred_element_type=F32).astype(BF16)


def base_product(order, tokens, weight, out, after, strips=3):
    rows, width = tokens.shape
    flops, nbytes = 4 * rows * width * out, 2 * (rows * (width + 2 * out) + 2 * width * out)
    return pl.pallas_call(
        base_kernel,
        grid_spec=pltpu.PrefetchScalarGridSpec(
            num_scalar_prefetch=1,
            grid=(strips,),
            in_specs=[
                pl.BlockSpec((rows // strips, width), lambda m, order: (m, 0)),
                pl.BlockSpec((width, out), lambda m, order: (0, order[0])),
                pl.BlockSpec((width, out), lambda m, order: (0, order[1])),
            ]
            + [ANY] * len(after),
            out_specs=[pl.BlockSpec((rows // strips, out), lambda m, order: (m, 0))] * 2,
        ),
        out_shape=[shape(rows, out)] * 2,
        compiler_params=pltpu.CompilerParams(vmem_limit_bytes=24 * MIB),
        cost_estimate=pl.CostEstimate(flops=int(SHARE * flops), bytes_accessed=int(SHARE * nbytes), transcendentals=0),
    )(order, tokens, placed(weight), placed(weight), *after)


def near_kernel(ins, a_ref, b_ref, *outs):
    rows = outs[0].shape[0]
    for i, out_ref in enumerate(outs):
        at = slice(i * rows, (i + 1) * rows)
        out_ref[...] = (a_ref[at, :].astype(F32) + b_ref[at, :].astype(F32)).astype(BF16)


def add_halves(a, b):
    rows, width = a.shape
    return call(near_kernel, [a, b], [VMEM] * 2, [shape(rows // 2, width)] * 2, [VMEM] * 2, nbytes=6 * rows * width)


def gather_kernel(ins, a_ref, b_ref, *refs):
    rows = refs[0].shape[0]
    for i, part_ref in enumerate(refs[: ins - 2]):
        at = slice(i * rows, (i + 1) * rows)
        total = a_ref[at, :].astype(F32) + b_ref[at, :].astype(F32) + part_ref[...].astype(F32)
        refs[-1][at, :] = total.astype(BF16)


def gather_base(a, b, halves, after):
    return call(
        gather_kernel, [a, b, *halves], [VMEM] * 4, shape(*a.shape), VMEM, after=after, nbytes=8 * a.size
    )


def finish_kernel(row, per, ins, tab_ref, up_ref, *refs):
    lows, base_ref, out_ref = refs[:4], refs[4], refs[5]
    width = out_ref.shape[1]
    low = lows[0][...].astype(F32)
    for other in lows[1:]:
        low = low + other[...].astype(F32)
    low = low.astype(BF16)
    for j in range(per):
        b = pl.program_id(0) * per + j
        at = slice(j * LANES, (j + 1) * LANES)
        total = lax.dot_general(low[:, at], up_ref[b], TN, preferred_element_type=F32)
        total = total + base_ref[at, :].astype(F32)
        live = lax.broadcasted_iota(I32, (LANES, width), 0) < tab_ref[row, b]
        out_ref[at, :] = jnp.where(live, total, 0.0).astype(out_ref.dtype)


def finish(tab, row, up, lows, base, per):
    rank, rows = lows[0].shape
    width = base.shape[1]
    blocks = rows // LANES
    whole = pl.BlockSpec((per * LANES, width), lambda j: (j, 0))
    return call(
        functools.partial(finish_kernel, row, per),
        [tab, up, *lows, pltpu.with_memory_space_constraint(base, pltpu.HBM)],
        [SMEM, VMEM] + [pl.BlockSpec((rank, per * LANES), lambda j: (0, j))] * 4 + [whole],
        shape(rows, width),
        whole,
        free=True,
        grid=(blocks // per,),
        flops=2 * rows * rank * width,
        nbytes=4 * rows * width,
    )


def swap(x, axis):
    return lax.ppermute(x, axis, [(0, 1), (1, 0)])


def ends(x):
    return lax.ppermute(x, "skill", [(0, 1), (1, 0), (2, 3), (3, 2)])


def inward(x):
    return lax.ppermute(x, "skill", [(0, 1), (3, 2)])


def outward(x):
    return lax.ppermute(x, "skill", [(1, 0), (2, 3)])


def middle(x):
    pairs = [(2 + c, 4 + c) for c in (0, 1)] + [(0, 1), (6, 7)]
    return lax.ppermute(x, ("skill", "tensor"), pairs + [(b, a) for a, b in pairs])


def line_body(tokens, base_weight, skill_down, skill_up, alloc, block_tenant, block_len):
    n = 4
    rows, width = tokens.shape
    tenants, local_skills = alloc.shape
    rank = skill_down.shape[2]
    out = skill_up.shape[2]
    blocks = block_len.shape[0]
    me = lax.axis_index("skill")
    tensor, dp = lax.axis_index("tensor"), lax.axis_index("dp")
    hops = [ends, middle, ends]
    full = [min(tenants, blocks * (n - 1 - h)) for h in range(n - 1)]
    plans = [[min(f, p) for f, p in zip(full, plan)] for plan in PLANS] + [full]
    tile = width // 8
    parts = [(0, 3 * tile), (3 * tile, 3 * tile), (6 * tile, 2 * tile)]

    own_t = block_tenant.reshape(1, blocks)
    seen = jnp.concatenate(
        [own_t]
        + [lax.ppermute(own_t, "skill", [(j, (j + k) % n) for j in range(n)]) for k in range(1, n)],
        axis=0,
    )
    library = jnp.transpose(skill_down, (0, 2, 1)).reshape(local_skills * rank, width)
    own_up, kron = compose_first(alloc, skill_up.reshape(local_skills * rank, out), rank)
    own_up, seen = lax.optimization_barrier((own_up, seen))
    up_0 = ends(own_up)
    seen = [seen, swap(seen, "group")]
    own_0 = compose(kron, library, rank, parts[0], tile, after=[own_up])
    tab, plan = make_tables(n, tenants, plans, me.reshape(1).astype(I32), block_len.reshape(1, blocks), seen)
    theirs, ours = (1 - tensor) * 2, tensor * 2
    order_cross = jnp.stack([theirs + 1 - dp, ours + 1 - dp]).astype(I32)
    order_stay = jnp.stack([theirs + dp, ours + dp]).astype(I32)

    def planned(sizes):
        owns, arrived, up_came = [own_0], [[], [], []], [up_0]

        def job(h, k):
            return h, sizes[h], [(owns[k], arrived[k][h - 1] if h else None, False)]

        up_piece = (own_up, up_0, True)
        first, up_1 = step(n, tab, [job(0, 0), (1, sizes[1], [up_piece])])
        arrived[0].append(ends(first))
        up_came.append(middle(up_1))
        own, message = compose(kron, library, rank, parts[1], tile, sizes[0], tab)
        owns.append(own)
        arrived[1].append(ends(message))
        away, keep = base_product(order_cross, tokens, base_weight, out, [message])

        to_1, away = step(n, tab, [job(1, 0)], [keep, up_came[1]], [away])
        arrived[0].append(middle(to_1))
        from_core = swap(away, "tensor")
        own, message = compose(kron, library, rank, parts[2], tile, sizes[0], tab, [to_1])
        owns.append(own)

        first_and_up = 2, ((max(sizes[2], (sizes[0] + 1) // 2)), message), [(owns[0], arrived[0][1], False), (own_up, up_came[1], False)]
        to_1, to_2, keep = step(n, tab, [job(1, 1), first_and_up], [from_core], [keep])
        arrived[1].append(middle(to_1))
        exchanged = ends(to_2)
        arrived[0].append(exchanged)
        arrived[2].append(exchanged)
        up_came.append(exchanged)
        near = add_halves(keep, from_core)
        across = [swap(near[0], "dp")]
        away, keep = base_product(order_stay, tokens, base_weight, out, [owns[2]])

        to_1, to_2, away, near_2 = step(
            n, tab, [job(1, 2), job(2, 1)], [across[0], arrived[0][2], keep], [away, near[1]]
        )
        arrived[2].append(middle(to_1))
        arrived[1].append(outward(to_2))
        across.append(swap(near_2, "dp"))
        from_core = swap(away, "tensor")
        low, up = project(n, tab, tokens, owns[0], parts[0], arrived[0], None, False, (own_up, up_came), [to_1])

        (to_2,) = step(n, tab, [job(2, 2)], [low, from_core])
        arrived[2].append(outward(to_2))
        (low,) = project(n, tab, tokens, owns[1], parts[1], arrived[1], low, False, None, [to_2])
        base = gather_base(keep, from_core, across, [low])
        (low,) = project(n, tab, tokens, owns[2], parts[2], arrived[2], low, True, None, [base])
        return low, up, base

    low, up, base = lax.switch(plan[0], [functools.partial(planned, sizes) for sizes in plans])
    lows = [low, swap(low, "tensor"), swap(low, "dp")]
    lows.append(lax.ppermute(low, ("tensor", "dp"), [(0, 3), (1, 2), (2, 1), (3, 0)]))
    return finish(tab, 3 * (n - 1) + 2, up, lows, base, PER)


def plain_body(tokens, base_weight, skill_down, skill_up, alloc, block_tenant, block_len):
    rows, width = tokens.shape
    blocks = block_len.shape[0]
    block_rows = rows // blocks
    local_skills, slice_width, rank = skill_down.shape
    slice_out = skill_up.shape[2]
    down_size = slice_width * rank
    stacked = jnp.concatenate(
        [
            skill_down.reshape(local_skills, down_size),
            skill_up.reshape(local_skills, rank * slice_out),
        ],
        1,
    ).astype(F32)
    partial_sum = jnp.dot(alloc, stacked, precision=lax.Precision.HIGHEST)
    composed = lax.psum(partial_sum.astype(BF16), "skill")
    factors = jnp.take(composed, block_tenant, axis=0)
    down_part = factors[:, :down_size].reshape(blocks, slice_width, rank)
    up_part = factors[:, down_size:].reshape(blocks, rank, slice_out).astype(F32)
    grouped = tokens.reshape(blocks, block_rows, width)
    projected = jnp.einsum("bnd,bdr->bnr", grouped, down_part, preferred_element_type=F32)
    base_term = jnp.dot(tokens, base_weight, preferred_element_type=F32)
    lowrank = lax.psum(projected.astype(BF16), ("tensor", "dp")).astype(F32)
    base = lax.psum_scatter(
        base_term.astype(BF16), ("tensor", "dp"), scatter_dimension=1, tiled=True
    ).astype(F32)
    adapter = jnp.einsum("bnr,bro->bno", lowrank, up_part, precision=lax.Precision.HIGHEST)
    total = base.reshape(blocks, block_rows, slice_out) + adapter
    live = (jnp.arange(block_rows, dtype=I32)[None, :] < block_len[:, None])[:, :, None]
    return jnp.where(live, total, 0.0).astype(BF16).reshape(rows, slice_out)


def solution(mesh):
    placed = (
        P(("group", "skill"), ("tensor", "dp")),
        P(("tensor", "dp"), None),
        P("skill", ("tensor", "dp"), None),
        P("skill", None, ("tensor", "dp")),
        P("group", "skill"),
        P(("group", "skill")),
        P(("group", "skill")),
    )
    fits = (mesh.shape["skill"], mesh.shape["tensor"], mesh.shape["dp"]) == (4, 2, 2)
    body = line_body if fits else plain_body
    return jax.shard_map(
        body,
        mesh=mesh,
        in_specs=placed,
        out_specs=P(("group", "skill"), ("tensor", "dp")),
        check_vma=False,
    )
```

```python
import functools

import jax
import jax.numpy as jnp
from jax import lax
from jax.experimental import pallas as pl
from jax.experimental.pallas import tpu as pltpu
from jax.sharding import PartitionSpec as P

F32, BF16, I32 = jnp.float32, jnp.bfloat16, jnp.int32
MIB = 1 << 20
LANES = 128
LARGE = 1 << 21
PER = 6
EARLY = 0
SHARE = 1.0
VMEM = pl.BlockSpec(memory_space=pltpu.VMEM)
SMEM = pl.BlockSpec(memory_space=pltpu.SMEM)
ANY = pl.BlockSpec(memory_space=pl.ANY)
NT = (((1,), (1,)), ((), ()))
TN = (((0,), (0,)), ((), ()))
PLANS = ((17, 15, 10), (18, 16, 11), (20, 17, 12), (23, 20, 12))


def call(kernel, ins, specs, outs, out_specs, *, after=(), free=None, vmem=24, flops=0, nbytes=0, **kwargs):
    return pl.pallas_call(
        functools.partial(kernel, len(ins)),
        in_specs=specs + [ANY] * len(after),
        out_specs=out_specs,
        out_shape=outs,
        compiler_params=pltpu.CompilerParams(vmem_limit_bytes=vmem * MIB),
        cost_estimate=pl.CostEstimate(flops=int(SHARE * flops), bytes_accessed=int(SHARE * nbytes), transcendentals=0),
        **kwargs,
    )(*[x if free is True or x is free else placed(x) for x in ins], *after)


def placed(x):
    if x.dtype != BF16:
        return x
    return pltpu.with_memory_space_constraint(x, pltpu.HBM if x.size >= LARGE else pltpu.VMEM)


def shape(*dims, dtype=BF16):
    return jax.ShapeDtypeStruct(dims, dtype)


def kron_kernel(rank, ins, alloc_ref, kron_ref):
    tenants, skills = alloc_ref.shape
    depth = skills * rank
    at = lax.broadcasted_iota(I32, (skills, depth), 1)
    row = lax.broadcasted_iota(I32, (skills, depth), 0)
    inside = jnp.logical_and(at >= row * rank, at < (row + 1) * rank)
    repeat = jnp.where(inside, 1.0, 0.0).astype(BF16)
    spread = jnp.dot(alloc_ref[...].astype(BF16), repeat, preferred_element_type=F32)
    lane = lax.rem(lax.broadcasted_iota(I32, (rank, depth), 1), rank)
    diagonal = lane == lax.broadcasted_iota(I32, (rank, depth), 0)
    for t in range(tenants):
        kron_ref[t * rank : (t + 1) * rank, :] = jnp.where(diagonal, spread[t : t + 1, :], 0.0).astype(BF16)


def first_kernel(rank, ins, alloc_ref, library_ref, own_ref, kron_ref):
    kron_kernel(rank, 1, alloc_ref, kron_ref)
    made = jnp.dot(kron_ref[...], library_ref[...], preferred_element_type=F32).astype(BF16)
    own_ref[...] = made.reshape(own_ref.shape)


def compose_first(alloc, library, rank):
    tenants, skills = alloc.shape
    depth, out = library.shape
    return call(
        functools.partial(first_kernel, rank),
        [pltpu.with_memory_space_constraint(x, pltpu.HBM) for x in (alloc, library)],
        [pl.BlockSpec(x.shape, lambda j: (0, 0)) for x in (alloc, library)],
        [shape(tenants, rank, out), shape(tenants * rank, depth)],
        [VMEM] * 2,
        free=True,
        grid=(1,),
        flops=2 * tenants * rank * depth * out,
        nbytes=2 * depth * out,
    )


def compose_kernel(slots, ins, *refs):
    kron_ref, library_ref = refs[:2] if not slots else refs[1:3]
    own_ref = refs[-2] if slots else refs[-1]
    tenants, rank, size = own_ref.shape
    made = jnp.dot(kron_ref[...], library_ref[...], preferred_element_type=F32).astype(BF16)
    own_ref[...] = made.reshape(tenants, rank, size)
    if slots:
        copy_slots(refs[0], own_ref, refs[-1], slots)


def copy_slots(tab_ref, own_ref, out_ref, slots):
    def one(slot, carry):
        out_ref[slot] = own_ref[tab_ref[0, slot]]
        return carry

    lax.fori_loop(0, slots, one, 0, unroll=2)


def compose(kron, library, rank, part, tile, slots=0, tab=None, after=()):
    rows, depth = kron.shape
    tenants = rows // rank
    start, size = part
    at = start // tile
    outs, out_specs = [shape(tenants, rank, size)], [pl.BlockSpec((tenants, rank, tile), lambda j: (0, 0, j))]
    if slots:
        outs.append(shape(slots, rank, size))
        out_specs.append(pl.BlockSpec((slots, rank, tile), lambda j: (0, 0, j)))
    made = call(
        functools.partial(compose_kernel, slots),
        ([tab] if slots else []) + [kron, library],
        ([SMEM] if slots else []) + [VMEM, pl.BlockSpec((depth, tile), lambda j: (0, at + j))],
        outs,
        out_specs,
        after=after,
        grid=(size // tile,),
        flops=2 * rows * depth * size,
        nbytes=2 * (depth + rows) * size,
    )
    return made if slots else made[0]


def tables_kernel(n, tenants, plans, ins, place_ref, len_ref, *refs):
    arrays, tab_ref, plan_ref = refs[:-2], refs[-2], refs[-1]
    me = place_ref[0]
    blocks = arrays[0].shape[1]
    sub = lax.broadcasted_iota(I32, (tenants, tenants), 0)
    lane = lax.broadcasted_iota(I32, (tenants, tenants), 1)
    wide = lax.broadcasted_iota(I32, (tenants, LANES), 1)
    tenant = lax.broadcasted_iota(I32, (tenants, LANES), 0)
    one = lax.broadcasted_iota(I32, (tenants, blocks), 0)
    zs = [me ^ k for k in range(n)]
    groups = len(arrays)
    present = [
        [
            jnp.max(jnp.where(one == arrays[g][k : k + 1, :], 1.0, 0.0), axis=1, keepdims=True)
            for k in range(n)
        ]
        for g in range(groups)
    ]

    def union(keep, group=0):
        total = jnp.zeros((tenants, 1), F32)
        for z, here in zip(zs, present[group]):
            total = jnp.maximum(total, here * jnp.where(keep(z), 1.0, 0.0))
        return total

    def positions(held):
        across = jnp.sum(jnp.where(sub == lane, held, 0.0), axis=0, keepdims=True)
        return jnp.sum(jnp.where(lane < sub, across, 0.0), axis=1, keepdims=True)

    def pack(held, value):
        slot = positions(held).astype(I32)
        chosen = jnp.logical_and(slot == wide, held > 0.5)
        return jnp.sum(jnp.where(chosen, value, 0.0), axis=0, keepdims=True)

    send_right, send_left = union(lambda z: z > me), union(lambda z: z < me)
    from_left, from_right = positions(union(lambda z: z >= me)), positions(union(lambda z: z <= me))
    number = tenant.astype(F32)
    right = pack(send_right, number), pack(send_right, from_left)
    left = pack(send_left, number), pack(send_left, from_right)
    own = jnp.concatenate([arrays[0][0:1, :], jnp.zeros((1, LANES - blocks), I32)], axis=1)
    mine = own == tenant

    def at(place, rows, otherwise):
        return jnp.where(me == place, rows, otherwise)

    none = jnp.zeros((1, LANES), F32)
    final_right = jnp.sum(jnp.where(mine, from_left, 0.0), axis=0, keepdims=True)
    final_left = jnp.sum(jnp.where(mine, from_right, 0.0), axis=0, keepdims=True)
    rows = []
    for part in (0, 1):
        for hop in range(n - 1):
            rows.append(at(hop, right[part], at(n - 1 - hop, left[part], none)))
    for hop in range(n - 1):
        rows.append(at(hop + 1, final_right, at(n - 2 - hop, final_left, none)))
    for row, value in enumerate(rows):
        tab_ref[row : row + 1, :] = value.astype(I32)
    tab_ref[len(rows) : len(rows) + 1, :] = own
    tab_ref[len(rows) + 2 : len(rows) + 3, :] = jnp.concatenate([len_ref[...], jnp.zeros((1, LANES - blocks), I32)], axis=1)
    ends_here = jnp.logical_or(me == 0, me == n - 1)
    tab_ref[len(rows) + 1 : len(rows) + 2, :] = jnp.where(ends_here, jnp.ones_like(own), jnp.zeros_like(own))

    held = jnp.zeros((tenants, LANES), F32)
    hop_of = lax.broadcasted_iota(I32, (1, LANES), 1)
    limits = [jnp.full((1, LANES), float(tenants), F32) for _ in plans]
    column = 0
    for group in range(groups):
        for hop in range(n - 1):
            for keep in (lambda z: z > hop, lambda z: z < n - 1 - hop):
                held = jnp.where(wide == column, union(keep, group), held)
                limits = [jnp.where(hop_of == column, float(p[hop]), l) for p, l in zip(plans, limits)]
                column += 1
    counts = jnp.sum(held, axis=0, keepdims=True)
    plan = jnp.int32(0)
    for limit in limits[:-1]:
        plan = plan + jnp.where(jnp.max(counts - limit) > 0.5, 1, 0)
    plan_ref[0] = plan


def make_tables(n, tenants, plans, place, lens, arrays):
    rows = -(-(3 * (n - 1) + 3) // 8) * 8
    return call(
        functools.partial(tables_kernel, n, tenants, plans),
        [place, lens, *arrays],
        [SMEM] + [VMEM] * (1 + len(arrays)),
        [shape(rows, LANES, dtype=I32), shape(1, dtype=I32)],
        [VMEM, SMEM],
    )


def step_kernel(n, jobs, passed, ins, tab_ref, *refs):
    given, outs = list(refs[: ins - 1]), refs[ins - 1 + passed :]
    for (hop, slots, pieces), out_ref in zip(jobs, outs):
        both = slots is None
        if both:
            slots = out_ref.shape[0] // 2
            fresh_ref = given.pop(0)

            @pl.when(tab_ref[3 * (n - 1) + 1, 0] > 0)
            def _(fresh_ref=fresh_ref, out_ref=out_ref):
                out_ref[: fresh_ref.shape[0]] = fresh_ref[...]

        held = [(given.pop(0), given.pop(0) if hop else None) for _ in pieces]

        def one(slot, carry, hop=hop, pieces=pieces, held=held, out_ref=out_ref, both=both, slots=slots):
            tenant = tab_ref[hop, slot]
            at = 0
            made = []
            for by_tenant, (own_ref, in_ref) in zip(pieces, held):
                block = own_ref[tenant]
                if hop:
                    index = tenant if by_tenant else tab_ref[n - 1 + hop, slot]
                    block = (block.astype(F32) + in_ref[index].astype(F32)).astype(BF16)
                made.append(block)
            block = jnp.concatenate(made, axis=1) if len(made) > 1 else made[0]
            if both:
                half = out_ref.shape[2]
                out_ref[slot] = block[:, :half]
                out_ref[slots + slot] = block[:, half:]
            else:
                out_ref[slot] = block
            return carry

        def all_slots(one=one, slots=slots):
            lax.fori_loop(0, slots, one, 0, unroll=4)

        if both:
            pl.when(tab_ref[3 * (n - 1) + 1, 0] == 0)(all_slots)
        else:
            all_slots()


def step(n, tab, jobs, after=(), through=()):
    ins, shapes, plan = [], [], []
    for hop, slots, pieces in jobs:
        columns = sum(own.shape[2] for own, _, _ in pieces)
        if isinstance(slots, tuple):
            plan.append((hop, None, [by_tenant for _, _, by_tenant in pieces]))
            ins.append(slots[1])
            slots, columns = 2 * slots[0], columns // 2
            assert slots >= ins[-1].shape[0] and columns == ins[-1].shape[2]
        else:
            plan.append((hop, slots, [by_tenant for _, _, by_tenant in pieces]))
        for own, arrived, _ in pieces:
            ins += [own, arrived] if hop else [own]
        shapes.append(shape(slots, pieces[0][0].shape[1], columns))
    return call(
        functools.partial(step_kernel, n, plan, len(after) + len(through)),
        [tab, *ins],
        [SMEM] + [VMEM] * len(ins),
        shapes + [shape(*x.shape) for x in through],
        [VMEM] * len(shapes) + [ANY] * len(through),
        after=list(after) + list(through),
        input_output_aliases={1 + len(ins) + len(after) + i: len(shapes) + i for i in range(len(through))},
        nbytes=sum(2 * 3 * x.size for x in shapes),
    )


def read(ref, slot, start, size):
    half = ref.shape[2]
    if start + size <= half and start == 0 and size == half:
        return ref[slot]
    slots = ref.shape[0] // 2
    pieces = []
    while size:
        part, at = divmod(start, half)
        count = min(size, half - at)
        pieces.append(ref[part * slots + slot, :, at : at + count])
        start, size = start + count, size - count
    return jnp.concatenate(pieces, axis=1) if len(pieces) > 1 else pieces[0]


def factor_of(n, b, by_tenant, tab_ref, own_ref, arrived, lead=0):
    tenant = tab_ref[3 * (n - 1), b]
    factor = own_ref[tenant].astype(F32)
    outer = tab_ref[3 * (n - 1) + 1, 0] > 0
    for hop in range(n - 1):
        index = tenant if by_tenant and hop == 0 else tab_ref[2 * (n - 1) + hop, b]
        came = read(arrived[hop], index, lead, own_ref.shape[2]) if hop == n - 2 else arrived[hop][index]
        came = came.astype(F32)
        used = jnp.where(outer, 1, 0) if hop == n - 2 else jnp.where(outer, 0, 1)
        factor = jnp.where(used > 0, factor + came, factor)
    return factor.astype(BF16)


def project_kernel(n, first, out, ins, tab_ref, tokens_ref, own_ref, *refs):
    arrived = refs[: n - 1]
    total_ref = None if first else refs[ins - 4]
    outs = refs[-2:] if out else refs[-1:]
    size = tokens_ref.shape[1]

    def one(b, carry):
        factor = factor_of(n, b, False, tab_ref, own_ref, arrived)
        at = pl.ds(pl.multiple_of(b * LANES, LANES), LANES)
        part = lax.dot_general(factor, tokens_ref[at, :], NT, preferred_element_type=F32)
        if not first:
            part = total_ref[:, at] + part
        outs[0][:, at] = part.astype(outs[0].dtype)
        if out:
            outs[1][b] = factor_of(n, b, True, tab_ref, refs[n - 1], refs[n : 2 * n - 1], own_ref.shape[2])
        return carry

    lax.fori_loop(0, tokens_ref.shape[0] // LANES, one, 0, unroll=4)


def project(n, tab, tokens, own, part, arrived, total, last, up=None, after=()):
    tenants, rank, size = own.shape
    rows = tokens.shape[0]
    at = part[0] // size
    outs = [shape(rank, rows, dtype=BF16 if last else F32)]
    ins = [tab, tokens, own, *arrived]
    if up:
        outs.append(shape(rows // LANES, rank, up[0].shape[2]))
        ins += [up[0], *up[1]]
    if total is not None:
        ins.append(total)
    return call(
        functools.partial(project_kernel, n, total is None, up is not None),
        ins,
        [SMEM, pl.BlockSpec((rows, size), lambda j: (0, at))] + [VMEM] * (len(ins) - 2),
        outs,
        [VMEM] * len(outs),
        after=after,
        free=tokens,
        grid=(1,),
        flops=2 * rows * size * rank,
        nbytes=2 * size * (rows + 2 * tenants * rank),
    )


def base_kernel(order_ref, tokens_ref, first_ref, second_ref, *refs):
    for weight_ref, out_ref in ((first_ref, refs[-2]), (second_ref, refs[-1])):
        out_ref[...] = jnp.dot(tokens_ref[...], weight_ref[...], preferred_element_type=F32).astype(BF16)


def base_product(order, tokens, weight, out, after, first, last):
    strip, width = tokens.shape[0] // 3, tokens.shape[1]
    rows = (last - first) * strip
    flops, nbytes = 4 * rows * width * out, 2 * (rows * (width + 2 * out) + 2 * width * out)
    return pl.pallas_call(
        base_kernel,
        grid_spec=pltpu.PrefetchScalarGridSpec(
            num_scalar_prefetch=1,
            grid=(last - first,),
            in_specs=[
                pl.BlockSpec((strip, width), lambda m, order: (first + m, 0)),
                pl.BlockSpec((width, out), lambda m, order: (0, order[0])),
                pl.BlockSpec((width, out), lambda m, order: (0, order[1])),
            ]
            + [ANY] * len(after),
            out_specs=[pl.BlockSpec((strip, out), lambda m, order: (m, 0))] * 2,
        ),
        out_shape=[shape(rows, out)] * 2,
        compiler_params=pltpu.CompilerParams(vmem_limit_bytes=24 * MIB),
        cost_estimate=pl.CostEstimate(flops=int(SHARE * flops), bytes_accessed=int(SHARE * nbytes), transcendentals=0),
    )(order, tokens, placed(weight), placed(weight), *after)


def rows_kernel(pieces, ins, *refs):
    at = 0
    for length, terms in pieces:
        total = 0.0
        for which, start in terms:
            total = total + refs[which][start : start + length, :].astype(F32)
        refs[-1][at : at + length, :] = total.astype(BF16)
        at += length


def add_rows(arrays, pieces, after=()):
    rows, width = sum(length for length, _ in pieces), arrays[0].shape[1]
    return call(
        functools.partial(rows_kernel, pieces),
        list(arrays),
        [VMEM] * len(arrays),
        shape(rows, width),
        VMEM,
        after=after,
        nbytes=8 * rows * width,
    )


def finish_kernel(row, per, ins, tab_ref, up_ref, *refs):
    lows, base_ref, out_ref = refs[:4], refs[4], refs[5]
    width = out_ref.shape[1]
    low = lows[0][...].astype(F32)
    for other in lows[1:]:
        low = low + other[...].astype(F32)
    low = low.astype(BF16)
    for j in range(per):
        b = pl.program_id(0) * per + j
        at = slice(j * LANES, (j + 1) * LANES)
        total = lax.dot_general(low[:, at], up_ref[b], TN, preferred_element_type=F32)
        total = total + base_ref[at, :].astype(F32)
        live = lax.broadcasted_iota(I32, (LANES, width), 0) < tab_ref[row, b]
        out_ref[at, :] = jnp.where(live, total, 0.0).astype(out_ref.dtype)


def finish(tab, row, up, lows, base, per):
    rank, rows = lows[0].shape
    width = base.shape[1]
    blocks = rows // LANES
    whole = pl.BlockSpec((per * LANES, width), lambda j: (j, 0))
    return call(
        functools.partial(finish_kernel, row, per),
        [tab, up, *lows, pltpu.with_memory_space_constraint(base, pltpu.HBM)],
        [SMEM, VMEM] + [pl.BlockSpec((rank, per * LANES), lambda j: (0, j))] * 4 + [whole],
        shape(rows, width),
        whole,
        free=True,
        grid=(blocks // per,),
        flops=2 * rows * rank * width,
        nbytes=4 * rows * width,
    )


def swap(x, axis):
    return lax.ppermute(x, axis, [(0, 1), (1, 0)])


def ends(x):
    return lax.ppermute(x, "skill", [(0, 1), (1, 0), (2, 3), (3, 2)])


def inward(x):
    return lax.ppermute(x, "skill", [(0, 1), (3, 2)])


def outward(x):
    return lax.ppermute(x, "skill", [(1, 0), (2, 3)])


def middle(x):
    pairs = [(2 + c, 4 + c) for c in (0, 1)] + [(0, 1), (6, 7)]
    return lax.ppermute(x, ("skill", "tensor"), pairs + [(b, a) for a, b in pairs])


def line_body(tokens, base_weight, skill_down, skill_up, alloc, block_tenant, block_len):
    n = 4
    rows, width = tokens.shape
    tenants, local_skills = alloc.shape
    rank = skill_down.shape[2]
    out = skill_up.shape[2]
    blocks = block_len.shape[0]
    me = lax.axis_index("skill")
    tensor, dp = lax.axis_index("tensor"), lax.axis_index("dp")
    hops = [ends, middle, ends]
    full = [min(tenants, blocks * (n - 1 - h)) for h in range(n - 1)]
    plans = [[min(f, p) for f, p in zip(full, plan)] for plan in PLANS] + [full]
    tile = width // 8
    parts = [(0, 3 * tile), (3 * tile, 3 * tile), (6 * tile, 2 * tile)]

    own_t = block_tenant.reshape(1, blocks)
    seen = jnp.concatenate(
        [own_t]
        + [lax.ppermute(own_t, "skill", [(j, j ^ k) for j in range(n)]) for k in range(1, n)],
        axis=0,
    )
    library = jnp.transpose(skill_down, (0, 2, 1)).reshape(local_skills * rank, width)
    own_up, kron = compose_first(alloc, skill_up.reshape(local_skills * rank, out), rank)
    own_up, seen = lax.optimization_barrier((own_up, seen))
    up_0 = ends(own_up)
    seen = [seen, swap(seen, "group")]
    own_0 = compose(kron, library, rank, parts[0], tile, after=[own_up])
    tab, plan = make_tables(n, tenants, plans, me.reshape(1).astype(I32), block_len.reshape(1, blocks), seen)
    theirs, ours = (1 - tensor) * 2, tensor * 2
    order_cross = jnp.stack([theirs + 1 - dp, ours + 1 - dp]).astype(I32)
    order_stay = jnp.stack([theirs + dp, ours + dp]).astype(I32)

    def planned(sizes):
        owns, arrived, up_came = [own_0], [[], [], []], [up_0]

        def job(h, k):
            return h, sizes[h], [(owns[k], arrived[k][h - 1] if h else None, False)]

        up_piece = (own_up, up_0, True)
        first, up_1 = step(n, tab, [job(0, 0), (1, sizes[1], [up_piece])])
        arrived[0].append(ends(first))
        up_came.append(middle(up_1))
        own, message = compose(kron, library, rank, parts[1], tile, sizes[0], tab)
        owns.append(own)
        arrived[1].append(ends(message))
        cut = rows // 3
        away, keep = base_product(order_cross, tokens, base_weight, out, [message], 0, 1)

        to_1, away = step(n, tab, [job(1, 0)], [keep, up_came[1]], [away])
        arrived[0].append(middle(to_1))
        core = swap(away, "tensor")
        own, message = compose(kron, library, rank, parts[2], tile, sizes[0], tab, [to_1])
        owns.append(own)
        away_2, keep_2 = base_product(order_cross, tokens, base_weight, out, [own], 1, 3)
        if EARLY:
            stay, stay_keep = base_product(order_stay, tokens, base_weight, out, [keep_2], 0, 3)

        first_and_up = 2, (max(sizes[2], (sizes[0] + 1) // 2), message), [
            (owns[0], arrived[0][1], False),
            (own_up, up_came[1], False),
        ]
        to_1, to_2, away_2 = step(n, tab, [job(1, 1), first_and_up], [core, keep_2] + ([stay] if EARLY else []), [away_2])
        arrived[1].append(middle(to_1))
        exchanged = ends(to_2)
        arrived[0].append(exchanged)
        arrived[2].append(exchanged)
        up_came.append(exchanged)
        core_2 = swap(away_2, "tensor")
        near = add_rows([keep, core], [(cut, [(0, 0), (1, 0)])], [to_1])
        across = swap(near, "dp")
        if not EARLY:
            stay, stay_keep = base_product(order_stay, tokens, base_weight, out, [near], 0, 3)
        near_2 = add_rows([keep_2, core_2], [(rows - cut, [(0, 0), (1, 0)])])

        to_1, to_2, stay, near_2 = step(n, tab, [job(1, 2), job(2, 1)], [across, stay_keep], [stay, near_2])
        arrived[2].append(middle(to_1))
        arrived[1].append(outward(to_2))
        across_2 = swap(near_2, "dp")
        core = swap(stay, "tensor")
        low, up = project(n, tab, tokens, owns[0], parts[0], arrived[0], None, False, (own_up, up_came), [to_1])

        (to_2,) = step(n, tab, [job(2, 2)], [low, core])
        arrived[2].append(outward(to_2))
        (low,) = project(n, tab, tokens, owns[1], parts[1], arrived[1], low, False, None, [to_2])
        base = add_rows(
            [stay_keep, core, across, across_2],
            [(cut, [(0, 0), (1, 0), (2, 0)]), (rows - cut, [(0, cut), (1, cut), (3, 0)])],
            [low],
        )
        (low,) = project(n, tab, tokens, owns[2], parts[2], arrived[2], low, True, None, [base])
        return low, up, base

    low, up, base = lax.switch(plan[0], [functools.partial(planned, sizes) for sizes in plans])
    lows = [low, swap(low, "tensor"), swap(low, "dp")]
    lows.append(lax.ppermute(low, ("tensor", "dp"), [(0, 3), (1, 2), (2, 1), (3, 0)]))
    return finish(tab, 3 * (n - 1) + 2, up, lows, base, PER)


def plain_body(tokens, base_weight, skill_down, skill_up, alloc, block_tenant, block_len):
    rows, width = tokens.shape
    blocks = block_len.shape[0]
    block_rows = rows // blocks
    local_skills, slice_width, rank = skill_down.shape
    slice_out = skill_up.shape[2]
    down_size = slice_width * rank
    stacked = jnp.concatenate(
        [
            skill_down.reshape(local_skills, down_size),
            skill_up.reshape(local_skills, rank * slice_out),
        ],
        1,
    ).astype(F32)
    partial_sum = jnp.dot(alloc, stacked, precision=lax.Precision.HIGHEST)
    composed = lax.psum(partial_sum.astype(BF16), "skill")
    factors = jnp.take(composed, block_tenant, axis=0)
    down_part = factors[:, :down_size].reshape(blocks, slice_width, rank)
    up_part = factors[:, down_size:].reshape(blocks, rank, slice_out).astype(F32)
    grouped = tokens.reshape(blocks, block_rows, width)
    projected = jnp.einsum("bnd,bdr->bnr", grouped, down_part, preferred_element_type=F32)
    base_term = jnp.dot(tokens, base_weight, preferred_element_type=F32)
    lowrank = lax.psum(projected.astype(BF16), ("tensor", "dp")).astype(F32)
    base = lax.psum_scatter(
        base_term.astype(BF16), ("tensor", "dp"), scatter_dimension=1, tiled=True
    ).astype(F32)
    adapter = jnp.einsum("bnr,bro->bno", lowrank, up_part, precision=lax.Precision.HIGHEST)
    total = base.reshape(blocks, block_rows, slice_out) + adapter
    live = (jnp.arange(block_rows, dtype=I32)[None, :] < block_len[:, None])[:, :, None]
    return jnp.where(live, total, 0.0).astype(BF16).reshape(rows, slice_out)


def solution(mesh):
    placed = (
        P(("group", "skill"), ("tensor", "dp")),
        P(("tensor", "dp"), None),
        P("skill", ("tensor", "dp"), None),
        P("skill", None, ("tensor", "dp")),
        P("group", "skill"),
        P(("group", "skill")),
        P(("group", "skill")),
    )
    fits = (mesh.shape["skill"], mesh.shape["tensor"], mesh.shape["dp"]) == (4, 2, 2)
    body = line_body if fits else plain_body
    return jax.shard_map(
        body,
        mesh=mesh,
        in_specs=placed,
        out_specs=P(("group", "skill"), ("tensor", "dp")),
        check_vma=False,
    )
```

```python
import functools

import jax
import jax.numpy as jnp
from jax import lax
from jax.experimental import pallas as pl
from jax.experimental.pallas import tpu as pltpu
from jax.sharding import PartitionSpec as P

F32, BF16, I32 = jnp.float32, jnp.bfloat16, jnp.int32
MIB = 1 << 20
LANES = 128
LARGE = 1 << 21
PER = 6
EARLY = 0
SHARE = 1.0
VMEM = pl.BlockSpec(memory_space=pltpu.VMEM)
SMEM = pl.BlockSpec(memory_space=pltpu.SMEM)
ANY = pl.BlockSpec(memory_space=pl.ANY)
NT = (((1,), (1,)), ((), ()))
TN = (((0,), (0,)), ((), ()))
PLANS = ((17, 14, 10), (18, 15, 11), (20, 16, 11), (22, 18, 12))


def call(kernel, ins, specs, outs, out_specs, *, after=(), free=None, vmem=24, flops=0, nbytes=0, **kwargs):
    return pl.pallas_call(
        functools.partial(kernel, len(ins)),
        in_specs=specs + [ANY] * len(after),
        out_specs=out_specs,
        out_shape=outs,
        compiler_params=pltpu.CompilerParams(vmem_limit_bytes=vmem * MIB),
        cost_estimate=pl.CostEstimate(flops=int(SHARE * flops), bytes_accessed=int(SHARE * nbytes), transcendentals=0),
        **kwargs,
    )(*[x if free is True or x is free else placed(x) for x in ins], *after)


def placed(x):
    if x.dtype != BF16:
        return x
    return pltpu.with_memory_space_constraint(x, pltpu.HBM if x.size >= LARGE else pltpu.VMEM)


def shape(*dims, dtype=BF16):
    return jax.ShapeDtypeStruct(dims, dtype)


def kron_kernel(rank, ins, alloc_ref, kron_ref):
    tenants, skills = alloc_ref.shape
    depth = skills * rank
    at = lax.broadcasted_iota(I32, (skills, depth), 1)
    row = lax.broadcasted_iota(I32, (skills, depth), 0)
    inside = jnp.logical_and(at >= row * rank, at < (row + 1) * rank)
    repeat = jnp.where(inside, 1.0, 0.0).astype(BF16)
    spread = jnp.dot(alloc_ref[...].astype(BF16), repeat, preferred_element_type=F32)
    lane = lax.rem(lax.broadcasted_iota(I32, (rank, depth), 1), rank)
    diagonal = lane == lax.broadcasted_iota(I32, (rank, depth), 0)
    for t in range(tenants):
        kron_ref[t * rank : (t + 1) * rank, :] = jnp.where(diagonal, spread[t : t + 1, :], 0.0).astype(BF16)


def first_kernel(rank, ins, alloc_ref, library_ref, own_ref, kron_ref):
    kron_kernel(rank, 1, alloc_ref, kron_ref)
    made = jnp.dot(kron_ref[...], library_ref[...], preferred_element_type=F32).astype(BF16)
    own_ref[...] = made.reshape(own_ref.shape)


def compose_first(alloc, library, rank):
    tenants, skills = alloc.shape
    depth, out = library.shape
    return call(
        functools.partial(first_kernel, rank),
        [pltpu.with_memory_space_constraint(x, pltpu.HBM) for x in (alloc, library)],
        [pl.BlockSpec(x.shape, lambda j: (0, 0)) for x in (alloc, library)],
        [shape(tenants, rank, out), shape(tenants * rank, depth)],
        [VMEM] * 2,
        free=True,
        grid=(1,),
        flops=2 * tenants * rank * depth * out,
        nbytes=2 * depth * out,
    )


def compose_kernel(slots, ins, *refs):
    kron_ref, library_ref = refs[:2] if not slots else refs[1:3]
    own_ref = refs[-2] if slots else refs[-1]
    tenants, rank, size = own_ref.shape
    made = jnp.dot(kron_ref[...], library_ref[...], preferred_element_type=F32).astype(BF16)
    own_ref[...] = made.reshape(tenants, rank, size)
    if slots:
        copy_slots(refs[0], own_ref, refs[-1], slots)


def copy_slots(tab_ref, own_ref, out_ref, slots):
    def one(slot, carry):
        out_ref[slot] = own_ref[tab_ref[0, slot]]
        return carry

    lax.fori_loop(0, slots, one, 0, unroll=2)


def compose(kron, library, rank, part, tile, slots=0, tab=None, after=()):
    rows, depth = kron.shape
    tenants = rows // rank
    start, size = part
    at = start // tile
    outs, out_specs = [shape(tenants, rank, size)], [pl.BlockSpec((tenants, rank, tile), lambda j: (0, 0, j))]
    if slots:
        outs.append(shape(slots, rank, size))
        out_specs.append(pl.BlockSpec((slots, rank, tile), lambda j: (0, 0, j)))
    made = call(
        functools.partial(compose_kernel, slots),
        ([tab] if slots else []) + [kron, library],
        ([SMEM] if slots else []) + [VMEM, pl.BlockSpec((depth, tile), lambda j: (0, at + j))],
        outs,
        out_specs,
        after=after,
        grid=(size // tile,),
        flops=2 * rows * depth * size,
        nbytes=2 * (depth + rows) * size,
    )
    return made if slots else made[0]


def tables_kernel(n, tenants, plans, ins, place_ref, len_ref, *refs):
    arrays, tab_ref, plan_ref = refs[:-2], refs[-2], refs[-1]
    me = place_ref[0]
    blocks = arrays[0].shape[1]
    sub = lax.broadcasted_iota(I32, (tenants, tenants), 0)
    lane = lax.broadcasted_iota(I32, (tenants, tenants), 1)
    wide = lax.broadcasted_iota(I32, (tenants, LANES), 1)
    tenant = lax.broadcasted_iota(I32, (tenants, LANES), 0)
    one = lax.broadcasted_iota(I32, (tenants, blocks), 0)
    zs = [me ^ k for k in range(n)]
    groups = len(arrays)
    present = [
        [
            jnp.max(jnp.where(one == arrays[g][k : k + 1, :], 1.0, 0.0), axis=1, keepdims=True)
            for k in range(n)
        ]
        for g in range(groups)
    ]

    def union(keep, group=0):
        total = jnp.zeros((tenants, 1), F32)
        for z, here in zip(zs, present[group]):
            total = jnp.maximum(total, here * jnp.where(keep(z), 1.0, 0.0))
        return total

    def positions(held):
        across = jnp.sum(jnp.where(sub == lane, held, 0.0), axis=0, keepdims=True)
        return jnp.sum(jnp.where(lane < sub, across, 0.0), axis=1, keepdims=True)

    def pack(held, value):
        slot = positions(held).astype(I32)
        chosen = jnp.logical_and(slot == wide, held > 0.5)
        return jnp.sum(jnp.where(chosen, value, 0.0), axis=0, keepdims=True)

    send_right, send_left = union(lambda z: z > me), union(lambda z: z < me)
    from_left, from_right = positions(union(lambda z: z >= me)), positions(union(lambda z: z <= me))
    number = tenant.astype(F32)
    right = pack(send_right, number), pack(send_right, from_left)
    left = pack(send_left, number), pack(send_left, from_right)
    own = jnp.concatenate([arrays[0][0:1, :], jnp.zeros((1, LANES - blocks), I32)], axis=1)
    mine = own == tenant

    def at(place, rows, otherwise):
        return jnp.where(me == place, rows, otherwise)

    none = jnp.zeros((1, LANES), F32)
    final_right = jnp.sum(jnp.where(mine, from_left, 0.0), axis=0, keepdims=True)
    final_left = jnp.sum(jnp.where(mine, from_right, 0.0), axis=0, keepdims=True)
    rows = []
    for part in (0, 1):
        for hop in range(n - 1):
            rows.append(at(hop, right[part], at(n - 1 - hop, left[part], none)))
    for hop in range(n - 1):
        rows.append(at(hop + 1, final_right, at(n - 2 - hop, final_left, none)))
    for row, value in enumerate(rows):
        tab_ref[row : row + 1, :] = value.astype(I32)
    tab_ref[len(rows) : len(rows) + 1, :] = own
    tab_ref[len(rows) + 2 : len(rows) + 3, :] = jnp.concatenate([len_ref[...], jnp.zeros((1, LANES - blocks), I32)], axis=1)
    ends_here = jnp.logical_or(me == 0, me == n - 1)
    tab_ref[len(rows) + 1 : len(rows) + 2, :] = jnp.where(ends_here, jnp.ones_like(own), jnp.zeros_like(own))

    held = jnp.zeros((tenants, LANES), F32)
    hop_of = lax.broadcasted_iota(I32, (1, LANES), 1)
    limits = [jnp.full((1, LANES), float(tenants), F32) for _ in plans]
    column = 0
    for group in range(groups):
        for hop in range(n - 1):
            for keep in (lambda z: z > hop, lambda z: z < n - 1 - hop):
                held = jnp.where(wide == column, union(keep, group), held)
                limits = [jnp.where(hop_of == column, float(p[hop]), l) for p, l in zip(plans, limits)]
                column += 1
    counts = jnp.sum(held, axis=0, keepdims=True)
    plan = jnp.int32(0)
    for limit in limits[:-1]:
        plan = plan + jnp.where(jnp.max(counts - limit) > 0.5, 1, 0)
    plan_ref[0] = plan


def make_tables(n, tenants, plans, place, lens, arrays):
    rows = -(-(3 * (n - 1) + 3) // 8) * 8
    return call(
        functools.partial(tables_kernel, n, tenants, plans),
        [place, lens, *arrays],
        [SMEM] + [VMEM] * (1 + len(arrays)),
        [shape(rows, LANES, dtype=I32), shape(1, dtype=I32)],
        [VMEM, SMEM],
    )


def step_kernel(n, jobs, passed, ins, tab_ref, *refs):
    given, outs = list(refs[: ins - 1]), refs[ins - 1 + passed :]
    for (hop, slots, pieces), out_ref in zip(jobs, outs):
        both = slots is None
        if both:
            slots = out_ref.shape[0] // 2
            fresh_ref = given.pop(0)

            @pl.when(tab_ref[3 * (n - 1) + 1, 0] > 0)
            def _(fresh_ref=fresh_ref, out_ref=out_ref):
                out_ref[: fresh_ref.shape[0]] = fresh_ref[...]

        held = [(given.pop(0), given.pop(0) if hop else None) for _ in pieces]

        def one(slot, carry, hop=hop, pieces=pieces, held=held, out_ref=out_ref, both=both, slots=slots):
            tenant = tab_ref[hop, slot]
            at = 0
            made = []
            for by_tenant, (own_ref, in_ref) in zip(pieces, held):
                block = own_ref[tenant]
                if hop:
                    index = tenant if by_tenant else tab_ref[n - 1 + hop, slot]
                    block = (block.astype(F32) + in_ref[index].astype(F32)).astype(BF16)
                made.append(block)
            block = jnp.concatenate(made, axis=1) if len(made) > 1 else made[0]
            if both:
                half = out_ref.shape[2]
                out_ref[slot] = block[:, :half]
                out_ref[slots + slot] = block[:, half:]
            else:
                out_ref[slot] = block
            return carry

        def all_slots(one=one, slots=slots):
            lax.fori_loop(0, slots, one, 0, unroll=True)

        if both:
            pl.when(tab_ref[3 * (n - 1) + 1, 0] == 0)(all_slots)
        else:
            all_slots()


def step(n, tab, jobs, after=(), through=()):
    ins, shapes, plan = [], [], []
    for hop, slots, pieces in jobs:
        columns = sum(own.shape[2] for own, _, _ in pieces)
        if isinstance(slots, tuple):
            plan.append((hop, None, [by_tenant for _, _, by_tenant in pieces]))
            ins.append(slots[1])
            slots, columns = 2 * slots[0], columns // 2
            assert slots >= ins[-1].shape[0] and columns == ins[-1].shape[2]
        else:
            plan.append((hop, slots, [by_tenant for _, _, by_tenant in pieces]))
        for own, arrived, _ in pieces:
            ins += [own, arrived] if hop else [own]
        shapes.append(shape(slots, pieces[0][0].shape[1], columns))
    return call(
        functools.partial(step_kernel, n, plan, len(after) + len(through)),
        [tab, *ins],
        [SMEM] + [VMEM] * len(ins),
        shapes + [shape(*x.shape) for x in through],
        [VMEM] * len(shapes) + [ANY] * len(through),
        after=list(after) + list(through),
        input_output_aliases={1 + len(ins) + len(after) + i: len(shapes) + i for i in range(len(through))},
        nbytes=sum(2 * 3 * x.size for x in shapes),
    )


def read(ref, slot, start, size):
    half = ref.shape[2]
    if start + size <= half and start == 0 and size == half:
        return ref[slot]
    slots = ref.shape[0] // 2
    pieces = []
    while size:
        part, at = divmod(start, half)
        count = min(size, half - at)
        pieces.append(ref[part * slots + slot, :, at : at + count])
        start, size = start + count, size - count
    return jnp.concatenate(pieces, axis=1) if len(pieces) > 1 else pieces[0]


def factor_of(n, b, by_tenant, tab_ref, own_ref, arrived, lead=0):
    tenant = tab_ref[3 * (n - 1), b]
    factor = own_ref[tenant].astype(F32)
    outer = tab_ref[3 * (n - 1) + 1, 0] > 0
    for hop in range(n - 1):
        index = tenant if by_tenant and hop == 0 else tab_ref[2 * (n - 1) + hop, b]
        came = read(arrived[hop], index, lead, own_ref.shape[2]) if hop == n - 2 else arrived[hop][index]
        came = came.astype(F32)
        used = jnp.where(outer, 1, 0) if hop == n - 2 else jnp.where(outer, 0, 1)
        factor = jnp.where(used > 0, factor + came, factor)
    return factor.astype(BF16)


def project_kernel(n, first, out, ins, tab_ref, tokens_ref, own_ref, *refs):
    arrived = refs[: n - 1]
    total_ref = None if first else refs[ins - 4]
    outs = refs[-2:] if out else refs[-1:]
    size = tokens_ref.shape[1]

    def one(b, carry):
        factor = factor_of(n, b, False, tab_ref, own_ref, arrived)
        at = pl.ds(pl.multiple_of(b * LANES, LANES), LANES)
        part = lax.dot_general(factor, tokens_ref[at, :], NT, preferred_element_type=F32)
        if not first:
            part = total_ref[:, at] + part
        outs[0][:, at] = part.astype(outs[0].dtype)
        if out:
            outs[1][b] = factor_of(n, b, True, tab_ref, refs[n - 1], refs[n : 2 * n - 1], own_ref.shape[2])
        return carry

    lax.fori_loop(0, tokens_ref.shape[0] // LANES, one, 0, unroll=True)


def project(n, tab, tokens, own, part, arrived, total, last, up=None, after=()):
    tenants, rank, size = own.shape
    rows = tokens.shape[0]
    at = part[0] // size
    outs = [shape(rank, rows, dtype=BF16 if last else F32)]
    ins = [tab, tokens, own, *arrived]
    if up:
        outs.append(shape(rows // LANES, rank, up[0].shape[2]))
        ins += [up[0], *up[1]]
    if total is not None:
        ins.append(total)
    return call(
        functools.partial(project_kernel, n, total is None, up is not None),
        ins,
        [SMEM, pl.BlockSpec((rows, size), lambda j: (0, at))] + [VMEM] * (len(ins) - 2),
        outs,
        [VMEM] * len(outs),
        after=after,
        free=tokens,
        grid=(1,),
        flops=2 * rows * size * rank,
        nbytes=2 * size * (rows + 2 * tenants * rank),
    )


def base_kernel(order_ref, tokens_ref, first_ref, second_ref, *refs):
    for weight_ref, out_ref in ((first_ref, refs[-2]), (second_ref, refs[-1])):
        out_ref[...] = jnp.dot(tokens_ref[...], weight_ref[...], preferred_element_type=F32).astype(BF16)


def base_product(order, tokens, weight, out, after, first, last):
    strip, width = tokens.shape[0] // 3, tokens.shape[1]
    rows = (last - first) * strip
    flops, nbytes = 4 * rows * width * out, 2 * (rows * (width + 2 * out) + 2 * width * out)
    return pl.pallas_call(
        base_kernel,
        grid_spec=pltpu.PrefetchScalarGridSpec(
            num_scalar_prefetch=1,
            grid=(last - first,),
            in_specs=[
                pl.BlockSpec((strip, width), lambda m, order: (first + m, 0)),
                pl.BlockSpec((width, out), lambda m, order: (0, order[0])),
                pl.BlockSpec((width, out), lambda m, order: (0, order[1])),
            ]
            + [ANY] * len(after),
            out_specs=[pl.BlockSpec((strip, out), lambda m, order: (m, 0))] * 2,
        ),
        out_shape=[shape(rows, out)] * 2,
        compiler_params=pltpu.CompilerParams(vmem_limit_bytes=24 * MIB),
        cost_estimate=pl.CostEstimate(flops=int(SHARE * flops), bytes_accessed=int(SHARE * nbytes), transcendentals=0),
    )(order, tokens, placed(weight), placed(weight), *after)


def rows_kernel(pieces, ins, *refs):
    at = 0
    for length, terms in pieces:
        total = 0.0
        for which, start in terms:
            total = total + refs[which][start : start + length, :].astype(F32)
        refs[-1][at : at + length, :] = total.astype(BF16)
        at += length


def add_rows(arrays, pieces, after=()):
    rows, width = sum(length for length, _ in pieces), arrays[0].shape[1]
    return call(
        functools.partial(rows_kernel, pieces),
        list(arrays),
        [VMEM] * len(arrays),
        shape(rows, width),
        VMEM,
        after=after,
        nbytes=8 * rows * width,
    )


def finish_kernel(row, per, ins, tab_ref, up_ref, *refs):
    lows, base_ref, out_ref = refs[:4], refs[4], refs[5]
    width = out_ref.shape[1]
    low = lows[0][...].astype(F32)
    for other in lows[1:]:
        low = low + other[...].astype(F32)
    low = low.astype(BF16)
    for j in range(per):
        b = pl.program_id(0) * per + j
        at = slice(j * LANES, (j + 1) * LANES)
        total = lax.dot_general(low[:, at], up_ref[b], TN, preferred_element_type=F32)
        total = total + base_ref[at, :].astype(F32)
        live = lax.broadcasted_iota(I32, (LANES, width), 0) < tab_ref[row, b]
        out_ref[at, :] = jnp.where(live, total, 0.0).astype(out_ref.dtype)


def finish(tab, row, up, lows, base, per):
    rank, rows = lows[0].shape
    width = base.shape[1]
    blocks = rows // LANES
    whole = pl.BlockSpec((per * LANES, width), lambda j: (j, 0))
    return call(
        functools.partial(finish_kernel, row, per),
        [tab, up, *lows, pltpu.with_memory_space_constraint(base, pltpu.HBM)],
        [SMEM, VMEM] + [pl.BlockSpec((rank, per * LANES), lambda j: (0, j))] * 4 + [whole],
        shape(rows, width),
        whole,
        free=True,
        grid=(blocks // per,),
        flops=2 * rows * rank * width,
        nbytes=4 * rows * width,
    )


def swap(x, axis):
    return lax.ppermute(x, axis, [(0, 1), (1, 0)])


def ends(x):
    return lax.ppermute(x, "skill", [(0, 1), (1, 0), (2, 3), (3, 2)])


def inward(x):
    return lax.ppermute(x, "skill", [(0, 1), (3, 2)])


def outward(x):
    return lax.ppermute(x, "skill", [(1, 0), (2, 3)])


def middle(x):
    pairs = [(2 + c, 4 + c) for c in (0, 1)] + [(0, 1), (6, 7)]
    return lax.ppermute(x, ("skill", "tensor"), pairs + [(b, a) for a, b in pairs])


def line_body(tokens, base_weight, skill_down, skill_up, alloc, block_tenant, block_len):
    n = 4
    rows, width = tokens.shape
    tenants, local_skills = alloc.shape
    rank = skill_down.shape[2]
    out = skill_up.shape[2]
    blocks = block_len.shape[0]
    me = lax.axis_index("skill")
    tensor, dp = lax.axis_index("tensor"), lax.axis_index("dp")
    hops = [ends, middle, ends]
    full = [min(tenants, blocks * (n - 1 - h)) for h in range(n - 1)]
    plans = [[min(f, p) for f, p in zip(full, plan)] for plan in PLANS] + [full]
    tile = width // 8
    parts = [(0, 3 * tile), (3 * tile, 3 * tile), (6 * tile, 2 * tile)]

    own_t = block_tenant.reshape(1, blocks)
    seen = jnp.concatenate(
        [own_t]
        + [lax.ppermute(own_t, "skill", [(j, j ^ k) for j in range(n)]) for k in range(1, n)],
        axis=0,
    )
    library = jnp.transpose(skill_down, (0, 2, 1)).reshape(local_skills * rank, width)
    own_up, kron = compose_first(alloc, skill_up.reshape(local_skills * rank, out), rank)
    own_up, seen = lax.optimization_barrier((own_up, seen))
    up_0 = ends(own_up)
    seen = [seen, swap(seen, "group")]
    own_0 = compose(kron, library, rank, parts[0], tile, after=[own_up])
    tab, plan = make_tables(n, tenants, plans, me.reshape(1).astype(I32), block_len.reshape(1, blocks), seen)
    theirs, ours = (1 - tensor) * 2, tensor * 2
    order_cross = jnp.stack([theirs + 1 - dp, ours + 1 - dp]).astype(I32)
    order_stay = jnp.stack([theirs + dp, ours + dp]).astype(I32)

    def planned(sizes):
        owns, arrived, up_came = [own_0], [[], [], []], [up_0]

        def job(h, k):
            return h, sizes[h], [(owns[k], arrived[k][h - 1] if h else None, False)]

        up_piece = (own_up, up_0, True)
        first, up_1 = step(n, tab, [job(0, 0), (1, sizes[1], [up_piece])])
        arrived[0].append(ends(first))
        up_came.append(middle(up_1))
        own, message = compose(kron, library, rank, parts[1], tile, sizes[0], tab)
        owns.append(own)
        arrived[1].append(ends(message))
        cut = rows // 3
        away, keep = base_product(order_cross, tokens, base_weight, out, [message], 0, 1)

        to_1, away = step(n, tab, [job(1, 0)], [keep, up_came[1]], [away])
        arrived[0].append(middle(to_1))
        core = swap(away, "tensor")
        own, message = compose(kron, library, rank, parts[2], tile, sizes[0], tab, [to_1])
        owns.append(own)
        away_2, keep_2 = base_product(order_cross, tokens, base_weight, out, [own], 1, 3)
        if EARLY:
            stay, stay_keep = base_product(order_stay, tokens, base_weight, out, [keep_2], 0, 3)

        first_and_up = 2, (max(sizes[2], (sizes[0] + 1) // 2), message), [
            (owns[0], arrived[0][1], False),
            (own_up, up_came[1], False),
        ]
        to_1, to_2, away_2 = step(n, tab, [job(1, 1), first_and_up], [core, keep_2] + ([stay] if EARLY else []), [away_2])
        arrived[1].append(middle(to_1))
        exchanged = ends(to_2)
        arrived[0].append(exchanged)
        arrived[2].append(exchanged)
        up_came.append(exchanged)
        core_2 = swap(away_2, "tensor")
        near = add_rows([keep, core], [(cut, [(0, 0), (1, 0)])], [to_1])
        across = swap(near, "dp")
        if not EARLY:
            stay, stay_keep = base_product(order_stay, tokens, base_weight, out, [near], 0, 3)
        near_2 = add_rows([keep_2, core_2], [(rows - cut, [(0, 0), (1, 0)])])

        to_1, to_2, stay, near_2 = step(n, tab, [job(1, 2), job(2, 1)], [across, stay_keep], [stay, near_2])
        arrived[2].append(middle(to_1))
        arrived[1].append(outward(to_2))
        across_2 = swap(near_2, "dp")
        core = swap(stay, "tensor")
        low, up = project(n, tab, tokens, owns[0], parts[0], arrived[0], None, False, (own_up, up_came), [to_1])

        (to_2,) = step(n, tab, [job(2, 2)], [low, core])
        arrived[2].append(outward(to_2))
        (low,) = project(n, tab, tokens, owns[1], parts[1], arrived[1], low, False, None, [to_2])
        base = add_rows(
            [stay_keep, core, across, across_2],
            [(cut, [(0, 0), (1, 0), (2, 0)]), (rows - cut, [(0, cut), (1, cut), (3, 0)])],
            [low],
        )
        (low,) = project(n, tab, tokens, owns[2], parts[2], arrived[2], low, True, None, [base])
        return low, up, base

    low, up, base = lax.switch(plan[0], [functools.partial(planned, sizes) for sizes in plans])
    lows = [low, swap(low, "tensor"), swap(low, "dp")]
    lows.append(lax.ppermute(low, ("tensor", "dp"), [(0, 3), (1, 2), (2, 1), (3, 0)]))
    return finish(tab, 3 * (n - 1) + 2, up, lows, base, PER)


def plain_body(tokens, base_weight, skill_down, skill_up, alloc, block_tenant, block_len):
    rows, width = tokens.shape
    blocks = block_len.shape[0]
    block_rows = rows // blocks
    local_skills, slice_width, rank = skill_down.shape
    slice_out = skill_up.shape[2]
    down_size = slice_width * rank
    stacked = jnp.concatenate(
        [
            skill_down.reshape(local_skills, down_size),
            skill_up.reshape(local_skills, rank * slice_out),
        ],
        1,
    ).astype(F32)
    partial_sum = jnp.dot(alloc, stacked, precision=lax.Precision.HIGHEST)
    composed = lax.psum(partial_sum.astype(BF16), "skill")
    factors = jnp.take(composed, block_tenant, axis=0)
    down_part = factors[:, :down_size].reshape(blocks, slice_width, rank)
    up_part = factors[:, down_size:].reshape(blocks, rank, slice_out).astype(F32)
    grouped = tokens.reshape(blocks, block_rows, width)
    projected = jnp.einsum("bnd,bdr->bnr", grouped, down_part, preferred_element_type=F32)
    base_term = jnp.dot(tokens, base_weight, preferred_element_type=F32)
    lowrank = lax.psum(projected.astype(BF16), ("tensor", "dp")).astype(F32)
    base = lax.psum_scatter(
        base_term.astype(BF16), ("tensor", "dp"), scatter_dimension=1, tiled=True
    ).astype(F32)
    adapter = jnp.einsum("bnr,bro->bno", lowrank, up_part, precision=lax.Precision.HIGHEST)
    total = base.reshape(blocks, block_rows, slice_out) + adapter
    live = (jnp.arange(block_rows, dtype=I32)[None, :] < block_len[:, None])[:, :, None]
    return jnp.where(live, total, 0.0).astype(BF16).reshape(rows, slice_out)


def solution(mesh):
    placed = (
        P(("group", "skill"), ("tensor", "dp")),
        P(("tensor", "dp"), None),
        P("skill", ("tensor", "dp"), None),
        P("skill", None, ("tensor", "dp")),
        P("group", "skill"),
        P(("group", "skill")),
        P(("group", "skill")),
    )
    fits = (mesh.shape["skill"], mesh.shape["tensor"], mesh.shape["dp"]) == (4, 2, 2)
    body = line_body if fits else plain_body
    return jax.shard_map(
        body,
        mesh=mesh,
        in_specs=placed,
        out_specs=P(("group", "skill"), ("tensor", "dp")),
        check_vma=False,
    )
```

```python
import functools

import jax
import jax.numpy as jnp
from jax import lax
from jax.experimental import pallas as pl
from jax.experimental.pallas import tpu as pltpu
from jax.sharding import PartitionSpec as P

F32, BF16, I32 = jnp.float32, jnp.bfloat16, jnp.int32
MIB = 1 << 20
LANES = 128
LARGE = 1 << 21
PER = 6
EARLY = 0
BLOCKS_AT_ONCE = 4
SHARE = 1.0
VMEM = pl.BlockSpec(memory_space=pltpu.VMEM)
SMEM = pl.BlockSpec(memory_space=pltpu.SMEM)
ANY = pl.BlockSpec(memory_space=pl.ANY)
NT = (((1,), (1,)), ((), ()))
TN = (((0,), (0,)), ((), ()))
PLANS = ((17, 14, 10), (18, 15, 11), (20, 16, 11), (22, 18, 12))


def call(kernel, ins, specs, outs, out_specs, *, after=(), free=None, vmem=24, flops=0, nbytes=0, **kwargs):
    return pl.pallas_call(
        functools.partial(kernel, len(ins)),
        in_specs=specs + [ANY] * len(after),
        out_specs=out_specs,
        out_shape=outs,
        compiler_params=pltpu.CompilerParams(vmem_limit_bytes=vmem * MIB),
        cost_estimate=pl.CostEstimate(flops=int(SHARE * flops), bytes_accessed=int(SHARE * nbytes), transcendentals=0),
        **kwargs,
    )(*[x if free is True or x is free else placed(x) for x in ins], *after)


def placed(x):
    if x.dtype != BF16:
        return x
    return pltpu.with_memory_space_constraint(x, pltpu.HBM if x.size >= LARGE else pltpu.VMEM)


def shape(*dims, dtype=BF16):
    return jax.ShapeDtypeStruct(dims, dtype)


def kron_kernel(rank, ins, alloc_ref, kron_ref):
    tenants, skills = alloc_ref.shape
    depth = skills * rank
    at = lax.broadcasted_iota(I32, (skills, depth), 1)
    row = lax.broadcasted_iota(I32, (skills, depth), 0)
    inside = jnp.logical_and(at >= row * rank, at < (row + 1) * rank)
    repeat = jnp.where(inside, 1.0, 0.0).astype(BF16)
    spread = jnp.dot(alloc_ref[...].astype(BF16), repeat, preferred_element_type=F32)
    lane = lax.rem(lax.broadcasted_iota(I32, (rank, depth), 1), rank)
    diagonal = lane == lax.broadcasted_iota(I32, (rank, depth), 0)
    for t in range(tenants):
        kron_ref[t * rank : (t + 1) * rank, :] = jnp.where(diagonal, spread[t : t + 1, :], 0.0).astype(BF16)


def first_kernel(rank, ins, alloc_ref, library_ref, own_ref, kron_ref):
    kron_kernel(rank, 1, alloc_ref, kron_ref)
    made = jnp.dot(kron_ref[...], library_ref[...], preferred_element_type=F32).astype(BF16)
    own_ref[...] = made.reshape(own_ref.shape)


def compose_first(alloc, library, rank):
    tenants, skills = alloc.shape
    depth, out = library.shape
    return call(
        functools.partial(first_kernel, rank),
        [pltpu.with_memory_space_constraint(x, pltpu.HBM) for x in (alloc, library)],
        [pl.BlockSpec(x.shape, lambda j: (0, 0)) for x in (alloc, library)],
        [shape(tenants, rank, out), shape(tenants * rank, depth)],
        [VMEM] * 2,
        free=True,
        grid=(1,),
        flops=2 * tenants * rank * depth * out,
        nbytes=2 * depth * out,
    )


def compose_kernel(slots, ins, *refs):
    kron_ref, library_ref = refs[:2] if not slots else refs[1:3]
    own_ref = refs[-2] if slots else refs[-1]
    tenants, rank, size = own_ref.shape
    made = jnp.dot(kron_ref[...], library_ref[...], preferred_element_type=F32).astype(BF16)
    own_ref[...] = made.reshape(tenants, rank, size)
    if slots:
        copy_slots(refs[0], own_ref, refs[-1], slots)


def copy_slots(tab_ref, own_ref, out_ref, slots):
    def one(slot, carry):
        out_ref[slot] = own_ref[tab_ref[0, slot]]
        return carry

    lax.fori_loop(0, slots, one, 0, unroll=2)


def compose(kron, library, rank, part, tile, slots=0, tab=None, after=()):
    rows, depth = kron.shape
    tenants = rows // rank
    start, size = part
    at = start // tile
    outs, out_specs = [shape(tenants, rank, size)], [pl.BlockSpec((tenants, rank, tile), lambda j: (0, 0, j))]
    if slots:
        outs.append(shape(slots, rank, size))
        out_specs.append(pl.BlockSpec((slots, rank, tile), lambda j: (0, 0, j)))
    made = call(
        functools.partial(compose_kernel, slots),
        ([tab] if slots else []) + [kron, library],
        ([SMEM] if slots else []) + [VMEM, pl.BlockSpec((depth, tile), lambda j: (0, at + j))],
        outs,
        out_specs,
        after=after,
        grid=(size // tile,),
        flops=2 * rows * depth * size,
        nbytes=2 * (depth + rows) * size,
    )
    return made if slots else made[0]


def tables_kernel(n, tenants, plans, ins, place_ref, len_ref, *refs):
    arrays, tab_ref, plan_ref = refs[:-2], refs[-2], refs[-1]
    me = place_ref[0]
    blocks = arrays[0].shape[1]
    sub = lax.broadcasted_iota(I32, (tenants, tenants), 0)
    lane = lax.broadcasted_iota(I32, (tenants, tenants), 1)
    wide = lax.broadcasted_iota(I32, (tenants, LANES), 1)
    tenant = lax.broadcasted_iota(I32, (tenants, LANES), 0)
    one = lax.broadcasted_iota(I32, (tenants, blocks), 0)
    zs = [me ^ k for k in range(n)]
    groups = len(arrays)
    present = [
        [
            jnp.max(jnp.where(one == arrays[g][k : k + 1, :], 1.0, 0.0), axis=1, keepdims=True)
            for k in range(n)
        ]
        for g in range(groups)
    ]

    def union(keep, group=0):
        total = jnp.zeros((tenants, 1), F32)
        for z, here in zip(zs, present[group]):
            total = jnp.maximum(total, here * jnp.where(keep(z), 1.0, 0.0))
        return total

    def positions(held):
        across = jnp.sum(jnp.where(sub == lane, held, 0.0), axis=0, keepdims=True)
        return jnp.sum(jnp.where(lane < sub, across, 0.0), axis=1, keepdims=True)

    def pack(held, value):
        slot = positions(held).astype(I32)
        chosen = jnp.logical_and(slot == wide, held > 0.5)
        return jnp.sum(jnp.where(chosen, value, 0.0), axis=0, keepdims=True)

    send_right, send_left = union(lambda z: z > me), union(lambda z: z < me)
    from_left, from_right = positions(union(lambda z: z >= me)), positions(union(lambda z: z <= me))
    number = tenant.astype(F32)
    right = pack(send_right, number), pack(send_right, from_left)
    left = pack(send_left, number), pack(send_left, from_right)
    own = jnp.concatenate([arrays[0][0:1, :], jnp.zeros((1, LANES - blocks), I32)], axis=1)
    mine = own == tenant

    def at(place, rows, otherwise):
        return jnp.where(me == place, rows, otherwise)

    none = jnp.zeros((1, LANES), F32)
    final_right = jnp.sum(jnp.where(mine, from_left, 0.0), axis=0, keepdims=True)
    final_left = jnp.sum(jnp.where(mine, from_right, 0.0), axis=0, keepdims=True)
    rows = []
    for part in (0, 1):
        for hop in range(n - 1):
            rows.append(at(hop, right[part], at(n - 1 - hop, left[part], none)))
    for hop in range(n - 1):
        rows.append(at(hop + 1, final_right, at(n - 2 - hop, final_left, none)))
    for row, value in enumerate(rows):
        tab_ref[row : row + 1, :] = value.astype(I32)
    tab_ref[len(rows) : len(rows) + 1, :] = own
    tab_ref[len(rows) + 2 : len(rows) + 3, :] = jnp.concatenate([len_ref[...], jnp.zeros((1, LANES - blocks), I32)], axis=1)
    ends_here = jnp.logical_or(me == 0, me == n - 1)
    tab_ref[len(rows) + 1 : len(rows) + 2, :] = jnp.where(ends_here, jnp.ones_like(own), jnp.zeros_like(own))

    held = jnp.zeros((tenants, LANES), F32)
    hop_of = lax.broadcasted_iota(I32, (1, LANES), 1)
    limits = [jnp.full((1, LANES), float(tenants), F32) for _ in plans]
    column = 0
    for group in range(groups):
        for hop in range(n - 1):
            for keep in (lambda z: z > hop, lambda z: z < n - 1 - hop):
                held = jnp.where(wide == column, union(keep, group), held)
                limits = [jnp.where(hop_of == column, float(p[hop]), l) for p, l in zip(plans, limits)]
                column += 1
    counts = jnp.sum(held, axis=0, keepdims=True)
    plan = jnp.int32(0)
    for limit in limits[:-1]:
        plan = plan + jnp.where(jnp.max(counts - limit) > 0.5, 1, 0)
    plan_ref[0] = plan


def make_tables(n, tenants, plans, place, lens, arrays):
    rows = -(-(3 * (n - 1) + 3) // 8) * 8
    return call(
        functools.partial(tables_kernel, n, tenants, plans),
        [place, lens, *arrays],
        [SMEM] + [VMEM] * (1 + len(arrays)),
        [shape(rows, LANES, dtype=I32), shape(1, dtype=I32)],
        [VMEM, SMEM],
    )


def step_kernel(n, jobs, passed, unroll, ins, tab_ref, *refs):
    given, outs = list(refs[: ins - 1]), refs[ins - 1 + passed :]
    for (hop, slots, pieces), out_ref in zip(jobs, outs):
        both = slots is None
        if both:
            slots = out_ref.shape[0] // 2
            fresh_ref = given.pop(0)

            @pl.when(tab_ref[3 * (n - 1) + 1, 0] > 0)
            def _(fresh_ref=fresh_ref, out_ref=out_ref):
                out_ref[: fresh_ref.shape[0]] = fresh_ref[...]

        held = [(given.pop(0), given.pop(0) if hop else None) for _ in pieces]

        def one(slot, carry, hop=hop, pieces=pieces, held=held, out_ref=out_ref, both=both, slots=slots):
            tenant = tab_ref[hop, slot]
            at = 0
            made = []
            for by_tenant, (own_ref, in_ref) in zip(pieces, held):
                block = own_ref[tenant]
                if hop:
                    index = tenant if by_tenant else tab_ref[n - 1 + hop, slot]
                    block = (block.astype(F32) + in_ref[index].astype(F32)).astype(BF16)
                made.append(block)
            block = jnp.concatenate(made, axis=1) if len(made) > 1 else made[0]
            if both:
                half = out_ref.shape[2]
                out_ref[slot] = block[:, :half]
                out_ref[slots + slot] = block[:, half:]
            else:
                out_ref[slot] = block
            return carry

        def all_slots(one=one, slots=slots):
            lax.fori_loop(0, slots, one, 0, unroll=unroll)

        if both:
            pl.when(tab_ref[3 * (n - 1) + 1, 0] == 0)(all_slots)
        else:
            all_slots()


def step(n, tab, jobs, after=(), through=(), rare=0):
    ins, shapes, plan = [], [], []
    for hop, slots, pieces in jobs:
        columns = sum(own.shape[2] for own, _, _ in pieces)
        if isinstance(slots, tuple):
            plan.append((hop, None, [by_tenant for _, _, by_tenant in pieces]))
            ins.append(slots[1])
            slots, columns = 2 * slots[0], columns // 2
            assert slots >= ins[-1].shape[0] and columns == ins[-1].shape[2]
        else:
            plan.append((hop, slots, [by_tenant for _, _, by_tenant in pieces]))
        for own, arrived, _ in pieces:
            ins += [own, arrived] if hop else [own]
        shapes.append(shape(slots, pieces[0][0].shape[1], columns))
    return call(
        functools.partial(step_kernel, n, plan, len(after) + len(through), rare or True),
        [tab, *ins],
        [SMEM] + [VMEM] * len(ins),
        shapes + [shape(*x.shape) for x in through],
        [VMEM] * len(shapes) + [ANY] * len(through),
        after=list(after) + list(through),
        input_output_aliases={1 + len(ins) + len(after) + i: len(shapes) + i for i in range(len(through))},
        nbytes=sum(2 * 3 * x.size for x in shapes),
    )


def read(ref, slot, start, size):
    half = ref.shape[2]
    if start + size <= half and start == 0 and size == half:
        return ref[slot]
    slots = ref.shape[0] // 2
    pieces = []
    while size:
        part, at = divmod(start, half)
        count = min(size, half - at)
        pieces.append(ref[part * slots + slot, :, at : at + count])
        start, size = start + count, size - count
    return jnp.concatenate(pieces, axis=1) if len(pieces) > 1 else pieces[0]


def factor_of(n, b, by_tenant, tab_ref, own_ref, arrived, lead=0):
    tenant = tab_ref[3 * (n - 1), b]
    factor = own_ref[tenant].astype(F32)
    outer = tab_ref[3 * (n - 1) + 1, 0] > 0
    for hop in range(n - 1):
        index = tenant if by_tenant and hop == 0 else tab_ref[2 * (n - 1) + hop, b]
        came = read(arrived[hop], index, lead, own_ref.shape[2]) if hop == n - 2 else arrived[hop][index]
        came = came.astype(F32)
        used = jnp.where(outer, 1, 0) if hop == n - 2 else jnp.where(outer, 0, 1)
        factor = jnp.where(used > 0, factor + came, factor)
    return factor.astype(BF16)


def project_kernel(n, unroll, first, out, ins, tab_ref, tokens_ref, own_ref, *refs):
    arrived = refs[: n - 1]
    total_ref = None if first else refs[ins - 4]
    outs = refs[-2:] if out else refs[-1:]
    size = tokens_ref.shape[1]

    def one(b, carry):
        factor = factor_of(n, b, False, tab_ref, own_ref, arrived)
        at = pl.ds(pl.multiple_of(b * LANES, LANES), LANES)
        part = lax.dot_general(factor, tokens_ref[at, :], NT, preferred_element_type=F32)
        if not first:
            part = total_ref[:, at] + part
        outs[0][:, at] = part.astype(outs[0].dtype)
        if out:
            outs[1][b] = factor_of(n, b, True, tab_ref, refs[n - 1], refs[n : 2 * n - 1], own_ref.shape[2])
        return carry

    lax.fori_loop(0, tokens_ref.shape[0] // LANES, one, 0, unroll=unroll)


def project(n, tab, tokens, own, part, arrived, total, last, up=None, after=(), rare=0):
    tenants, rank, size = own.shape
    rows = tokens.shape[0]
    at = part[0] // size
    outs = [shape(rank, rows, dtype=BF16 if last else F32)]
    ins = [tab, tokens, own, *arrived]
    if up:
        outs.append(shape(rows // LANES, rank, up[0].shape[2]))
        ins += [up[0], *up[1]]
    if total is not None:
        ins.append(total)
    return call(
        functools.partial(project_kernel, n, rare or BLOCKS_AT_ONCE, total is None, up is not None),
        ins,
        [SMEM, pl.BlockSpec((rows, size), lambda j: (0, at))] + [VMEM] * (len(ins) - 2),
        outs,
        [VMEM] * len(outs),
        after=after,
        free=tokens,
        grid=(1,),
        flops=2 * rows * size * rank,
        nbytes=2 * size * (rows + 2 * tenants * rank),
    )


def base_kernel(order_ref, tokens_ref, first_ref, second_ref, *refs):
    for weight_ref, out_ref in ((first_ref, refs[-2]), (second_ref, refs[-1])):
        out_ref[...] = jnp.dot(tokens_ref[...], weight_ref[...], preferred_element_type=F32).astype(BF16)


def base_product(order, tokens, weight, out, after, first, last):
    strip, width = tokens.shape[0] // 3, tokens.shape[1]
    rows = (last - first) * strip
    flops, nbytes = 4 * rows * width * out, 2 * (rows * (width + 2 * out) + 2 * width * out)
    return pl.pallas_call(
        base_kernel,
        grid_spec=pltpu.PrefetchScalarGridSpec(
            num_scalar_prefetch=1,
            grid=(last - first,),
            in_specs=[
                pl.BlockSpec((strip, width), lambda m, order: (first + m, 0)),
                pl.BlockSpec((width, out), lambda m, order: (0, order[0])),
                pl.BlockSpec((width, out), lambda m, order: (0, order[1])),
            ]
            + [ANY] * len(after),
            out_specs=[pl.BlockSpec((strip, out), lambda m, order: (m, 0))] * 2,
        ),
        out_shape=[shape(rows, out)] * 2,
        compiler_params=pltpu.CompilerParams(vmem_limit_bytes=24 * MIB),
        cost_estimate=pl.CostEstimate(flops=int(SHARE * flops), bytes_accessed=int(SHARE * nbytes), transcendentals=0),
    )(order, tokens, placed(weight), placed(weight), *after)


def rows_kernel(pieces, ins, *refs):
    at = 0
    for length, terms in pieces:
        total = 0.0
        for which, start in terms:
            total = total + refs[which][start : start + length, :].astype(F32)
        refs[-1][at : at + length, :] = total.astype(BF16)
        at += length


def add_rows(arrays, pieces, after=()):
    rows, width = sum(length for length, _ in pieces), arrays[0].shape[1]
    return call(
        functools.partial(rows_kernel, pieces),
        list(arrays),
        [VMEM] * len(arrays),
        shape(rows, width),
        VMEM,
        after=after,
        nbytes=8 * rows * width,
    )


def finish_kernel(row, per, ins, tab_ref, up_ref, *refs):
    lows, base_ref, out_ref = refs[:4], refs[4], refs[5]
    width = out_ref.shape[1]
    low = lows[0][...].astype(F32)
    for other in lows[1:]:
        low = low + other[...].astype(F32)
    low = low.astype(BF16)
    for j in range(per):
        b = pl.program_id(0) * per + j
        at = slice(j * LANES, (j + 1) * LANES)
        total = lax.dot_general(low[:, at], up_ref[b], TN, preferred_element_type=F32)
        total = total + base_ref[at, :].astype(F32)
        live = lax.broadcasted_iota(I32, (LANES, width), 0) < tab_ref[row, b]
        out_ref[at, :] = jnp.where(live, total, 0.0).astype(out_ref.dtype)


def finish(tab, row, up, lows, base, per):
    rank, rows = lows[0].shape
    width = base.shape[1]
    blocks = rows // LANES
    whole = pl.BlockSpec((per * LANES, width), lambda j: (j, 0))
    return call(
        functools.partial(finish_kernel, row, per),
        [tab, up, *lows, pltpu.with_memory_space_constraint(base, pltpu.HBM)],
        [SMEM, VMEM] + [pl.BlockSpec((rank, per * LANES), lambda j: (0, j))] * 4 + [whole],
        shape(rows, width),
        whole,
        free=True,
        grid=(blocks // per,),
        flops=2 * rows * rank * width,
        nbytes=4 * rows * width,
    )


def swap(x, axis):
    return lax.ppermute(x, axis, [(0, 1), (1, 0)])


def ends(x):
    return lax.ppermute(x, "skill", [(0, 1), (1, 0), (2, 3), (3, 2)])


def inward(x):
    return lax.ppermute(x, "skill", [(0, 1), (3, 2)])


def outward(x):
    return lax.ppermute(x, "skill", [(1, 0), (2, 3)])


def middle(x):
    pairs = [(2 + c, 4 + c) for c in (0, 1)] + [(0, 1), (6, 7)]
    return lax.ppermute(x, ("skill", "tensor"), pairs + [(b, a) for a, b in pairs])


def line_body(tokens, base_weight, skill_down, skill_up, alloc, block_tenant, block_len):
    n = 4
    rows, width = tokens.shape
    tenants, local_skills = alloc.shape
    rank = skill_down.shape[2]
    out = skill_up.shape[2]
    blocks = block_len.shape[0]
    me = lax.axis_index("skill")
    tensor, dp = lax.axis_index("tensor"), lax.axis_index("dp")
    hops = [ends, middle, ends]
    full = [min(tenants, blocks * (n - 1 - h)) for h in range(n - 1)]
    plans = [[min(f, p) for f, p in zip(full, plan)] for plan in PLANS] + [full]
    tile = width // 8
    parts = [(0, 3 * tile), (3 * tile, 3 * tile), (6 * tile, 2 * tile)]

    own_t = block_tenant.reshape(1, blocks)
    seen = jnp.concatenate(
        [own_t]
        + [lax.ppermute(own_t, "skill", [(j, j ^ k) for j in range(n)]) for k in range(1, n)],
        axis=0,
    )
    library = jnp.transpose(skill_down, (0, 2, 1)).reshape(local_skills * rank, width)
    own_up, kron = compose_first(alloc, skill_up.reshape(local_skills * rank, out), rank)
    own_up, seen = lax.optimization_barrier((own_up, seen))
    up_0 = ends(own_up)
    seen = [seen, swap(seen, "group")]
    own_0 = compose(kron, library, rank, parts[0], tile, after=[own_up])
    tab, plan = make_tables(n, tenants, plans, me.reshape(1).astype(I32), block_len.reshape(1, blocks), seen)
    theirs, ours = (1 - tensor) * 2, tensor * 2
    order_cross = jnp.stack([theirs + 1 - dp, ours + 1 - dp]).astype(I32)
    order_stay = jnp.stack([theirs + dp, ours + dp]).astype(I32)

    def planned(rare, sizes):
        step_, project_ = functools.partial(step, rare=rare), functools.partial(project, rare=rare)
        owns, arrived, up_came = [own_0], [[], [], []], [up_0]

        def job(h, k):
            return h, sizes[h], [(owns[k], arrived[k][h - 1] if h else None, False)]

        up_piece = (own_up, up_0, True)
        first, up_1 = step_(n, tab, [job(0, 0), (1, sizes[1], [up_piece])])
        arrived[0].append(ends(first))
        up_came.append(middle(up_1))
        own, message = compose(kron, library, rank, parts[1], tile, sizes[0], tab)
        owns.append(own)
        arrived[1].append(ends(message))
        cut = rows // 3
        away, keep = base_product(order_cross, tokens, base_weight, out, [message], 0, 1)

        to_1, away = step_(n, tab, [job(1, 0)], [keep, up_came[1]], [away])
        arrived[0].append(middle(to_1))
        core = swap(away, "tensor")
        own, message = compose(kron, library, rank, parts[2], tile, sizes[0], tab, [to_1])
        owns.append(own)
        away_2, keep_2 = base_product(order_cross, tokens, base_weight, out, [own], 1, 3)
        if EARLY:
            stay, stay_keep = base_product(order_stay, tokens, base_weight, out, [keep_2], 0, 3)

        first_and_up = 2, (max(sizes[2], (sizes[0] + 1) // 2), message), [
            (owns[0], arrived[0][1], False),
            (own_up, up_came[1], False),
        ]
        to_1, to_2, away_2 = step_(n, tab, [job(1, 1), first_and_up], [core, keep_2] + ([stay] if EARLY else []), [away_2])
        arrived[1].append(middle(to_1))
        exchanged = ends(to_2)
        arrived[0].append(exchanged)
        arrived[2].append(exchanged)
        up_came.append(exchanged)
        core_2 = swap(away_2, "tensor")
        near = add_rows([keep, core], [(cut, [(0, 0), (1, 0)])], [to_1])
        across = swap(near, "dp")
        if not EARLY:
            stay, stay_keep = base_product(order_stay, tokens, base_weight, out, [near], 0, 3)
        near_2 = add_rows([keep_2, core_2], [(rows - cut, [(0, 0), (1, 0)])])

        to_1, to_2, stay, near_2 = step_(n, tab, [job(1, 2), job(2, 1)], [across, stay_keep], [stay, near_2])
        arrived[2].append(middle(to_1))
        arrived[1].append(outward(to_2))
        across_2 = swap(near_2, "dp")
        core = swap(stay, "tensor")
        low, up = project_(n, tab, tokens, owns[0], parts[0], arrived[0], None, False, (own_up, up_came), [to_1])

        (to_2,) = step_(n, tab, [job(2, 2)], [low, core])
        arrived[2].append(outward(to_2))
        (low,) = project_(n, tab, tokens, owns[1], parts[1], arrived[1], low, False, None, [to_2])
        base = add_rows(
            [stay_keep, core, across, across_2],
            [(cut, [(0, 0), (1, 0), (2, 0)]), (rows - cut, [(0, cut), (1, cut), (3, 0)])],
            [low],
        )
        (low,) = project_(n, tab, tokens, owns[2], parts[2], arrived[2], low, True, None, [base])
        return low, up, base

    low, up, base = lax.switch(plan[0], [functools.partial(planned, int(k > 2), sizes) for k, sizes in enumerate(plans)])
    lows = [low, swap(low, "tensor"), swap(low, "dp")]
    lows.append(lax.ppermute(low, ("tensor", "dp"), [(0, 3), (1, 2), (2, 1), (3, 0)]))
    return finish(tab, 3 * (n - 1) + 2, up, lows, base, PER)


def plain_body(tokens, base_weight, skill_down, skill_up, alloc, block_tenant, block_len):
    rows, width = tokens.shape
    blocks = block_len.shape[0]
    block_rows = rows // blocks
    local_skills, slice_width, rank = skill_down.shape
    slice_out = skill_up.shape[2]
    down_size = slice_width * rank
    stacked = jnp.concatenate(
        [
            skill_down.reshape(local_skills, down_size),
            skill_up.reshape(local_skills, rank * slice_out),
        ],
        1,
    ).astype(F32)
    partial_sum = jnp.dot(alloc, stacked, precision=lax.Precision.HIGHEST)
    composed = lax.psum(partial_sum.astype(BF16), "skill")
    factors = jnp.take(composed, block_tenant, axis=0)
    down_part = factors[:, :down_size].reshape(blocks, slice_width, rank)
    up_part = factors[:, down_size:].reshape(blocks, rank, slice_out).astype(F32)
    grouped = tokens.reshape(blocks, block_rows, width)
    projected = jnp.einsum("bnd,bdr->bnr", grouped, down_part, preferred_element_type=F32)
    base_term = jnp.dot(tokens, base_weight, preferred_element_type=F32)
    lowrank = lax.psum(projected.astype(BF16), ("tensor", "dp")).astype(F32)
    base = lax.psum_scatter(
        base_term.astype(BF16), ("tensor", "dp"), scatter_dimension=1, tiled=True
    ).astype(F32)
    adapter = jnp.einsum("bnr,bro->bno", lowrank, up_part, precision=lax.Precision.HIGHEST)
    total = base.reshape(blocks, block_rows, slice_out) + adapter
    live = (jnp.arange(block_rows, dtype=I32)[None, :] < block_len[:, None])[:, :, None]
    return jnp.where(live, total, 0.0).astype(BF16).reshape(rows, slice_out)


def solution(mesh):
    placed = (
        P(("group", "skill"), ("tensor", "dp")),
        P(("tensor", "dp"), None),
        P("skill", ("tensor", "dp"), None),
        P("skill", None, ("tensor", "dp")),
        P("group", "skill"),
        P(("group", "skill")),
        P(("group", "skill")),
    )
    fits = (mesh.shape["skill"], mesh.shape["tensor"], mesh.shape["dp"]) == (4, 2, 2)
    body = line_body if fits else plain_body
    return jax.shard_map(
        body,
        mesh=mesh,
        in_specs=placed,
        out_specs=P(("group", "skill"), ("tensor", "dp")),
        check_vma=False,
    )
```

```python
import functools

import jax
import jax.numpy as jnp
from jax import lax
from jax.experimental import pallas as pl
from jax.experimental.pallas import tpu as pltpu
from jax.sharding import PartitionSpec as P

F32, BF16, I32 = jnp.float32, jnp.bfloat16, jnp.int32
MIB = 1 << 20
LANES = 128
LARGE = 1 << 21
PER = 6
EARLY = 0
BLOCKS_AT_ONCE = 4
SHARE = 1.0
VMEM = pl.BlockSpec(memory_space=pltpu.VMEM)
SMEM = pl.BlockSpec(memory_space=pltpu.SMEM)
ANY = pl.BlockSpec(memory_space=pl.ANY)
NT = (((1,), (1,)), ((), ()))
TN = (((0,), (0,)), ((), ()))
PLANS = ((17, 14, 10), (18, 15, 11), (20, 16, 11), (22, 18, 12))


def call(kernel, ins, specs, outs, out_specs, *, after=(), free=None, vmem=24, flops=0, nbytes=0, **kwargs):
    return pl.pallas_call(
        functools.partial(kernel, len(ins)),
        in_specs=specs + [ANY] * len(after),
        out_specs=out_specs,
        out_shape=outs,
        compiler_params=pltpu.CompilerParams(vmem_limit_bytes=vmem * MIB),
        cost_estimate=pl.CostEstimate(flops=int(SHARE * flops), bytes_accessed=int(SHARE * nbytes), transcendentals=0),
        **kwargs,
    )(*[x if free is True or x is free else placed(x) for x in ins], *after)


def placed(x):
    if x.dtype != BF16:
        return x
    return pltpu.with_memory_space_constraint(x, pltpu.HBM if x.size >= LARGE else pltpu.VMEM)


def shape(*dims, dtype=BF16):
    return jax.ShapeDtypeStruct(dims, dtype)


def kron_kernel(rank, ins, alloc_ref, kron_ref):
    tenants, skills = alloc_ref.shape
    depth = skills * rank
    at = lax.broadcasted_iota(I32, (skills, depth), 1)
    row = lax.broadcasted_iota(I32, (skills, depth), 0)
    inside = jnp.logical_and(at >= row * rank, at < (row + 1) * rank)
    repeat = jnp.where(inside, 1.0, 0.0).astype(BF16)
    spread = jnp.dot(alloc_ref[...].astype(BF16), repeat, preferred_element_type=F32)
    lane = lax.rem(lax.broadcasted_iota(I32, (rank, depth), 1), rank)
    diagonal = lane == lax.broadcasted_iota(I32, (rank, depth), 0)
    for t in range(tenants):
        kron_ref[t * rank : (t + 1) * rank, :] = jnp.where(diagonal, spread[t : t + 1, :], 0.0).astype(BF16)


def first_kernel(rank, ins, alloc_ref, library_ref, own_ref, kron_ref):
    kron_kernel(rank, 1, alloc_ref, kron_ref)
    made = jnp.dot(kron_ref[...], library_ref[...], preferred_element_type=F32).astype(BF16)
    own_ref[...] = made.reshape(own_ref.shape)


def compose_first(alloc, library, rank):
    tenants, skills = alloc.shape
    depth, out = library.shape
    return call(
        functools.partial(first_kernel, rank),
        [pltpu.with_memory_space_constraint(x, pltpu.HBM) for x in (alloc, library)],
        [pl.BlockSpec(x.shape, lambda j: (0, 0)) for x in (alloc, library)],
        [shape(tenants, rank, out), shape(tenants * rank, depth)],
        [VMEM] * 2,
        free=True,
        grid=(1,),
        flops=2 * tenants * rank * depth * out,
        nbytes=2 * depth * out,
    )


def compose_kernel(slots, ins, *refs):
    kron_ref, library_ref = refs[:2] if not slots else refs[1:3]
    own_ref = refs[-2] if slots else refs[-1]
    tenants, rank, size = own_ref.shape
    made = jnp.dot(kron_ref[...], library_ref[...], preferred_element_type=F32).astype(BF16)
    own_ref[...] = made.reshape(tenants, rank, size)
    if slots:
        copy_slots(refs[0], own_ref, refs[-1], slots)


def copy_slots(tab_ref, own_ref, out_ref, slots):
    def one(slot, carry):
        out_ref[slot] = own_ref[tab_ref[0, slot]]
        return carry

    lax.fori_loop(0, slots, one, 0, unroll=2)


def compose(kron, library, rank, part, tile, slots=0, tab=None, after=()):
    rows, depth = kron.shape
    tenants = rows // rank
    start, size = part
    at = start // tile
    outs, out_specs = [shape(tenants, rank, size)], [pl.BlockSpec((tenants, rank, tile), lambda j: (0, 0, j))]
    if slots:
        outs.append(shape(slots, rank, size))
        out_specs.append(pl.BlockSpec((slots, rank, tile), lambda j: (0, 0, j)))
    made = call(
        functools.partial(compose_kernel, slots),
        ([tab] if slots else []) + [kron, library],
        ([SMEM] if slots else []) + [VMEM, pl.BlockSpec((depth, tile), lambda j: (0, at + j))],
        outs,
        out_specs,
        after=after,
        grid=(size // tile,),
        flops=2 * rows * depth * size,
        nbytes=2 * (depth + rows) * size,
    )
    return made if slots else made[0]


def tables_kernel(n, tenants, plans, ins, place_ref, len_ref, *refs):
    arrays, tab_ref, plan_ref = refs[:-2], refs[-2], refs[-1]
    me = place_ref[0]
    blocks = arrays[0].shape[1]
    sub = lax.broadcasted_iota(I32, (tenants, tenants), 0)
    lane = lax.broadcasted_iota(I32, (tenants, tenants), 1)
    wide = lax.broadcasted_iota(I32, (tenants, LANES), 1)
    tenant = lax.broadcasted_iota(I32, (tenants, LANES), 0)
    one = lax.broadcasted_iota(I32, (tenants, blocks), 0)
    zs = [me ^ k for k in range(n)]
    groups = len(arrays)
    present = [
        [
            jnp.max(jnp.where(one == arrays[g][k : k + 1, :], 1.0, 0.0), axis=1, keepdims=True)
            for k in range(n)
        ]
        for g in range(groups)
    ]

    def union(keep, group=0):
        total = jnp.zeros((tenants, 1), F32)
        for z, here in zip(zs, present[group]):
            total = jnp.maximum(total, here * jnp.where(keep(z), 1.0, 0.0))
        return total

    def positions(held):
        across = jnp.sum(jnp.where(sub == lane, held, 0.0), axis=0, keepdims=True)
        return jnp.sum(jnp.where(lane < sub, across, 0.0), axis=1, keepdims=True)

    def pack(held, value):
        slot = positions(held).astype(I32)
        chosen = jnp.logical_and(slot == wide, held > 0.5)
        return jnp.sum(jnp.where(chosen, value, 0.0), axis=0, keepdims=True)

    send_right, send_left = union(lambda z: z > me), union(lambda z: z < me)
    from_left, from_right = positions(union(lambda z: z >= me)), positions(union(lambda z: z <= me))
    number = tenant.astype(F32)
    right = pack(send_right, number), pack(send_right, from_left)
    left = pack(send_left, number), pack(send_left, from_right)
    own = jnp.concatenate([arrays[0][0:1, :], jnp.zeros((1, LANES - blocks), I32)], axis=1)
    mine = own == tenant

    def at(place, rows, otherwise):
        return jnp.where(me == place, rows, otherwise)

    none = jnp.zeros((1, LANES), F32)
    final_right = jnp.sum(jnp.where(mine, from_left, 0.0), axis=0, keepdims=True)
    final_left = jnp.sum(jnp.where(mine, from_right, 0.0), axis=0, keepdims=True)
    rows = []
    for part in (0, 1):
        for hop in range(n - 1):
            rows.append(at(hop, right[part], at(n - 1 - hop, left[part], none)))
    for hop in range(n - 1):
        rows.append(at(hop + 1, final_right, at(n - 2 - hop, final_left, none)))
    for row, value in enumerate(rows):
        tab_ref[row : row + 1, :] = value.astype(I32)
    tab_ref[len(rows) : len(rows) + 1, :] = own
    tab_ref[len(rows) + 2 : len(rows) + 3, :] = jnp.concatenate([len_ref[...], jnp.zeros((1, LANES - blocks), I32)], axis=1)
    ends_here = jnp.logical_or(me == 0, me == n - 1)
    tab_ref[len(rows) + 1 : len(rows) + 2, :] = jnp.where(ends_here, jnp.ones_like(own), jnp.zeros_like(own))

    held = jnp.zeros((tenants, LANES), F32)
    hop_of = lax.broadcasted_iota(I32, (1, LANES), 1)
    limits = [jnp.full((1, LANES), float(tenants), F32) for _ in plans]
    column = 0
    for group in range(groups):
        for hop in range(n - 1):
            for keep in (lambda z: z > hop, lambda z: z < n - 1 - hop):
                held = jnp.where(wide == column, union(keep, group), held)
                limits = [jnp.where(hop_of == column, float(p[hop]), l) for p, l in zip(plans, limits)]
                column += 1
    counts = jnp.sum(held, axis=0, keepdims=True)
    plan = jnp.int32(0)
    for limit in limits[:-1]:
        plan = plan + jnp.where(jnp.max(counts - limit) > 0.5, 1, 0)
    plan_ref[0] = plan


def make_tables(n, tenants, plans, place, lens, arrays):
    rows = -(-(3 * (n - 1) + 3) // 8) * 8
    return call(
        functools.partial(tables_kernel, n, tenants, plans),
        [place, lens, *arrays],
        [SMEM] + [VMEM] * (1 + len(arrays)),
        [shape(rows, LANES, dtype=I32), shape(1, dtype=I32)],
        [VMEM, SMEM],
    )


def step_kernel(n, jobs, passed, unroll, ins, tab_ref, *refs):
    given, outs = list(refs[: ins - 1]), refs[ins - 1 + passed :]
    for (hop, slots, pieces), out_ref in zip(jobs, outs):
        both = slots is None
        if both:
            slots = out_ref.shape[0] // 2
            fresh_ref = given.pop(0)

            @pl.when(tab_ref[3 * (n - 1) + 1, 0] > 0)
            def _(fresh_ref=fresh_ref, out_ref=out_ref):
                out_ref[: fresh_ref.shape[0]] = fresh_ref[...]

        held = [(given.pop(0), given.pop(0) if hop else None) for _ in pieces]

        def one(slot, carry, hop=hop, pieces=pieces, held=held, out_ref=out_ref, both=both, slots=slots):
            tenant = tab_ref[hop, slot]
            at = 0
            made = []
            for by_tenant, (own_ref, in_ref) in zip(pieces, held):
                block = own_ref[tenant]
                if hop:
                    index = tenant if by_tenant else tab_ref[n - 1 + hop, slot]
                    block = (block.astype(F32) + in_ref[index].astype(F32)).astype(BF16)
                made.append(block)
            block = jnp.concatenate(made, axis=1) if len(made) > 1 else made[0]
            if both:
                half = out_ref.shape[2]
                out_ref[slot] = block[:, :half]
                out_ref[slots + slot] = block[:, half:]
            else:
                out_ref[slot] = block
            return carry

        def all_slots(one=one, slots=slots):
            lax.fori_loop(0, slots, one, 0, unroll=unroll)

        if both:
            pl.when(tab_ref[3 * (n - 1) + 1, 0] == 0)(all_slots)
        else:
            all_slots()


def step(n, tab, jobs, after=(), through=(), rare=0):
    ins, shapes, plan = [], [], []
    for hop, slots, pieces in jobs:
        columns = sum(own.shape[2] for own, _, _ in pieces)
        if isinstance(slots, tuple):
            plan.append((hop, None, [by_tenant for _, _, by_tenant in pieces]))
            ins.append(slots[1])
            slots, columns = 2 * slots[0], columns // 2
            assert slots >= ins[-1].shape[0] and columns == ins[-1].shape[2]
        else:
            plan.append((hop, slots, [by_tenant for _, _, by_tenant in pieces]))
        for own, arrived, _ in pieces:
            ins += [own, arrived] if hop else [own]
        shapes.append(shape(slots, pieces[0][0].shape[1], columns))
    return call(
        functools.partial(step_kernel, n, plan, len(after) + len(through), rare or True),
        [tab, *ins],
        [SMEM] + [VMEM] * len(ins),
        shapes + [shape(*x.shape) for x in through],
        [VMEM] * len(shapes) + [ANY] * len(through),
        after=list(after) + list(through),
        input_output_aliases={1 + len(ins) + len(after) + i: len(shapes) + i for i in range(len(through))},
        nbytes=sum(2 * 3 * x.size for x in shapes),
    )


def read(ref, slot, start, size):
    half = ref.shape[2]
    if start + size <= half and start == 0 and size == half:
        return ref[slot]
    slots = ref.shape[0] // 2
    pieces = []
    while size:
        part, at = divmod(start, half)
        count = min(size, half - at)
        pieces.append(ref[part * slots + slot, :, at : at + count])
        start, size = start + count, size - count
    return jnp.concatenate(pieces, axis=1) if len(pieces) > 1 else pieces[0]


def factor_of(n, b, by_tenant, tab_ref, own_ref, arrived, lead=0):
    tenant = tab_ref[3 * (n - 1), b]
    factor = own_ref[tenant].astype(F32)
    outer = tab_ref[3 * (n - 1) + 1, 0] > 0
    for hop in range(n - 1):
        index = tenant if by_tenant and hop == 0 else tab_ref[2 * (n - 1) + hop, b]
        came = read(arrived[hop], index, lead, own_ref.shape[2]) if hop == n - 2 else arrived[hop][index]
        came = came.astype(F32)
        used = jnp.where(outer, 1, 0) if hop == n - 2 else jnp.where(outer, 0, 1)
        factor = jnp.where(used > 0, factor + came, factor)
    return factor.astype(BF16)


def project_kernel(n, unroll, first, out, ins, tab_ref, tokens_ref, own_ref, *refs):
    arrived = refs[: n - 1]
    total_ref = None if first else refs[ins - 4]
    outs = refs[-2:] if out else refs[-1:]
    size = tokens_ref.shape[1]

    def one(b, carry):
        factor = factor_of(n, b, False, tab_ref, own_ref, arrived)
        at = pl.ds(pl.multiple_of(b * LANES, LANES), LANES)
        part = lax.dot_general(factor, tokens_ref[at, :], NT, preferred_element_type=F32)
        if not first:
            part = total_ref[:, at] + part
        outs[0][:, at] = part.astype(outs[0].dtype)
        if out:
            outs[1][b] = factor_of(n, b, True, tab_ref, refs[n - 1], refs[n : 2 * n - 1], own_ref.shape[2])
        return carry

    lax.fori_loop(0, tokens_ref.shape[0] // LANES, one, 0, unroll=unroll)


def project(n, tab, tokens, own, part, arrived, total, last, up=None, after=(), rare=0):
    tenants, rank, size = own.shape
    rows = tokens.shape[0]
    at = part[0] // size
    outs = [shape(rank, rows, dtype=BF16 if last else F32)]
    ins = [tab, tokens, own, *arrived]
    if up:
        outs.append(shape(rows // LANES, rank, up[0].shape[2]))
        ins += [up[0], *up[1]]
    if total is not None:
        ins.append(total)
    return call(
        functools.partial(project_kernel, n, rare or BLOCKS_AT_ONCE, total is None, up is not None),
        ins,
        [SMEM, pl.BlockSpec((rows, size), lambda j: (0, at))] + [VMEM] * (len(ins) - 2),
        outs,
        [VMEM] * len(outs),
        after=after,
        free=tokens,
        grid=(1,),
        flops=2 * rows * size * rank,
        nbytes=2 * size * (rows + 2 * tenants * rank),
    )


def base_kernel(order_ref, tokens_ref, first_ref, second_ref, *refs):
    for weight_ref, out_ref in ((first_ref, refs[-2]), (second_ref, refs[-1])):
        out_ref[...] = jnp.dot(tokens_ref[...], weight_ref[...], preferred_element_type=F32).astype(BF16)


def base_product(order, tokens, weight, out, after, first, last):
    strip, width = tokens.shape[0] // 3, tokens.shape[1]
    rows = (last - first) * strip
    flops, nbytes = 4 * rows * width * out, 2 * (rows * (width + 2 * out) + 2 * width * out)
    return pl.pallas_call(
        base_kernel,
        grid_spec=pltpu.PrefetchScalarGridSpec(
            num_scalar_prefetch=1,
            grid=(last - first,),
            in_specs=[
                pl.BlockSpec((strip, width), lambda m, order: (first + m, 0)),
                pl.BlockSpec((width, out), lambda m, order: (0, order[0])),
                pl.BlockSpec((width, out), lambda m, order: (0, order[1])),
            ]
            + [ANY] * len(after),
            out_specs=[pl.BlockSpec((strip, out), lambda m, order: (m, 0))] * 2,
        ),
        out_shape=[shape(rows, out)] * 2,
        compiler_params=pltpu.CompilerParams(vmem_limit_bytes=24 * MIB),
        cost_estimate=pl.CostEstimate(flops=int(SHARE * flops), bytes_accessed=int(SHARE * nbytes), transcendentals=0),
    )(order, tokens, placed(weight), placed(weight), *after)


def rows_kernel(pieces, ins, *refs):
    at = 0
    for length, terms in pieces:
        total = 0.0
        for which, start in terms:
            total = total + refs[which][start : start + length, :].astype(F32)
        refs[-1][at : at + length, :] = total.astype(BF16)
        at += length


def add_rows(arrays, pieces, after=()):
    rows, width = sum(length for length, _ in pieces), arrays[0].shape[1]
    return call(
        functools.partial(rows_kernel, pieces),
        list(arrays),
        [VMEM] * len(arrays),
        shape(rows, width),
        VMEM,
        after=after,
        nbytes=8 * rows * width,
    )


def finish_kernel(row, per, ins, tab_ref, up_ref, *refs):
    lows, base_ref, out_ref = refs[:4], refs[4], refs[5]
    width = out_ref.shape[1]
    low = lows[0][...].astype(F32)
    for other in lows[1:]:
        low = low + other[...].astype(F32)
    low = low.astype(BF16)
    for j in range(per):
        b = pl.program_id(0) * per + j
        at = slice(j * LANES, (j + 1) * LANES)
        total = lax.dot_general(low[:, at], up_ref[b], TN, preferred_element_type=F32)
        total = total + base_ref[at, :].astype(F32)
        live = lax.broadcasted_iota(I32, (LANES, width), 0) < tab_ref[row, b]
        out_ref[at, :] = jnp.where(live, total, 0.0).astype(out_ref.dtype)


def finish(tab, row, up, lows, base, per):
    rank, rows = lows[0].shape
    width = base.shape[1]
    blocks = rows // LANES
    whole = pl.BlockSpec((per * LANES, width), lambda j: (j, 0))
    return call(
        functools.partial(finish_kernel, row, per),
        [tab, up, *lows, pltpu.with_memory_space_constraint(base, pltpu.HBM)],
        [SMEM, VMEM] + [pl.BlockSpec((rank, per * LANES), lambda j: (0, j))] * 4 + [whole],
        shape(rows, width),
        whole,
        free=True,
        grid=(blocks // per,),
        flops=2 * rows * rank * width,
        nbytes=4 * rows * width,
    )


def swap(x, axis):
    return lax.ppermute(x, axis, [(0, 1), (1, 0)])


def ends(x):
    return lax.ppermute(x, "skill", [(0, 1), (1, 0), (2, 3), (3, 2)])


def inward(x):
    return lax.ppermute(x, "skill", [(0, 1), (3, 2)])


def outward(x):
    return lax.ppermute(x, "skill", [(1, 0), (2, 3)])


def middle(x):
    pairs = [(2 + c, 4 + c) for c in (0, 1)] + [(0, 1), (6, 7)]
    return lax.ppermute(x, ("skill", "tensor"), pairs + [(b, a) for a, b in pairs])


def line_body(tokens, base_weight, skill_down, skill_up, alloc, block_tenant, block_len):
    n = 4
    rows, width = tokens.shape
    tenants, local_skills = alloc.shape
    rank = skill_down.shape[2]
    out = skill_up.shape[2]
    blocks = block_len.shape[0]
    me = lax.axis_index("skill")
    tensor, dp = lax.axis_index("tensor"), lax.axis_index("dp")
    hops = [ends, middle, ends]
    full = [min(tenants, blocks * (n - 1 - h)) for h in range(n - 1)]
    plans = [[min(f, p) for f, p in zip(full, plan)] for plan in PLANS] + [full]
    tile = width // 8
    parts = [(0, 3 * tile), (3 * tile, 3 * tile), (6 * tile, 2 * tile)]

    own_t = block_tenant.reshape(1, blocks)
    seen = jnp.concatenate(
        [own_t]
        + [lax.ppermute(own_t, "skill", [(j, j ^ k) for j in range(n)]) for k in range(1, n)],
        axis=0,
    )
    library = jnp.transpose(skill_down, (0, 2, 1)).reshape(local_skills * rank, width)
    own_up, kron = compose_first(alloc, skill_up.reshape(local_skills * rank, out), rank)
    own_up, seen = lax.optimization_barrier((own_up, seen))
    up_0 = ends(own_up)
    seen = [seen, swap(seen, "group")]
    own_0 = compose(kron, library, rank, parts[0], tile, after=[own_up])
    tab, plan = make_tables(n, tenants, plans, me.reshape(1).astype(I32), block_len.reshape(1, blocks), seen)
    theirs, ours = (1 - tensor) * 2, tensor * 2
    order_cross = jnp.stack([theirs + 1 - dp, ours + 1 - dp]).astype(I32)
    order_stay = jnp.stack([theirs + dp, ours + dp]).astype(I32)

    def planned(rare, sizes):
        step_, project_ = functools.partial(step, rare=rare), functools.partial(project, rare=rare)
        owns, arrived, up_came = [own_0], [[], [], []], [up_0]

        def job(h, k):
            return h, sizes[h], [(owns[k], arrived[k][h - 1] if h else None, False)]

        up_piece = (own_up, up_0, True)
        first, up_1 = step_(n, tab, [job(0, 0), (1, sizes[1], [up_piece])])
        arrived[0].append(ends(first))
        up_came.append(middle(up_1))
        own, message = compose(kron, library, rank, parts[1], tile, sizes[0], tab)
        owns.append(own)
        arrived[1].append(ends(message))
        cut = rows // 3
        away, keep = base_product(order_cross, tokens, base_weight, out, [message], 0, 1)

        to_1, away = step_(n, tab, [job(1, 0)], [keep, up_came[1]], [away])
        arrived[0].append(middle(to_1))
        core = swap(away, "tensor")
        own, message = compose(kron, library, rank, parts[2], tile, sizes[0], tab, [to_1])
        owns.append(own)
        away_2, keep_2 = base_product(order_cross, tokens, base_weight, out, [own], 1, 3)
        if EARLY:
            stay, stay_keep = base_product(order_stay, tokens, base_weight, out, [keep_2], 0, 3)

        first_and_up = 2, (max(sizes[2], (sizes[0] + 1) // 2), message), [
            (owns[0], arrived[0][1], False),
            (own_up, up_came[1], False),
        ]
        to_1, to_2, away_2 = step_(n, tab, [job(1, 1), first_and_up], [core, keep_2] + ([stay] if EARLY else []), [away_2])
        arrived[1].append(middle(to_1))
        exchanged = ends(to_2)
        arrived[0].append(exchanged)
        arrived[2].append(exchanged)
        up_came.append(exchanged)
        core_2 = swap(away_2, "tensor")
        near = add_rows([keep, core], [(cut, [(0, 0), (1, 0)])], [to_1])
        across = swap(near, "dp")
        if not EARLY:
            stay, stay_keep = base_product(order_stay, tokens, base_weight, out, [near], 0, 3)
        near_2 = add_rows([keep_2, core_2], [(rows - cut, [(0, 0), (1, 0)])])

        to_1, to_2, stay, near_2 = step_(n, tab, [job(1, 2), job(2, 1)], [across, stay_keep], [stay, near_2])
        arrived[2].append(middle(to_1))
        arrived[1].append(outward(to_2))
        across_2 = swap(near_2, "dp")
        core = swap(stay, "tensor")
        low, up = project_(n, tab, tokens, owns[0], parts[0], arrived[0], None, False, (own_up, up_came), [to_1])

        (to_2,) = step_(n, tab, [job(2, 2)], [low, core])
        arrived[2].append(ends(to_2))
        (low,) = project_(n, tab, tokens, owns[1], parts[1], arrived[1], low, False, None, [to_2])
        base = add_rows(
            [stay_keep, core, across, across_2],
            [(cut, [(0, 0), (1, 0), (2, 0)]), (rows - cut, [(0, cut), (1, cut), (3, 0)])],
            [low],
        )
        (low,) = project_(n, tab, tokens, owns[2], parts[2], arrived[2], low, True, None, [base])
        return low, up, base

    low, up, base = lax.switch(plan[0], [functools.partial(planned, int(k > 2), sizes) for k, sizes in enumerate(plans)])
    lows = [low, swap(low, "tensor"), swap(low, "dp")]
    lows.append(lax.ppermute(low, ("tensor", "dp"), [(0, 3), (1, 2), (2, 1), (3, 0)]))
    return finish(tab, 3 * (n - 1) + 2, up, lows, base, PER)


def plain_body(tokens, base_weight, skill_down, skill_up, alloc, block_tenant, block_len):
    rows, width = tokens.shape
    blocks = block_len.shape[0]
    block_rows = rows // blocks
    local_skills, slice_width, rank = skill_down.shape
    slice_out = skill_up.shape[2]
    down_size = slice_width * rank
    stacked = jnp.concatenate(
        [
            skill_down.reshape(local_skills, down_size),
            skill_up.reshape(local_skills, rank * slice_out),
        ],
        1,
    ).astype(F32)
    partial_sum = jnp.dot(alloc, stacked, precision=lax.Precision.HIGHEST)
    composed = lax.psum(partial_sum.astype(BF16), "skill")
    factors = jnp.take(composed, block_tenant, axis=0)
    down_part = factors[:, :down_size].reshape(blocks, slice_width, rank)
    up_part = factors[:, down_size:].reshape(blocks, rank, slice_out).astype(F32)
    grouped = tokens.reshape(blocks, block_rows, width)
    projected = jnp.einsum("bnd,bdr->bnr", grouped, down_part, preferred_element_type=F32)
    base_term = jnp.dot(tokens, base_weight, preferred_element_type=F32)
    lowrank = lax.psum(projected.astype(BF16), ("tensor", "dp")).astype(F32)
    base = lax.psum_scatter(
        base_term.astype(BF16), ("tensor", "dp"), scatter_dimension=1, tiled=True
    ).astype(F32)
    adapter = jnp.einsum("bnr,bro->bno", lowrank, up_part, precision=lax.Precision.HIGHEST)
    total = base.reshape(blocks, block_rows, slice_out) + adapter
    live = (jnp.arange(block_rows, dtype=I32)[None, :] < block_len[:, None])[:, :, None]
    return jnp.where(live, total, 0.0).astype(BF16).reshape(rows, slice_out)


def solution(mesh):
    placed = (
        P(("group", "skill"), ("tensor", "dp")),
        P(("tensor", "dp"), None),
        P("skill", ("tensor", "dp"), None),
        P("skill", None, ("tensor", "dp")),
        P("group", "skill"),
        P(("group", "skill")),
        P(("group", "skill")),
    )
    fits = (mesh.shape["skill"], mesh.shape["tensor"], mesh.shape["dp"]) == (4, 2, 2)
    body = line_body if fits else plain_body
    return jax.shard_map(
        body,
        mesh=mesh,
        in_specs=placed,
        out_specs=P(("group", "skill"), ("tensor", "dp")),
        check_vma=False,
    )
```

```python
import functools

import jax
import jax.numpy as jnp
from jax import lax
from jax.experimental import pallas as pl
from jax.experimental.pallas import tpu as pltpu
from jax.sharding import PartitionSpec as P

F32, BF16, I32 = jnp.float32, jnp.bfloat16, jnp.int32
MIB = 1 << 20
LANES = 128
LARGE = 1 << 21
PER = 6
EARLY = 0
BLOCKS_AT_ONCE = 2
SHARE = 1.0
VMEM = pl.BlockSpec(memory_space=pltpu.VMEM)
SMEM = pl.BlockSpec(memory_space=pltpu.SMEM)
ANY = pl.BlockSpec(memory_space=pl.ANY)
NT = (((1,), (1,)), ((), ()))
TN = (((0,), (0,)), ((), ()))
PLANS = ((17, 14, 10), (18, 15, 11), (19, 16, 11), (20, 17, 11), (22, 18, 12))


def call(kernel, ins, specs, outs, out_specs, *, after=(), free=None, vmem=24, flops=0, nbytes=0, **kwargs):
    return pl.pallas_call(
        functools.partial(kernel, len(ins)),
        in_specs=specs + [ANY] * len(after),
        out_specs=out_specs,
        out_shape=outs,
        compiler_params=pltpu.CompilerParams(vmem_limit_bytes=vmem * MIB),
        cost_estimate=pl.CostEstimate(flops=int(SHARE * flops), bytes_accessed=int(SHARE * nbytes), transcendentals=0),
        **kwargs,
    )(*[x if free is True or x is free else placed(x) for x in ins], *after)


def placed(x):
    if x.dtype != BF16:
        return x
    return pltpu.with_memory_space_constraint(x, pltpu.HBM if x.size >= LARGE else pltpu.VMEM)


def shape(*dims, dtype=BF16):
    return jax.ShapeDtypeStruct(dims, dtype)


def kron_kernel(rank, ins, alloc_ref, kron_ref):
    tenants, skills = alloc_ref.shape
    depth = skills * rank
    at = lax.broadcasted_iota(I32, (skills, depth), 1)
    row = lax.broadcasted_iota(I32, (skills, depth), 0)
    inside = jnp.logical_and(at >= row * rank, at < (row + 1) * rank)
    repeat = jnp.where(inside, 1.0, 0.0).astype(BF16)
    spread = jnp.dot(alloc_ref[...].astype(BF16), repeat, preferred_element_type=F32)
    lane = lax.rem(lax.broadcasted_iota(I32, (rank, depth), 1), rank)
    diagonal = lane == lax.broadcasted_iota(I32, (rank, depth), 0)
    for t in range(tenants):
        kron_ref[t * rank : (t + 1) * rank, :] = jnp.where(diagonal, spread[t : t + 1, :], 0.0).astype(BF16)


def first_kernel(rank, ins, alloc_ref, library_ref, own_ref, kron_ref):
    kron_kernel(rank, 1, alloc_ref, kron_ref)
    made = jnp.dot(kron_ref[...], library_ref[...], preferred_element_type=F32).astype(BF16)
    own_ref[...] = made.reshape(own_ref.shape)


def compose_first(alloc, library, rank):
    tenants, skills = alloc.shape
    depth, out = library.shape
    return call(
        functools.partial(first_kernel, rank),
        [pltpu.with_memory_space_constraint(x, pltpu.HBM) for x in (alloc, library)],
        [pl.BlockSpec(x.shape, lambda j: (0, 0)) for x in (alloc, library)],
        [shape(tenants, rank, out), shape(tenants * rank, depth)],
        [VMEM] * 2,
        free=True,
        grid=(1,),
        flops=2 * tenants * rank * depth * out,
        nbytes=2 * depth * out,
    )


def compose_kernel(slots, ins, *refs):
    kron_ref, library_ref = refs[:2] if not slots else refs[1:3]
    own_ref = refs[-2] if slots else refs[-1]
    tenants, rank, size = own_ref.shape
    made = jnp.dot(kron_ref[...], library_ref[...], preferred_element_type=F32).astype(BF16)
    own_ref[...] = made.reshape(tenants, rank, size)
    if slots:
        copy_slots(refs[0], own_ref, refs[-1], slots)


def copy_slots(tab_ref, own_ref, out_ref, slots):
    def one(slot, carry):
        out_ref[slot] = own_ref[tab_ref[0, slot]]
        return carry

    lax.fori_loop(0, slots, one, 0, unroll=2)


def compose(kron, library, rank, part, tile, slots=0, tab=None, after=()):
    rows, depth = kron.shape
    tenants = rows // rank
    start, size = part
    at = start // tile
    outs, out_specs = [shape(tenants, rank, size)], [pl.BlockSpec((tenants, rank, tile), lambda j: (0, 0, j))]
    if slots:
        outs.append(shape(slots, rank, size))
        out_specs.append(pl.BlockSpec((slots, rank, tile), lambda j: (0, 0, j)))
    made = call(
        functools.partial(compose_kernel, slots),
        ([tab] if slots else []) + [kron, library],
        ([SMEM] if slots else []) + [VMEM, pl.BlockSpec((depth, tile), lambda j: (0, at + j))],
        outs,
        out_specs,
        after=after,
        grid=(size // tile,),
        flops=2 * rows * depth * size,
        nbytes=2 * (depth + rows) * size,
    )
    return made if slots else made[0]


def tables_kernel(n, tenants, plans, ins, place_ref, len_ref, *refs):
    arrays, tab_ref, plan_ref = refs[:-2], refs[-2], refs[-1]
    me = place_ref[0]
    blocks = arrays[0].shape[1]
    sub = lax.broadcasted_iota(I32, (tenants, tenants), 0)
    lane = lax.broadcasted_iota(I32, (tenants, tenants), 1)
    wide = lax.broadcasted_iota(I32, (tenants, LANES), 1)
    tenant = lax.broadcasted_iota(I32, (tenants, LANES), 0)
    one = lax.broadcasted_iota(I32, (tenants, blocks), 0)
    zs = [me ^ k for k in range(n)]
    groups = len(arrays)
    present = [
        [
            jnp.max(jnp.where(one == arrays[g][k : k + 1, :], 1.0, 0.0), axis=1, keepdims=True)
            for k in range(n)
        ]
        for g in range(groups)
    ]

    def union(keep, group=0):
        total = jnp.zeros((tenants, 1), F32)
        for z, here in zip(zs, present[group]):
            total = jnp.maximum(total, here * jnp.where(keep(z), 1.0, 0.0))
        return total

    def positions(held):
        across = jnp.sum(jnp.where(sub == lane, held, 0.0), axis=0, keepdims=True)
        return jnp.sum(jnp.where(lane < sub, across, 0.0), axis=1, keepdims=True)

    def pack(held, value):
        slot = positions(held).astype(I32)
        chosen = jnp.logical_and(slot == wide, held > 0.5)
        return jnp.sum(jnp.where(chosen, value, 0.0), axis=0, keepdims=True)

    send_right, send_left = union(lambda z: z > me), union(lambda z: z < me)
    from_left, from_right = positions(union(lambda z: z >= me)), positions(union(lambda z: z <= me))
    number = tenant.astype(F32)
    right = pack(send_right, number), pack(send_right, from_left)
    left = pack(send_left, number), pack(send_left, from_right)
    own = jnp.concatenate([arrays[0][0:1, :], jnp.zeros((1, LANES - blocks), I32)], axis=1)
    mine = own == tenant

    def at(place, rows, otherwise):
        return jnp.where(me == place, rows, otherwise)

    none = jnp.zeros((1, LANES), F32)
    final_right = jnp.sum(jnp.where(mine, from_left, 0.0), axis=0, keepdims=True)
    final_left = jnp.sum(jnp.where(mine, from_right, 0.0), axis=0, keepdims=True)
    rows = []
    for part in (0, 1):
        for hop in range(n - 1):
            rows.append(at(hop, right[part], at(n - 1 - hop, left[part], none)))
    for hop in range(n - 1):
        rows.append(at(hop + 1, final_right, at(n - 2 - hop, final_left, none)))
    for row, value in enumerate(rows):
        tab_ref[row : row + 1, :] = value.astype(I32)
    tab_ref[len(rows) : len(rows) + 1, :] = own
    tab_ref[len(rows) + 2 : len(rows) + 3, :] = jnp.concatenate([len_ref[...], jnp.zeros((1, LANES - blocks), I32)], axis=1)
    ends_here = jnp.logical_or(me == 0, me == n - 1)
    tab_ref[len(rows) + 1 : len(rows) + 2, :] = jnp.where(ends_here, jnp.ones_like(own), jnp.zeros_like(own))

    held = jnp.zeros((tenants, LANES), F32)
    hop_of = lax.broadcasted_iota(I32, (1, LANES), 1)
    limits = [jnp.full((1, LANES), float(tenants), F32) for _ in plans]
    column = 0
    for group in range(groups):
        for hop in range(n - 1):
            for keep in (lambda z: z > hop, lambda z: z < n - 1 - hop):
                held = jnp.where(wide == column, union(keep, group), held)
                limits = [jnp.where(hop_of == column, float(p[hop]), l) for p, l in zip(plans, limits)]
                column += 1
    counts = jnp.sum(held, axis=0, keepdims=True)
    plan = jnp.int32(0)
    for limit in limits[:-1]:
        plan = plan + jnp.where(jnp.max(counts - limit) > 0.5, 1, 0)
    plan_ref[0] = plan


def make_tables(n, tenants, plans, place, lens, arrays):
    rows = -(-(3 * (n - 1) + 3) // 8) * 8
    return call(
        functools.partial(tables_kernel, n, tenants, plans),
        [place, lens, *arrays],
        [SMEM] + [VMEM] * (1 + len(arrays)),
        [shape(rows, LANES, dtype=I32), shape(1, dtype=I32)],
        [VMEM, SMEM],
    )


def step_kernel(n, jobs, passed, unroll, ins, tab_ref, *refs):
    given, outs = list(refs[: ins - 1]), refs[ins - 1 + passed :]
    for (hop, slots, pieces), out_ref in zip(jobs, outs):
        both = slots is None
        if both:
            slots = out_ref.shape[0] // 2
            fresh_ref = given.pop(0)

            @pl.when(tab_ref[3 * (n - 1) + 1, 0] > 0)
            def _(fresh_ref=fresh_ref, out_ref=out_ref):
                out_ref[: fresh_ref.shape[0]] = fresh_ref[...]

        held = [(given.pop(0), given.pop(0) if hop else None) for _ in pieces]

        def one(slot, carry, hop=hop, pieces=pieces, held=held, out_ref=out_ref, both=both, slots=slots):
            tenant = tab_ref[hop, slot]
            at = 0
            made = []
            for by_tenant, (own_ref, in_ref) in zip(pieces, held):
                block = own_ref[tenant]
                if hop:
                    index = tenant if by_tenant else tab_ref[n - 1 + hop, slot]
                    block = (block.astype(F32) + in_ref[index].astype(F32)).astype(BF16)
                made.append(block)
            block = jnp.concatenate(made, axis=1) if len(made) > 1 else made[0]
            if both:
                half = out_ref.shape[2]
                out_ref[slot] = block[:, :half]
                out_ref[slots + slot] = block[:, half:]
            else:
                out_ref[slot] = block
            return carry

        def all_slots(one=one, slots=slots):
            lax.fori_loop(0, slots, one, 0, unroll=unroll)

        if both:
            pl.when(tab_ref[3 * (n - 1) + 1, 0] == 0)(all_slots)
        else:
            all_slots()


def step(n, tab, jobs, after=(), through=(), rare=0):
    ins, shapes, plan = [], [], []
    for hop, slots, pieces in jobs:
        columns = sum(own.shape[2] for own, _, _ in pieces)
        if isinstance(slots, tuple):
            plan.append((hop, None, [by_tenant for _, _, by_tenant in pieces]))
            ins.append(slots[1])
            slots, columns = 2 * slots[0], columns // 2
            assert slots >= ins[-1].shape[0] and columns == ins[-1].shape[2]
        else:
            plan.append((hop, slots, [by_tenant for _, _, by_tenant in pieces]))
        for own, arrived, _ in pieces:
            ins += [own, arrived] if hop else [own]
        shapes.append(shape(slots, pieces[0][0].shape[1], columns))
    return call(
        functools.partial(step_kernel, n, plan, len(after) + len(through), rare or True),
        [tab, *ins],
        [SMEM] + [VMEM] * len(ins),
        shapes + [shape(*x.shape) for x in through],
        [VMEM] * len(shapes) + [ANY] * len(through),
        after=list(after) + list(through),
        input_output_aliases={1 + len(ins) + len(after) + i: len(shapes) + i for i in range(len(through))},
        nbytes=sum(2 * 3 * x.size for x in shapes),
    )


def read(ref, slot, start, size):
    half = ref.shape[2]
    if start + size <= half and start == 0 and size == half:
        return ref[slot]
    slots = ref.shape[0] // 2
    pieces = []
    while size:
        part, at = divmod(start, half)
        count = min(size, half - at)
        pieces.append(ref[part * slots + slot, :, at : at + count])
        start, size = start + count, size - count
    return jnp.concatenate(pieces, axis=1) if len(pieces) > 1 else pieces[0]


def factor_of(n, b, by_tenant, tab_ref, own_ref, arrived, lead=0):
    tenant = tab_ref[3 * (n - 1), b]
    factor = own_ref[tenant].astype(F32)
    outer = tab_ref[3 * (n - 1) + 1, 0] > 0
    for hop in range(n - 1):
        index = tenant if by_tenant and hop == 0 else tab_ref[2 * (n - 1) + hop, b]
        came = read(arrived[hop], index, lead, own_ref.shape[2]) if hop == n - 2 else arrived[hop][index]
        came = came.astype(F32)
        used = jnp.where(outer, 1, 0) if hop == n - 2 else jnp.where(outer, 0, 1)
        factor = jnp.where(used > 0, factor + came, factor)
    return factor.astype(BF16)


def project_kernel(n, unroll, first, out, ins, tab_ref, tokens_ref, own_ref, *refs):
    arrived = refs[: n - 1]
    total_ref = None if first else refs[ins - 4]
    outs = refs[-2:] if out else refs[-1:]
    size = tokens_ref.shape[1]

    def one(b, carry):
        factor = factor_of(n, b, False, tab_ref, own_ref, arrived)
        at = pl.ds(pl.multiple_of(b * LANES, LANES), LANES)
        part = lax.dot_general(factor, tokens_ref[at, :], NT, preferred_element_type=F32)
        if not first:
            part = total_ref[:, at] + part
        outs[0][:, at] = part.astype(outs[0].dtype)
        if out:
            outs[1][b] = factor_of(n, b, True, tab_ref, refs[n - 1], refs[n : 2 * n - 1], own_ref.shape[2])
        return carry

    lax.fori_loop(0, tokens_ref.shape[0] // LANES, one, 0, unroll=unroll)


def project(n, tab, tokens, own, part, arrived, total, last, up=None, after=(), rare=0):
    tenants, rank, size = own.shape
    rows = tokens.shape[0]
    at = part[0] // size
    outs = [shape(rank, rows, dtype=BF16 if last else F32)]
    ins = [tab, tokens, own, *arrived]
    if up:
        outs.append(shape(rows // LANES, rank, up[0].shape[2]))
        ins += [up[0], *up[1]]
    if total is not None:
        ins.append(total)
    return call(
        functools.partial(project_kernel, n, rare or BLOCKS_AT_ONCE, total is None, up is not None),
        ins,
        [SMEM, pl.BlockSpec((rows, size), lambda j: (0, at))] + [VMEM] * (len(ins) - 2),
        outs,
        [VMEM] * len(outs),
        after=after,
        free=tokens,
        grid=(1,),
        flops=2 * rows * size * rank,
        nbytes=2 * size * (rows + 2 * tenants * rank),
    )


def base_kernel(order_ref, tokens_ref, first_ref, second_ref, *refs):
    for weight_ref, out_ref in ((first_ref, refs[-2]), (second_ref, refs[-1])):
        out_ref[...] = jnp.dot(tokens_ref[...], weight_ref[...], preferred_element_type=F32).astype(BF16)


def base_product(order, tokens, weight, out, after, first, last):
    strip, width = tokens.shape[0] // 3, tokens.shape[1]
    rows = (last - first) * strip
    flops, nbytes = 4 * rows * width * out, 2 * (rows * (width + 2 * out) + 2 * width * out)
    return pl.pallas_call(
        base_kernel,
        grid_spec=pltpu.PrefetchScalarGridSpec(
            num_scalar_prefetch=1,
            grid=(last - first,),
            in_specs=[
                pl.BlockSpec((strip, width), lambda m, order: (first + m, 0)),
                pl.BlockSpec((width, out), lambda m, order: (0, order[0])),
                pl.BlockSpec((width, out), lambda m, order: (0, order[1])),
            ]
            + [ANY] * len(after),
            out_specs=[pl.BlockSpec((strip, out), lambda m, order: (m, 0))] * 2,
        ),
        out_shape=[shape(rows, out)] * 2,
        compiler_params=pltpu.CompilerParams(vmem_limit_bytes=24 * MIB),
        cost_estimate=pl.CostEstimate(flops=int(SHARE * flops), bytes_accessed=int(SHARE * nbytes), transcendentals=0),
    )(order, tokens, placed(weight), placed(weight), *after)


def rows_kernel(pieces, ins, *refs):
    at = 0
    for length, terms in pieces:
        total = 0.0
        for which, start in terms:
            total = total + refs[which][start : start + length, :].astype(F32)
        refs[-1][at : at + length, :] = total.astype(BF16)
        at += length


def add_rows(arrays, pieces, after=()):
    rows, width = sum(length for length, _ in pieces), arrays[0].shape[1]
    return call(
        functools.partial(rows_kernel, pieces),
        list(arrays),
        [VMEM] * len(arrays),
        shape(rows, width),
        VMEM,
        after=after,
        nbytes=8 * rows * width,
    )


def finish_kernel(row, per, ins, tab_ref, up_ref, *refs):
    lows, base_ref, out_ref = refs[:4], refs[4], refs[5]
    width = out_ref.shape[1]
    low = lows[0][...].astype(F32)
    for other in lows[1:]:
        low = low + other[...].astype(F32)
    low = low.astype(BF16)
    for j in range(per):
        b = pl.program_id(0) * per + j
        at = slice(j * LANES, (j + 1) * LANES)
        total = lax.dot_general(low[:, at], up_ref[b], TN, preferred_element_type=F32)
        total = total + base_ref[at, :].astype(F32)
        live = lax.broadcasted_iota(I32, (LANES, width), 0) < tab_ref[row, b]
        out_ref[at, :] = jnp.where(live, total, 0.0).astype(out_ref.dtype)


def finish(tab, row, up, lows, base, per):
    rank, rows = lows[0].shape
    width = base.shape[1]
    blocks = rows // LANES
    whole = pl.BlockSpec((per * LANES, width), lambda j: (j, 0))
    return call(
        functools.partial(finish_kernel, row, per),
        [tab, up, *lows, pltpu.with_memory_space_constraint(base, pltpu.HBM)],
        [SMEM, VMEM] + [pl.BlockSpec((rank, per * LANES), lambda j: (0, j))] * 4 + [whole],
        shape(rows, width),
        whole,
        free=True,
        grid=(blocks // per,),
        flops=2 * rows * rank * width,
        nbytes=4 * rows * width,
    )


def swap(x, axis):
    return lax.ppermute(x, axis, [(0, 1), (1, 0)])


def ends(x):
    return lax.ppermute(x, "skill", [(0, 1), (1, 0), (2, 3), (3, 2)])


def inward(x):
    return lax.ppermute(x, "skill", [(0, 1), (3, 2)])


def outward(x):
    return lax.ppermute(x, "skill", [(1, 0), (2, 3)])


def middle(x):
    pairs = [(2 + c, 4 + c) for c in (0, 1)] + [(0, 1), (6, 7)]
    return lax.ppermute(x, ("skill", "tensor"), pairs + [(b, a) for a, b in pairs])


def line_body(tokens, base_weight, skill_down, skill_up, alloc, block_tenant, block_len):
    n = 4
    rows, width = tokens.shape
    tenants, local_skills = alloc.shape
    rank = skill_down.shape[2]
    out = skill_up.shape[2]
    blocks = block_len.shape[0]
    me = lax.axis_index("skill")
    tensor, dp = lax.axis_index("tensor"), lax.axis_index("dp")
    hops = [ends, middle, ends]
    full = [min(tenants, blocks * (n - 1 - h)) for h in range(n - 1)]
    plans = [[min(f, p) for f, p in zip(full, plan)] for plan in PLANS] + [full]
    tile = width // 8
    parts = [(0, 3 * tile), (3 * tile, 3 * tile), (6 * tile, 2 * tile)]

    own_t = block_tenant.reshape(1, blocks)
    seen = jnp.concatenate(
        [own_t]
        + [lax.ppermute(own_t, "skill", [(j, j ^ k) for j in range(n)]) for k in range(1, n)],
        axis=0,
    )
    library = jnp.transpose(skill_down, (0, 2, 1)).reshape(local_skills * rank, width)
    own_up, kron = compose_first(alloc, skill_up.reshape(local_skills * rank, out), rank)
    own_up, seen = lax.optimization_barrier((own_up, seen))
    up_0 = ends(own_up)
    seen = [seen, swap(seen, "group")]
    own_0 = compose(kron, library, rank, parts[0], tile, after=[own_up])
    tab, plan = make_tables(n, tenants, plans, me.reshape(1).astype(I32), block_len.reshape(1, blocks), seen)
    theirs, ours = (1 - tensor) * 2, tensor * 2
    order_cross = jnp.stack([theirs + 1 - dp, ours + 1 - dp]).astype(I32)
    order_stay = jnp.stack([theirs + dp, ours + dp]).astype(I32)

    def planned(rare, sizes):
        step_, project_ = functools.partial(step, rare=rare), functools.partial(project, rare=rare)
        owns, arrived, up_came = [own_0], [[], [], []], [up_0]

        def job(h, k):
            return h, sizes[h], [(owns[k], arrived[k][h - 1] if h else None, False)]

        up_piece = (own_up, up_0, True)
        first, up_1 = step_(n, tab, [job(0, 0), (1, sizes[1], [up_piece])])
        arrived[0].append(ends(first))
        up_came.append(middle(up_1))
        own, message = compose(kron, library, rank, parts[1], tile, sizes[0], tab)
        owns.append(own)
        arrived[1].append(ends(message))
        cut = rows // 3
        away, keep = base_product(order_cross, tokens, base_weight, out, [message], 0, 1)

        to_1, away = step_(n, tab, [job(1, 0)], [keep, up_came[1]], [away])
        arrived[0].append(middle(to_1))
        core = swap(away, "tensor")
        own, message = compose(kron, library, rank, parts[2], tile, sizes[0], tab, [to_1])
        owns.append(own)
        away_2, keep_2 = base_product(order_cross, tokens, base_weight, out, [own], 1, 3)
        if EARLY:
            stay, stay_keep = base_product(order_stay, tokens, base_weight, out, [keep_2], 0, 3)

        first_and_up = 2, (max(sizes[2], (sizes[0] + 1) // 2), message), [
            (owns[0], arrived[0][1], False),
            (own_up, up_came[1], False),
        ]
        to_1, to_2, away_2 = step_(n, tab, [job(1, 1), first_and_up], [core, keep_2] + ([stay] if EARLY else []), [away_2])
        arrived[1].append(middle(to_1))
        exchanged = ends(to_2)
        arrived[0].append(exchanged)
        arrived[2].append(exchanged)
        up_came.append(exchanged)
        core_2 = swap(away_2, "tensor")
        near = add_rows([keep, core], [(cut, [(0, 0), (1, 0)])], [to_1])
        across = swap(near, "dp")
        if not EARLY:
            stay, stay_keep = base_product(order_stay, tokens, base_weight, out, [near], 0, 3)
        near_2 = add_rows([keep_2, core_2], [(rows - cut, [(0, 0), (1, 0)])])

        to_1, to_2, stay, near_2 = step_(n, tab, [job(1, 2), job(2, 1)], [across, stay_keep], [stay, near_2])
        arrived[2].append(middle(to_1))
        arrived[1].append(outward(to_2))
        across_2 = swap(near_2, "dp")
        core = swap(stay, "tensor")
        low, up = project_(n, tab, tokens, owns[0], parts[0], arrived[0], None, False, (own_up, up_came), [to_1])

        (to_2,) = step_(n, tab, [job(2, 2)], [low, core])
        arrived[2].append(ends(to_2))
        (low,) = project_(n, tab, tokens, owns[1], parts[1], arrived[1], low, False, None, [to_2])
        base = add_rows(
            [stay_keep, core, across, across_2],
            [(cut, [(0, 0), (1, 0), (2, 0)]), (rows - cut, [(0, cut), (1, cut), (3, 0)])],
            [low],
        )
        (low,) = project_(n, tab, tokens, owns[2], parts[2], arrived[2], low, True, None, [base])
        return low, up, base

    low, up, base = lax.switch(plan[0], [functools.partial(planned, int(k > 2), sizes) for k, sizes in enumerate(plans)])
    lows = [low, swap(low, "tensor"), swap(low, "dp")]
    lows.append(lax.ppermute(low, ("tensor", "dp"), [(0, 3), (1, 2), (2, 1), (3, 0)]))
    return finish(tab, 3 * (n - 1) + 2, up, lows, base, PER)


def plain_body(tokens, base_weight, skill_down, skill_up, alloc, block_tenant, block_len):
    rows, width = tokens.shape
    blocks = block_len.shape[0]
    block_rows = rows // blocks
    local_skills, slice_width, rank = skill_down.shape
    slice_out = skill_up.shape[2]
    down_size = slice_width * rank
    stacked = jnp.concatenate(
        [
            skill_down.reshape(local_skills, down_size),
            skill_up.reshape(local_skills, rank * slice_out),
        ],
        1,
    ).astype(F32)
    partial_sum = jnp.dot(alloc, stacked, precision=lax.Precision.HIGHEST)
    composed = lax.psum(partial_sum.astype(BF16), "skill")
    factors = jnp.take(composed, block_tenant, axis=0)
    down_part = factors[:, :down_size].reshape(blocks, slice_width, rank)
    up_part = factors[:, down_size:].reshape(blocks, rank, slice_out).astype(F32)
    grouped = tokens.reshape(blocks, block_rows, width)
    projected = jnp.einsum("bnd,bdr->bnr", grouped, down_part, preferred_element_type=F32)
    base_term = jnp.dot(tokens, base_weight, preferred_element_type=F32)
    lowrank = lax.psum(projected.astype(BF16), ("tensor", "dp")).astype(F32)
    base = lax.psum_scatter(
        base_term.astype(BF16), ("tensor", "dp"), scatter_dimension=1, tiled=True
    ).astype(F32)
    adapter = jnp.einsum("bnr,bro->bno", lowrank, up_part, precision=lax.Precision.HIGHEST)
    total = base.reshape(blocks, block_rows, slice_out) + adapter
    live = (jnp.arange(block_rows, dtype=I32)[None, :] < block_len[:, None])[:, :, None]
    return jnp.where(live, total, 0.0).astype(BF16).reshape(rows, slice_out)


def solution(mesh):
    placed = (
        P(("group", "skill"), ("tensor", "dp")),
        P(("tensor", "dp"), None),
        P("skill", ("tensor", "dp"), None),
        P("skill", None, ("tensor", "dp")),
        P("group", "skill"),
        P(("group", "skill")),
        P(("group", "skill")),
    )
    fits = (mesh.shape["skill"], mesh.shape["tensor"], mesh.shape["dp"]) == (4, 2, 2)
    body = line_body if fits else plain_body
    return jax.shard_map(
        body,
        mesh=mesh,
        in_specs=placed,
        out_specs=P(("group", "skill"), ("tensor", "dp")),
        check_vma=False,
    )
```
